128 devices in a mesh: dom: 128 (over y, x, z, core).
Axes of the slice: x: 4, y: 4, z: 4, core: 2. Of those that a mesh axis runs over, the one named last changes fastest.
Arguments:
- positions: float32 [204800, 3, 128], P('dom'), may hold values from 0 to 1
- velocity: float32 [204800, 3, 128], P('dom'), may hold values from -6 to 6
- mass: float32 [204800, 128], P('dom'), may hold values from 0.004 to 0.016
- smoothing: float32 [204800, 128], P('dom'), may hold values from 0.35 to 0.7
- energy: float32 [204800, 128], P('dom'), may hold values from 0.5 to 2
- density_old: float32 [204800, 128], P('dom'), may hold values from 0.3 to 3
- counts: int32 [204800], P('dom'), may hold values from 64 to 128
- active: int32 [2048], P('dom'), may hold values from 0 to 204799, as said below
- neighbours: int32 [2048, 27], P('dom'), may hold values from 0 to 204799, as said below
Outputs:
- hydro: float32 [2048, 5, 128], P('dom')
The draws below stay inside these ranges and needn't reach their ends.
Inputs may be any that keep to these rules, and one draw needn't show every extreme that they name: `active`: Distinct. The entries at positions k * 16 to (k + 1) * 16 - 1 are cells of device k; cells k * 1600 to (k + 1) * 1600 - 1 belong to device k. Domains lie in a box with helical periodic boundaries: the +z, +y and +x neighbours of device d's domain are devices d + 1, d + 4 and d + 16, modulo the number of devices. A device's active cells run along the high x-y edge of its domain, the last of its 16 rows being the high corner cell. So in row a of device d, slot k names a cell of device (d + 16 bx + 4 by + bz) modulo the number of devices, where bx = 1 if k // 9 == 2 else 0, by = 1 if (k // 3) % 3 == 2 else 0, and bz = 1 if k % 3 == 2 and a is the device's last row, else 0. Slot 13 of row a is active[a]. Entries may repeat.
All inputs are finite; a program needn't handle non-finite values.
Results may differ from the reference program's by a relative error of at most 0.0003.
Values sent between devices are 32-bit elements; how exact they have to be, the bound alone decides.
A program may use at most 64 MiB of HBM per device.

```python
import math
import jax
import jax.numpy as jnp
from jax import lax

BLOCK = 128
CELLS_DEV = 1600
ACT_DEV = 16
CELLS = 204800
ACTIVE = 2048
N_DOM = 128


def owned_active(key, owner):
    sub = jax.random.fold_in(jax.random.fold_in(key, 77), owner)
    return jax.random.permutation(sub, CELLS_DEV)[:ACT_DEV].astype(jnp.int32)


def all_owned(key):
    owners = jnp.arange(N_DOM, dtype=jnp.int32)
    return jax.vmap(lambda owner: owned_active(key, owner))(owners)


def draw_active(key, part):
    local = all_owned(key)
    owners = jnp.arange(N_DOM, dtype=jnp.int32)
    return (local + owners[:, None] * CELLS_DEV).reshape(-1).astype(jnp.int32)


def draw_neighbours(key, part):
    local = all_owned(key)
    key = jax.random.fold_in(key, 5)
    slots = jnp.arange(27, dtype=jnp.int32)
    rows = jnp.arange(ACT_DEV, dtype=jnp.int32)
    step_x = jnp.where(slots // 9 == 2, 16, 0)
    step_y = jnp.where(slots // 3 % 3 == 2, 4, 0)
    step_z = jnp.where((slots[None, :] % 3 == 2) & (rows[:, None] == ACT_DEV - 1), 1, 0)
    step = (step_x + step_y)[None, :] + step_z

    def one_device(device):
        keys = jax.random.split(jax.random.fold_in(key, device), 3)
        owner = (device + step) % N_DOM
        coin = jax.random.randint(keys[0], (ACT_DEV, 27), 0, 3)
        pick_active = local[owner, jax.random.randint(keys[1], (ACT_DEV, 27), 0, ACT_DEV)]
        pick_any = jax.random.randint(keys[2], (ACT_DEV, 27), 0, CELLS_DEV)
        chosen = jnp.where(coin == 0, pick_active, pick_any)
        cells = owner * CELLS_DEV + chosen
        itself = device * CELLS_DEV + local[device]
        return cells.at[:, 13].set(itself)
    rows_all = jax.vmap(one_device)(jnp.arange(N_DOM, dtype=jnp.int32))
    return rows_all.reshape(N_DOM * ACT_DEV, 27).astype(jnp.int32)


def place_ends(array, key, low, top_value):
    longest = array.shape.index(max(array.shape))
    spots = []
    for shift in (0, 1):
        where = [jax.random.randint(jax.random.fold_in(key, axis), (), 0, length) for axis, length in enumerate(array.shape)]
        where[longest] = (where[longest] + shift) % array.shape[longest]
        spots.append(tuple(where))
    return array.at[spots[0]].set(low).at[spots[1]].set(top_value)


def shard_levels(own_key, extent, cuts, low, high):
    gain = 1.0
    for axis_at, blocks in cuts:
        draws = jax.random.uniform(jax.random.fold_in(jax.random.fold_in(own_key, 6), axis_at), (blocks,), jnp.float32, low / len(cuts), high / len(cuts))
        gain = gain * jnp.repeat(jnp.exp(draws), extent[axis_at] // blocks).reshape((-1,) + (1,) * (len(extent) - 1 - axis_at))
    return gain


def normal_values(key, extent, spread, bound, shards=(), kind=jnp.bfloat16):
    level = shard_levels(key, extent, shards, -0.22, 0.18) if shards else 1.0
    result = jax.random.normal(key, extent, jnp.float32) * spread * level
    return jnp.minimum(jnp.maximum(result, -bound), bound).astype(kind)


def setup_inputs(seed: int = 0) -> dict:
    streams_of = jax.random.split(jax.random.key(seed), 10)
    return {
        "positions": jnp.clip(1.0 * jax.random.uniform(streams_of[0], (CELLS, 3, BLOCK), jnp.float32) ** shard_levels(streams_of[0], (CELLS, 3, BLOCK), ((0, 128),), -0.2, 0.2), 0.0, 1.0),
        "velocity": normal_values(streams_of[1], (CELLS, 3, BLOCK), 1.0, 6.0, ((0, 128),), jnp.float32),
        "mass": jnp.clip(jnp.exp(math.log(0.016) - 1.3862944 * jax.random.uniform(streams_of[2], (CELLS, BLOCK), jnp.float32) ** shard_levels(streams_of[2], (CELLS, BLOCK), ((0, 128),), -0.2, 0.2)), 0.004, 0.016),
        "smoothing": jnp.clip(jnp.exp(math.log(0.7) - 0.6931472 * jax.random.uniform(streams_of[3], (CELLS, BLOCK), jnp.float32) ** shard_levels(streams_of[3], (CELLS, BLOCK), ((0, 128),), -0.2, 0.2)), 0.35, 0.7),
        "energy": jnp.clip(jnp.exp(math.log(2.0) - 1.3862944 * jax.random.uniform(streams_of[4], (CELLS, BLOCK), jnp.float32) ** shard_levels(streams_of[4], (CELLS, BLOCK), ((0, 128),), -0.2, 0.2)), 0.5, 2.0),
        "density_old": jnp.clip(jnp.exp(math.log(3.0) - 2.3025851 * jax.random.uniform(streams_of[5], (CELLS, BLOCK), jnp.float32) ** shard_levels(streams_of[5], (CELLS, BLOCK), ((0, 128),), -0.2, 0.2)), 0.3, 3.0),
        "counts": place_ends(jax.random.randint(streams_of[6], (CELLS,), 64, 129), jax.random.fold_in(streams_of[6], 1), 64, 128).astype(jnp.int32),
        "active": draw_active(jax.random.fold_in(streams_of[9], 71), 0),
        "neighbours": draw_neighbours(jax.random.fold_in(streams_of[9], 71), 0),
    }


kernel_norm = 8.0 / math.pi
gas_factor = 2.0 / 3.0

def cell_shifts():
    slots = jnp.arange(27, dtype=jnp.int32)
    return jnp.stack([slots // 9 - 1, slots // 3 % 3 - 1, slots % 3 - 1], axis=1).astype(jnp.float32)

def kernel_value(dist_sq, smooth):
    ratio = jnp.sqrt(dist_sq) / smooth
    inner = 1.0 - 6.0 * ratio ** 2 + 6.0 * ratio ** 3
    outer = 2.0 * jnp.maximum(1.0 - ratio, 0.0) ** 3
    return kernel_norm / smooth ** 3 * jnp.where(ratio < 0.5, inner, outer)

def kernel_slope(dist_sq, smooth):
    ratio = jnp.sqrt(dist_sq) / smooth
    inner = -12.0 + 18.0 * ratio
    outer = -6.0 * jnp.maximum(1.0 - ratio, 0.0) ** 2 / jnp.maximum(ratio, 0.5)
    return kernel_norm / smooth ** 5 * jnp.where(ratio < 0.5, inner, outer)

def density_cell(pos_own, smooth_own, pos_near, mass_near):
    gap = pos_own[None, :, :, None] - pos_near[:, :, None, :]
    dist_sq = lax.optimization_barrier(jnp.sum(gap * gap, axis=1))
    weight = kernel_value(dist_sq, smooth_own[None, :, None])
    return lax.optimization_barrier(jnp.sum(mass_near[:, None, :] * weight, axis=(0, 2)))

def force_cell(pos_own, vel_own, smooth_own, energy_own, rho_own, valid_own, pos_near, vel_near, smooth_near, energy_near, rho_near, mass_near):
    gap = pos_own[None, :, :, None] - pos_near[:, :, None, :]
    dist_sq = lax.optimization_barrier(jnp.sum(gap * gap, axis=1))
    slope_own = kernel_slope(dist_sq, smooth_own[None, :, None])
    slope_near = kernel_slope(dist_sq, smooth_near[:, None, :])
    press_own = gas_factor * rho_own * energy_own / (rho_own * rho_own)
    press_near = gas_factor * rho_near * energy_near / (rho_near * rho_near)
    coeff = mass_near[:, None, :] * (press_own[None, :, None] * slope_own + press_near[:, None, :] * slope_near)
    accel = -lax.optimization_barrier(jnp.sum(coeff[:, None, :, :] * gap, axis=(0, 3)))
    vel_gap = vel_own[None, :, :, None] - vel_near[:, :, None, :]
    inner = lax.optimization_barrier(jnp.sum(vel_gap * gap, axis=1))
    rate = press_own * lax.optimization_barrier(jnp.sum(mass_near[:, None, :] * slope_own * inner, axis=(0, 2)))
    stacked = jnp.concatenate([rho_own[None, :], accel, rate[None, :]], axis=0)
    return stacked * valid_own[None, :]

def reference(positions, velocity, mass, smoothing, energy, density_old, counts, active, neighbours):
    valid = (jnp.arange(128, dtype=jnp.int32)[None, :] < counts[:, None]).astype(jnp.float32)
    weighed = mass * valid
    shifts = cell_shifts()

    def one_density(index):
        cell = active[index]
        near = neighbours[index]
        pos_near = positions[near] + shifts[:, :, None]
        fresh = density_cell(positions[cell], smoothing[cell], pos_near, weighed[near])
        return jnp.where(valid[cell] > 0, fresh, density_old[cell])
    fresh_rho = lax.map(one_density, jnp.arange(ACTIVE, dtype=jnp.int32))
    table = density_old.at[active].set(fresh_rho)

    def one_force(index):
        cell = active[index]
        near = neighbours[index]
        pos_near = positions[near] + shifts[:, :, None]
        return force_cell(positions[cell], velocity[cell], smoothing[cell], energy[cell], fresh_rho[index], valid[cell], pos_near, velocity[near], smoothing[near], energy[near], table[near], weighed[near])
    return lax.map(one_force, jnp.arange(ACTIVE, dtype=jnp.int32))
```

```python
import math

import jax
import jax.numpy as jnp
import numpy as np
from jax import lax
from jax.experimental import pallas as pl
from jax.experimental.pallas import tpu as pltpu
from jax.sharding import PartitionSpec as P

MESH = pl.DeviceIdType.MESH
NORM = 8.0 / math.pi
GAS = 2.0 / 3.0
TINY = 1e-14
LIMIT = 56 * 1024 * 1024

STEPS = (16, 4, 20, 1, 5, 17, 21)
WIDE = ((2, 8), (0, 6), (0, 7), (1, 2), (1, 5))
EDGE = ((6, 8), (5, 6), (5, 7), (4, 2), (4, 5), (3, 0), (3, 1), (3, 3), (3, 4))
HOME = (0, 1, 3, 4)
SPAN = 47


def shift_tiles():
    tiles = np.zeros((27, 8, 128), np.float32)
    for slot in range(27):
        tiles[slot, 1] = slot // 9 - 1.5
        tiles[slot, 2] = slot // 3 % 3 - 1.5
        tiles[slot, 3] = slot % 3 - 1.5
    return tiles


def greet(me, devices):
    barrier = pltpu.get_barrier_semaphore()
    for steps in STEPS:
        for other in (me + steps, me + devices - steps):
            pl.semaphore_signal(barrier, inc=1, device_id=(lax.rem(other, devices),), device_id_type=MESH)
    pl.semaphore_wait(barrier, 2 * len(STEPS))


def gather_kernel(
    devices, req_ref, req_send, counts_ref, pos_ref, vel_ref, mass_ref, smooth_ref,
    near_ref, asked_ref, send_ref, edge_ref, lists_ref, ask_out, ask_in, send_sem, recv_sem, local_sem,
):
    me = lax.axis_index("dom")
    cells = mass_ref.shape[0]
    first = me * cells
    lane = lax.broadcasted_iota(jnp.int32, (1, 128), 1)

    def fill(dst, place, cell):
        cell = jnp.clip(cell - first, 0, cells - 1)
        keep = lane < counts_ref[cell]
        dst[place, 0:1, :] = jnp.where(keep, mass_ref[pl.ds(cell, 1), :], 0.0)
        for axis in range(3):
            dst[place, 1 + axis : 2 + axis, :] = pos_ref[axis, pl.ds(cell, 1), :]
            dst[place, 4 + axis : 5 + axis, :] = vel_ref[axis, pl.ds(cell, 1), :]
        dst[place, 7:8, :] = smooth_ref[pl.ds(cell, 1), :]

    greet(me, devices)
    asks = []
    for place, steps in enumerate(STEPS):
        ask = pltpu.make_async_remote_copy(
            req_send, asked_ref.at[place], ask_out.at[place], ask_in.at[place],
            device_id=(lax.rem(me + steps, devices),), device_id_type=MESH,
        )
        ask.start()
        asks.append(ask)

    def home_step(entry, carry):
        for block in HOME:
            fill(near_ref, block * 48 + entry, req_ref[block, entry])
        return carry

    lax.fori_loop(0, SPAN, home_step, 0)
    for ask in asks:
        ask.wait()
    listed = pltpu.make_async_copy(asked_ref, lists_ref, local_sem)
    listed.start()
    listed.wait()
    copies = []

    def requester(place):
        return (lax.rem(me + devices - STEPS[place], devices),)

    def serve(group, start):
        def step(entry, carry):
            for place, block in group:
                fill(send_ref, block * 48 + entry, lists_ref[place, block, entry])
            return carry

        lax.fori_loop(0, SPAN, step, 0)
        for number, (place, block) in enumerate(group):
            rows = pl.ds(block * 48, SPAN)
            copy = pltpu.make_async_remote_copy(
                send_ref.at[rows], near_ref.at[rows], send_sem.at[start + number], recv_sem.at[start + number],
                device_id=requester(place), device_id_type=MESH,
            )
            copy.start()
            copies.append(copy)

    serve(WIDE[:3], 0)
    serve(WIDE[3:], 3)
    for number, (place, block) in enumerate(EDGE):
        fill(edge_ref, number, lists_ref[place, block, SPAN])
        copy = pltpu.make_async_remote_copy(
            edge_ref.at[number], near_ref.at[block * 48 + SPAN], send_sem.at[5 + number], recv_sem.at[5 + number],
            device_id=requester(place), device_id_type=MESH,
        )
        copy.start()
        copies.append(copy)
    for copy in copies:
        copy.wait()


def pieces(value):
    one = value.astype(jnp.bfloat16).astype(jnp.float32)
    rest = value - one
    two = rest.astype(jnp.bfloat16).astype(jnp.float32)
    return one, two, rest - two


def row_ids():
    return lax.broadcasted_iota(jnp.int32, (8, 128), 0)


def own_side(tile):
    rows = row_ids()
    near = tile - 0.5
    square = near * near
    norm = square[1:2] + square[2:3] + square[3:4]
    left = jnp.where(rows == 0, norm, jnp.where(rows < 4, -2.0 * near, jnp.where(rows == 4, 1.0, 0.0)))
    one, two, three = pieces(left)
    return jnp.concatenate([one, one, one, two, two, three], axis=0).T.astype(jnp.bfloat16)


def near_side(moved):
    rows = row_ids()
    square = moved * moved
    norm = square[1:2] + square[2:3] + square[3:4]
    right = jnp.where(rows == 0, 1.0, jnp.where(rows == 4, norm, moved))
    one, two, three = pieces(right)
    return jnp.concatenate([one, two, three, one, two, one], axis=0).astype(jnp.bfloat16)


def column(row):
    return jnp.broadcast_to(row, (128, 128)).T


def density_kernel(
    req_ref, lists_ref, counts_ref, active_ref, near_ref, shift_ref, energy_ref, old_ref,
    fresh_ref, mine_ref, edge_ref, table_ref, inv_ref,
):
    cells = old_ref.shape[0]
    first = lax.axis_index("dom") * cells
    lane = lax.broadcasted_iota(jnp.int32, (1, 128), 1)
    table_ref[...] = GAS * energy_ref[...] / old_ref[...]

    def row_step(row, carry):
        own = near_ref[13 * 16 + row]
        left = own_side(own)
        inverse = 1.0 / own[7:8]
        inv_ref[...] = column(inverse)

        def slot_step(slot, sums):
            tile = near_ref[slot * 16 + row]
            dist = jnp.dot(left, near_side(tile + shift_ref[slot]), preferred_element_type=jnp.float32)
            mass = tile[0:1]
            totals = []
            for part in range(8):
                square = jnp.maximum(dist[part * 16 : part * 16 + 16], TINY)
                ratio = square * lax.rsqrt(square) * inv_ref[part * 16 : part * 16 + 16, :]
                outer = 1.0 - jnp.minimum(ratio, 1.0)
                inner = 1.0 - jnp.minimum(ratio + ratio, 1.0)
                weight = (outer + outer) * (outer * outer) - inner * (inner * inner)
                totals.append(sums[part] + weight * mass)
            return tuple(totals)

        zero = jnp.zeros((16, 128), jnp.float32)
        sums = lax.fori_loop(0, 27, slot_step, (zero,) * 8, unroll=3)
        total = jnp.sum(jnp.concatenate(sums, axis=0).T, axis=0, keepdims=True)
        cell = active_ref[row] - first
        fresh = jnp.where(
            lane < counts_ref[cell], total * (NORM * inverse * inverse * inverse), old_ref[pl.ds(cell, 1), :]
        )
        fresh_ref[row] = fresh
        table_ref[pl.ds(cell, 1), :] = GAS * energy_ref[pl.ds(cell, 1), :] / fresh
        return carry

    lax.fori_loop(0, 16, row_step, 0)

    def collect(entry, carry):
        for block in HOME:
            mine_ref[block * 48 + entry] = table_ref[pl.ds(req_ref[block, entry] - first, 1), :]
        for place, block in WIDE:
            mine_ref[block * 48 + entry] = table_ref[pl.ds(lists_ref[place, block, entry] - first, 1), :]
        return carry

    lax.fori_loop(0, SPAN, collect, 0)
    for number, (place, block) in enumerate(EDGE):
        mine_ref[block * 48 + SPAN] = jnp.zeros((1, 128), jnp.float32)
        edge_ref[number] = table_ref[pl.ds(lists_ref[place, block, SPAN] - first, 1), :]


def pass_kernel(devices, mine_ref, edge_ref, near_ref, send_sem, recv_sem, local_sem):
    me = lax.axis_index("dom")
    greet(me, devices)
    copies = []

    def requester(place):
        return (lax.rem(me + devices - STEPS[place], devices),)

    for number, (place, block) in enumerate(WIDE):
        rows = pl.ds(block * 48, SPAN)
        copies.append(
            pltpu.make_async_remote_copy(
                mine_ref.at[rows], near_ref.at[rows], send_sem.at[number], recv_sem.at[number],
                device_id=requester(place), device_id_type=MESH,
            )
        )
    for number, (place, block) in enumerate(EDGE):
        copies.append(
            pltpu.make_async_remote_copy(
                edge_ref.at[number], near_ref.at[block * 48 + SPAN], send_sem.at[5 + number], recv_sem.at[5 + number],
                device_id=requester(place), device_id_type=MESH,
            )
        )
    for number, block in enumerate(HOME):
        rows = pl.ds(block * 48, SPAN)
        copies.append(pltpu.make_async_copy(mine_ref.at[rows], near_ref.at[rows], local_sem.at[number]))
    for copy in copies:
        copy.start()
    for copy in copies:
        copy.wait()


def slope(ratio):
    low = jnp.minimum(ratio, 1.0)
    high = jnp.minimum(ratio + ratio, 1.0)
    return (high - low) * (2.0 - (low + high))


def split(value):
    high = value.astype(jnp.bfloat16)
    return high, (value - high.astype(jnp.float32)).astype(jnp.bfloat16)


def split_rows(value):
    high = value.astype(jnp.bfloat16).astype(jnp.float32)
    both = jnp.concatenate([high, value - high], axis=0).astype(jnp.bfloat16)
    return jnp.concatenate([both, both], axis=1)


def pair_sum(rows, pairs):
    return lax.dot_general(rows, pairs, (((1,), (1,)), ((), ())), preferred_element_type=jnp.float32)


def force_kernel(
    counts_ref, active_ref, near_ref, press_ref, shift_ref, fresh_ref, hydro_ref, inv_ref,
):
    cells = counts_ref.shape[0]
    first = lax.axis_index("dom") * cells
    lane = lax.broadcasted_iota(jnp.int32, (1, 128), 1)
    rows = row_ids()

    def row_step(row, carry):
        own = near_ref[13 * 16 + row]
        left = own_side(own)
        inverse = 1.0 / own[7:8]
        inv_ref[...] = column(inverse)

        def slot_step(slot, sums):
            tile = near_ref[slot * 16 + row]
            moved = tile + shift_ref[slot]
            dist = jnp.dot(left, near_side(moved), preferred_element_type=jnp.float32)
            near_inv = 1.0 / tile[7:8]
            near_sq = near_inv * near_inv
            near_rows = jnp.broadcast_to(near_inv, (16, 128))
            work = moved[1:2] * tile[4:5] + moved[2:3] * tile[5:6] + moved[3:4] * tile[6:7]
            terms = tile[0:1] * jnp.where(rows == 0, 1.0, jnp.where(rows == 7, work, moved))
            press = terms * (press_ref[slot * 16 + row] * (near_sq * near_sq))
            own_pairs, own_rest, near_pairs, near_rest = [], [], [], []
            for part in range(8):
                square = jnp.maximum(dist[part * 16 : part * 16 + 16], TINY)
                root = lax.rsqrt(square)
                gap = square * root
                high, low = split(slope(gap * inv_ref[part * 16 : part * 16 + 16, :]) * root)
                own_pairs.append(high)
                own_rest.append(low)
                high, low = split(slope(gap * near_rows) * root)
                near_pairs.append(high)
                near_rest.append(low)
            def joined(high, low):
                return jnp.concatenate([jnp.concatenate(high, axis=0), jnp.concatenate(low, axis=0)], axis=1)

            return (
                sums[0] + pair_sum(split_rows(terms), joined(own_pairs, own_rest)),
                sums[1] + pair_sum(split_rows(press), joined(near_pairs, near_rest)),
            )

        zero = jnp.zeros((16, 128), jnp.float32)
        sums = lax.fori_loop(0, 27, slot_step, (zero, zero), unroll=3)
        by_own = sums[0][0:8] + sums[0][8:16]
        by_near = sums[1][0:8] + sums[1][8:16]
        place = own - 0.5
        inv_sq = inverse * inverse
        factor = (-6.0 * NORM) * (inv_sq * inv_sq) * press_ref[13 * 16 + row]
        accel = []
        rate = by_own[7:8]
        for axis in range(3):
            at = place[1 + axis : 2 + axis]
            speed = own[4 + axis : 5 + axis]
            pull = at * by_own[0:1] - by_own[1 + axis : 2 + axis]
            push = at * by_near[0:1] - by_near[1 + axis : 2 + axis]
            accel.append(-(factor * pull + (-6.0 * NORM) * push))
            rate = rate + speed * pull - at * by_own[4 + axis : 5 + axis]
        cell = active_ref[row] - first
        keep = lane < counts_ref[cell]
        values = jnp.concatenate([fresh_ref[row]] + accel + [factor * rate], axis=0)
        hydro_ref[row] = jnp.where(keep, values, 0.0)
        return carry

    lax.fori_loop(0, 16, row_step, 0)


def shards(positions, velocity, mass, smoothing, energy, density_old, counts, active, neighbours):
    devices = lax.axis_size("dom")
    vmem = pl.BlockSpec(memory_space=pltpu.VMEM)
    smem = pl.BlockSpec(memory_space=pltpu.SMEM)
    pos = jnp.transpose(positions, (1, 0, 2))
    vel = jnp.transpose(velocity, (1, 0, 2))
    requests = jnp.pad(neighbours.T.reshape(9, 48), ((0, 7), (0, 80)))
    shifts = jnp.asarray(shift_tiles())
    f32 = jnp.float32

    near, asked = pl.pallas_call(
        lambda *refs: gather_kernel(devices, *refs),
        out_shape=(jax.ShapeDtypeStruct((432, 8, 128), f32), jax.ShapeDtypeStruct((7, 16, 128), jnp.int32)),
        in_specs=[smem, vmem, smem, vmem, vmem, vmem, vmem],
        out_specs=(vmem, vmem),
        scratch_shapes=[
            pltpu.VMEM((432, 8, 128), f32),
            pltpu.VMEM((9, 8, 128), f32),
            pltpu.SMEM((7, 16, 128), jnp.int32),
            pltpu.SemaphoreType.DMA((7,)),
            pltpu.SemaphoreType.DMA((7,)),
            pltpu.SemaphoreType.DMA((14,)),
            pltpu.SemaphoreType.DMA((14,)),
            pltpu.SemaphoreType.DMA,
        ],
        compiler_params=pltpu.CompilerParams(collective_id=0, has_side_effects=True, vmem_limit_bytes=LIMIT),
    )(requests, requests, counts, pos, vel, mass, smoothing)

    fresh, mine, edge = pl.pallas_call(
        density_kernel,
        out_shape=(
            jax.ShapeDtypeStruct((16, 1, 128), f32),
            jax.ShapeDtypeStruct((432, 1, 128), f32),
            jax.ShapeDtypeStruct((9, 1, 128), f32),
        ),
        in_specs=[smem, smem, smem, smem, vmem, vmem, vmem, vmem],
        out_specs=(vmem, vmem, vmem),
        scratch_shapes=[pltpu.VMEM((1600, 128), f32), pltpu.VMEM((128, 128), f32)],
        compiler_params=pltpu.CompilerParams(vmem_limit_bytes=LIMIT),
    )(requests, asked, counts, active, near, shifts, energy, density_old)

    press = pl.pallas_call(
        lambda *refs: pass_kernel(devices, *refs),
        out_shape=jax.ShapeDtypeStruct((432, 1, 128), f32),
        in_specs=[vmem, vmem],
        out_specs=vmem,
        scratch_shapes=[
            pltpu.SemaphoreType.DMA((14,)),
            pltpu.SemaphoreType.DMA((14,)),
            pltpu.SemaphoreType.DMA((4,)),
        ],
        compiler_params=pltpu.CompilerParams(collective_id=1, has_side_effects=True, vmem_limit_bytes=LIMIT),
    )(mine, edge)

    return pl.pallas_call(
        force_kernel,
        out_shape=jax.ShapeDtypeStruct((16, 5, 128), f32),
        in_specs=[smem, smem, vmem, vmem, vmem, vmem],
        out_specs=vmem,
        scratch_shapes=[pltpu.VMEM((128, 128), f32)],
        compiler_params=pltpu.CompilerParams(vmem_limit_bytes=LIMIT),
    )(counts, active, near, press, shifts, fresh)


def solution(mesh):
    placed = (
        P("dom", None, None),
        P("dom", None, None),
        P("dom", None),
        P("dom", None),
        P("dom", None),
        P("dom", None),
        P("dom"),
        P("dom"),
        P("dom", None),
    )
    return jax.shard_map(
        shards, mesh=mesh, in_specs=placed, out_specs=P("dom", None, None), check_vma=False
    )
```

```python
import math

import jax
import jax.numpy as jnp
import numpy as np
from jax import lax
from jax.experimental import pallas as pl
from jax.experimental.pallas import tpu as pltpu
from jax.sharding import PartitionSpec as P

MESH = pl.DeviceIdType.MESH
NORM = 8.0 / math.pi
GAS = 2.0 / 3.0
TINY = 1e-14
LIMIT = 56 * 1024 * 1024

STEPS = (16, 4, 20, 1, 5, 17, 21)
WIDE = ((2, 8), (0, 6), (0, 7), (1, 2), (1, 5))
EDGE = ((6, 8), (5, 6), (5, 7), (4, 2), (4, 5), (3, 0), (3, 1), (3, 3), (3, 4))
HOME = (0, 1, 3, 4)
SPAN = 47


def shift_tiles():
    tiles = np.zeros((27, 8, 128), np.float32)
    for slot in range(27):
        tiles[slot, 1] = slot // 9 - 1
        tiles[slot, 2] = slot // 3 % 3 - 1
        tiles[slot, 3] = slot % 3 - 1
    return tiles


def greet(me, devices):
    barrier = pltpu.get_barrier_semaphore()
    for steps in STEPS:
        for other in (me + steps, me + devices - steps):
            pl.semaphore_signal(barrier, inc=1, device_id=(lax.rem(other, devices),), device_id_type=MESH)
    pl.semaphore_wait(barrier, 2 * len(STEPS))


def gather_kernel(
    devices, req_ref, req_send, counts_ref, pos_ref, vel_ref, mass_ref, smooth_ref,
    near_ref, asked_ref, send_ref, edge_ref, lists_ref, ask_out, ask_in, send_sem, recv_sem, local_sem,
):
    me = lax.axis_index("dom")
    cells = mass_ref.shape[0]
    first = me * cells
    lane = lax.broadcasted_iota(jnp.int32, (1, 128), 1)

    def fill(dst, place, cell):
        cell = jnp.clip(cell - first, 0, cells - 1)
        keep = lane < counts_ref[cell]
        dst[place, 0:1, :] = jnp.where(keep, mass_ref[pl.ds(cell, 1), :], 0.0)
        for axis in range(3):
            dst[place, 1 + axis : 2 + axis, :] = pos_ref[axis, pl.ds(cell, 1), :]
            dst[place, 4 + axis : 5 + axis, :] = vel_ref[axis, pl.ds(cell, 1), :]
        dst[place, 7:8, :] = smooth_ref[pl.ds(cell, 1), :]

    greet(me, devices)
    asks = []
    for place, steps in enumerate(STEPS):
        ask = pltpu.make_async_remote_copy(
            req_send, asked_ref.at[place], ask_out.at[place], ask_in.at[place],
            device_id=(lax.rem(me + steps, devices),), device_id_type=MESH,
        )
        ask.start()
        asks.append(ask)

    def home_step(entry, carry):
        for block in HOME:
            fill(near_ref, block * 48 + entry, req_ref[block, entry])
        return carry

    lax.fori_loop(0, SPAN, home_step, 0)
    for ask in asks:
        ask.wait()
    listed = pltpu.make_async_copy(asked_ref, lists_ref, local_sem)
    listed.start()
    listed.wait()
    copies = []

    def requester(place):
        return (lax.rem(me + devices - STEPS[place], devices),)

    def serve(group, start):
        def step(entry, carry):
            for place, block in group:
                fill(send_ref, block * 48 + entry, lists_ref[place, block, entry])
            return carry

        lax.fori_loop(0, SPAN, step, 0)
        for number, (place, block) in enumerate(group):
            rows = pl.ds(block * 48, SPAN)
            copy = pltpu.make_async_remote_copy(
                send_ref.at[rows], near_ref.at[rows], send_sem.at[start + number], recv_sem.at[start + number],
                device_id=requester(place), device_id_type=MESH,
            )
            copy.start()
            copies.append(copy)

    serve(WIDE[:3], 0)
    serve(WIDE[3:], 3)
    for number, (place, block) in enumerate(EDGE):
        fill(edge_ref, number, lists_ref[place, block, SPAN])
        copy = pltpu.make_async_remote_copy(
            edge_ref.at[number], near_ref.at[block * 48 + SPAN], send_sem.at[5 + number], recv_sem.at[5 + number],
            device_id=requester(place), device_id_type=MESH,
        )
        copy.start()
        copies.append(copy)
    for copy in copies:
        copy.wait()


def rows_of(ref, slot, feature):
    return ref[pl.ds(slot * 128 + feature, 16, stride=8), :]


def pick(values, index):
    return jnp.take_along_axis(values, index, axis=1, mode="promise_in_bounds")


def eye():
    return lax.broadcasted_iota(jnp.int32, (128, 128), 0) == lax.broadcasted_iota(jnp.int32, (128, 128), 1)


def column(row):
    return jnp.broadcast_to(jnp.sum(jnp.where(eye(), row, 0.0), axis=1, keepdims=True), (128, 128))


def row_sums(pairs):
    total = jnp.sum(pairs, axis=1, keepdims=True)
    return jnp.sum(jnp.where(eye(), total, 0.0), axis=0, keepdims=True)


def list_jobs(offs_ref, jobs_ref):
    def one_row(row, count):
        def one_chunk(chunk, count):
            jobs_ref[count] = row * 32 + chunk
            return count + 1

        return lax.fori_loop(0, (offs_ref[27, row] + 127) // 128, one_chunk, count)

    return lax.fori_loop(0, 16, one_row, 0)


def pack_rows(offs_ref, row, get, put, width):
    lane = lax.broadcasted_iota(jnp.int32, (width, 128), 1)

    def slot_step(slot, held):
        begin = offs_ref[slot, row]
        end = offs_ref[slot + 1, row]
        turned = get(slot)
        merged = jnp.where(lane >= begin % 128, turned, held)
        put(begin // 128, merged)
        return jnp.where(jnp.broadcast_to(end // 128 > begin // 128, (width, 128)), turned, merged)

    return lax.fori_loop(0, 27, slot_step, get(0), unroll=3)


def density_kernel(
    req_ref, lists_ref, counts_ref, active_ref, near_ref, shift_ref, energy_ref, old_ref,
    fresh_ref, mine_ref, edge_ref, pack_ref, index_ref, offs_out_ref,
    table_ref, mask_ref, offs_ref, jobs_ref, x_ref, y_ref, z_ref, inv_ref, sum_ref, local_sem,
):
    cells = old_ref.shape[0]
    first = lax.axis_index("dom") * cells
    lane = lax.broadcasted_iota(jnp.int32, (1, 128), 1)
    lanes = lax.broadcasted_iota(jnp.int32, (16, 128), 1)
    on_diagonal = lax.broadcasted_iota(jnp.int32, (16, 128), 0) == lanes

    lows, highs = [], []
    for axis in range(3):
        own = rows_of(near_ref, 13, 1 + axis)
        lows.append(jnp.min(own, axis=1, keepdims=True))
        highs.append(jnp.max(own, axis=1, keepdims=True))
    widest = jnp.max(rows_of(near_ref, 13, 7), axis=1, keepdims=True)

    def mask_step(slot, carry):
        away = jnp.zeros((16, 128), jnp.float32)
        for axis, step in enumerate((slot // 9, slot // 3 % 3, slot % 3)):
            at = rows_of(near_ref, slot, 1 + axis) + (step - 1).astype(jnp.float32)
            out = jnp.maximum(jnp.maximum(lows[axis] - at, at - highs[axis]), 0.0)
            away = away + out * out
        reach = jnp.maximum(rows_of(near_ref, slot, 7), widest)
        chosen = (rows_of(near_ref, slot, 0) > 0.0) & (away <= reach * reach * 1.0001)
        mask_ref[pl.ds(slot * 16, 16), :] = jnp.where(chosen, 1.0, 0.0)
        return carry

    lax.fori_loop(0, 27, mask_step, 0, unroll=3)
    high = lax.broadcasted_iota(jnp.int32, (128, 256), 0)
    wide = lax.broadcasted_iota(jnp.int32, (128, 256), 1)
    counter = jnp.where((wide >= 128) | (high <= wide), 1.0, 0.0).astype(jnp.bfloat16)

    def rank_step(slot, begin):
        chosen = mask_ref[pl.ds(slot * 16, 16), :].astype(jnp.bfloat16)
        ranks = jnp.dot(chosen, counter, preferred_element_type=jnp.float32).astype(jnp.int32)
        order = ranks[:, 0:128]
        wanted = (lanes - begin) & 127
        index = jnp.zeros((16, 128), jnp.int32)
        for step in (64, 32, 16, 8, 4, 2, 1):
            index = index + jnp.where(pick(order, index + (step - 1)) <= wanted, step, 0)
        index_ref[pl.ds(slot * 16, 16), :] = index
        offs_out_ref[pl.ds(slot, 1), :] = jnp.sum(jnp.where(on_diagonal, begin, 0), axis=0, keepdims=True)
        return begin + ranks[:, 128:256]

    total = lax.fori_loop(0, 27, rank_step, jnp.zeros((16, 128), jnp.int32), unroll=3)
    offs_out_ref[27:28, :] = jnp.sum(jnp.where(on_diagonal, total, 0), axis=0, keepdims=True)
    offs_out_ref[28:32, :] = jnp.zeros((4, 128), jnp.int32)
    moved = pltpu.make_async_copy(offs_out_ref, offs_ref, local_sem)
    moved.start()
    table_ref[...] = GAS * energy_ref[...] / old_ref[...]

    def own_step(row, carry):
        own = near_ref[pl.ds(1664 + row * 8, 8), :]
        at = pl.ds(row * 128, 128)
        x_ref[at, :] = column(own[1:2])
        y_ref[at, :] = column(own[2:3])
        z_ref[at, :] = column(own[3:4])
        inv_ref[at, :] = column(1.0 / own[7:8])
        sum_ref[at, :] = jnp.zeros((128, 128), jnp.float32)
        return carry

    lax.fori_loop(0, 16, own_step, 0)
    moved.wait()

    def pack_step(row, carry):
        def get(slot):
            tile = near_ref[pl.ds((slot * 16 + row) * 8, 8), :] + shift_ref[slot]
            index = index_ref[pl.ds(slot * 16 + row, 1), :]
            return pick(tile, jnp.broadcast_to(index, (8, 128)))

        def put(chunk, tile):
            pack_ref[row * 28 + chunk] = tile

        held = pack_rows(offs_ref, row, get, put, 8)
        total = offs_ref[27, row]
        wide = lax.broadcasted_iota(jnp.int32, (8, 128), 1)
        deep = lax.broadcasted_iota(jnp.int32, (8, 128), 0)
        put(total // 128, jnp.where((deep == 0) & (wide >= total % 128), 0.0, held))
        return carry

    lax.fori_loop(0, 16, pack_step, 0)
    count = list_jobs(offs_ref, jobs_ref)

    def job_step(job, carry):
        code = jobs_ref[job]
        row = code // 32
        tile = pack_ref[row * 28 + code % 32]
        mass, near_x, near_y, near_z = [jnp.broadcast_to(tile[f : f + 1], (8, 128)) for f in range(4)]
        for part in range(16):
            at = pl.ds(row * 128 + part * 8, 8)
            gap_x = x_ref[at, :] - near_x
            gap_y = y_ref[at, :] - near_y
            gap_z = z_ref[at, :] - near_z
            square = jnp.maximum(gap_x * gap_x + gap_y * gap_y + gap_z * gap_z, TINY)
            ratio = square * lax.rsqrt(square) * inv_ref[at, :]
            outer = 1.0 - jnp.minimum(ratio, 1.0)
            inner = 1.0 - jnp.minimum(ratio + ratio, 1.0)
            weight = (outer + outer) * (outer * outer) - inner * (inner * inner)
            sum_ref[at, :] = sum_ref[at, :] + weight * mass
        return carry

    lax.fori_loop(0, count, job_step, 0)

    def end_step(row, carry):
        own = near_ref[pl.ds(1664 + row * 8, 8), :]
        inverse = 1.0 / own[7:8]
        total = row_sums(sum_ref[pl.ds(row * 128, 128), :])
        cell = active_ref[row] - first
        fresh = jnp.where(
            lane < counts_ref[cell], total * (NORM * inverse * inverse * inverse), old_ref[pl.ds(cell, 1), :]
        )
        fresh_ref[row] = fresh
        table_ref[pl.ds(cell, 1), :] = GAS * energy_ref[pl.ds(cell, 1), :] / fresh
        return carry

    lax.fori_loop(0, 16, end_step, 0)

    def collect(entry, carry):
        for block in HOME:
            mine_ref[block * 48 + entry] = table_ref[pl.ds(req_ref[block, entry] - first, 1), :]
        for place, block in WIDE:
            mine_ref[block * 48 + entry] = table_ref[pl.ds(lists_ref[place, block, entry] - first, 1), :]
        return carry

    lax.fori_loop(0, SPAN, collect, 0)
    for number, (place, block) in enumerate(EDGE):
        mine_ref[block * 48 + SPAN] = jnp.zeros((1, 128), jnp.float32)
        edge_ref[number] = table_ref[pl.ds(lists_ref[place, block, SPAN] - first, 1), :]


def pass_kernel(devices, mine_ref, edge_ref, near_ref, send_sem, recv_sem, local_sem):
    me = lax.axis_index("dom")
    greet(me, devices)
    copies = []

    def requester(place):
        return (lax.rem(me + devices - STEPS[place], devices),)

    for number, (place, block) in enumerate(WIDE):
        rows = pl.ds(block * 48, SPAN)
        copies.append(
            pltpu.make_async_remote_copy(
                mine_ref.at[rows], near_ref.at[rows], send_sem.at[number], recv_sem.at[number],
                device_id=requester(place), device_id_type=MESH,
            )
        )
    for number, (place, block) in enumerate(EDGE):
        copies.append(
            pltpu.make_async_remote_copy(
                edge_ref.at[number], near_ref.at[block * 48 + SPAN], send_sem.at[5 + number], recv_sem.at[5 + number],
                device_id=requester(place), device_id_type=MESH,
            )
        )
    for number, block in enumerate(HOME):
        rows = pl.ds(block * 48, SPAN)
        copies.append(pltpu.make_async_copy(mine_ref.at[rows], near_ref.at[rows], local_sem.at[number]))
    for copy in copies:
        copy.start()
    for copy in copies:
        copy.wait()


def slope(ratio):
    low = jnp.minimum(ratio, 1.0)
    high = jnp.minimum(ratio + ratio, 1.0)
    return (high - low) * (2.0 - (low + high))


def force_kernel(
    counts_ref, active_ref, offs_ref, near_ref, press_ref, pack_ref, index_ref, fresh_ref,
    hydro_ref, turned_ref, chunk_ref, jobs_ref, x_ref, y_ref, z_ref, vx_ref, vy_ref, vz_ref, inv_ref, own_ref,
    ax_ref, ay_ref, az_ref, rate_ref,
):
    cells = counts_ref.shape[0]
    first = lax.axis_index("dom") * cells
    lane = lax.broadcasted_iota(jnp.int32, (1, 128), 1)

    def turn_step(slot, carry):
        at = pl.ds(slot * 16, 16)
        turned_ref[at, :] = pick(press_ref[at, :], index_ref[at, :])
        return carry

    lax.fori_loop(0, 27, turn_step, 0, unroll=3)

    def own_step(row, carry):
        own = near_ref[pl.ds(1664 + row * 8, 8), :]
        at = pl.ds(row * 128, 128)
        inverse = 1.0 / own[7:8]
        inv_sq = inverse * inverse
        for ref, value in (
            (x_ref, own[1:2]), (y_ref, own[2:3]), (z_ref, own[3:4]),
            (vx_ref, own[4:5]), (vy_ref, own[5:6]), (vz_ref, own[6:7]),
            (inv_ref, inverse), (own_ref, (6.0 * NORM) * (inv_sq * inv_sq) * press_ref[pl.ds(208 + row, 1), :]),
        ):
            ref[at, :] = column(value)
        for ref in (ax_ref, ay_ref, az_ref, rate_ref):
            ref[at, :] = jnp.zeros((128, 128), jnp.float32)

        def get(slot):
            return turned_ref[pl.ds(slot * 16 + row, 1), :]

        def put(chunk, value):
            chunk_ref[pl.ds(row * 28 + chunk, 1), :] = value

        held = pack_rows(offs_ref, row, get, put, 1)
        put(offs_ref[27, row] // 128, held)
        return carry

    lax.fori_loop(0, 16, own_step, 0)
    count = list_jobs(offs_ref, jobs_ref)

    def job_step(job, carry):
        code = jobs_ref[job]
        row = code // 32
        place = row * 28 + code % 32
        tile = pack_ref[place]
        near_inv = 1.0 / tile[7:8]
        near_sq = near_inv * near_inv
        push = (6.0 * NORM) * tile[0:1] * (near_sq * near_sq) * chunk_ref[pl.ds(place, 1), :]
        mass, near_x, near_y, near_z, near_vx, near_vy, near_vz = [
            jnp.broadcast_to(tile[f : f + 1], (8, 128)) for f in range(7)
        ]
        near_inv = jnp.broadcast_to(near_inv, (8, 128))
        push = jnp.broadcast_to(push, (8, 128))
        for part in range(16):
            at = pl.ds(row * 128 + part * 8, 8)
            gap_x = x_ref[at, :] - near_x
            gap_y = y_ref[at, :] - near_y
            gap_z = z_ref[at, :] - near_z
            square = jnp.maximum(gap_x * gap_x + gap_y * gap_y + gap_z * gap_z, TINY)
            root = lax.rsqrt(square)
            gap = square * root
            pull = slope(gap * inv_ref[at, :]) * root * mass
            both = own_ref[at, :] * pull + slope(gap * near_inv) * push * root
            work = (vx_ref[at, :] - near_vx) * gap_x + (vy_ref[at, :] - near_vy) * gap_y + (vz_ref[at, :] - near_vz) * gap_z
            ax_ref[at, :] = ax_ref[at, :] + both * gap_x
            ay_ref[at, :] = ay_ref[at, :] + both * gap_y
            az_ref[at, :] = az_ref[at, :] + both * gap_z
            rate_ref[at, :] = rate_ref[at, :] + pull * work
        return carry

    lax.fori_loop(0, count, job_step, 0)

    def end_step(row, carry):
        own = near_ref[pl.ds(1664 + row * 8, 8), :]
        inverse = 1.0 / own[7:8]
        inv_sq = inverse * inverse
        factor = (-6.0 * NORM) * (inv_sq * inv_sq) * press_ref[pl.ds(208 + row, 1), :]
        at = pl.ds(row * 128, 128)
        keep = lane < counts_ref[active_ref[row] - first]
        values = [fresh_ref[row]] + [row_sums(ref[at, :]) for ref in (ax_ref, ay_ref, az_ref)]
        values.append(factor * row_sums(rate_ref[at, :]))
        for number, value in enumerate(values):
            hydro_ref[number, pl.ds(row, 1), :] = jnp.where(keep, value, 0.0)
        return carry

    lax.fori_loop(0, 16, end_step, 0)


def specs(kinds):
    return [pl.BlockSpec(memory_space=pltpu.SMEM if kind == "s" else pltpu.VMEM) for kind in kinds]


def floats(*shape):
    return jax.ShapeDtypeStruct(shape, jnp.float32)


def density_call(*args):
    square = pltpu.VMEM((2048, 128), jnp.float32)
    return pl.pallas_call(
        density_kernel,
        out_shape=(
            floats(16, 1, 128), floats(432, 1, 128), floats(9, 1, 128), floats(448, 8, 128),
            jax.ShapeDtypeStruct((432, 128), jnp.int32), jax.ShapeDtypeStruct((32, 128), jnp.int32),
        ),
        in_specs=specs("ssssvvvv"),
        out_specs=tuple(specs("vvvvvv")),
        scratch_shapes=[
            pltpu.VMEM((1600, 128), jnp.float32), pltpu.VMEM((432, 128), jnp.float32),
            pltpu.SMEM((32, 128), jnp.int32), pltpu.SMEM((448,), jnp.int32),
        ] + [square] * 5 + [pltpu.SemaphoreType.DMA],
        compiler_params=pltpu.CompilerParams(vmem_limit_bytes=LIMIT),
        name="density",
    )(*args)


def force_call(*args):
    square = pltpu.VMEM((2048, 128), jnp.float32)
    return pl.pallas_call(
        force_kernel,
        out_shape=floats(5, 16, 128),
        in_specs=specs("sssvvvvv"),
        out_specs=specs("v")[0],
        scratch_shapes=[
            pltpu.VMEM((432, 128), jnp.float32), pltpu.VMEM((448, 128), jnp.float32), pltpu.SMEM((448,), jnp.int32),
        ] + [square] * 12,
        compiler_params=pltpu.CompilerParams(vmem_limit_bytes=LIMIT),
        name="force",
    )(*args)


def shards(positions, velocity, mass, smoothing, energy, density_old, counts, active, neighbours):
    devices = lax.axis_size("dom")
    vmem = pl.BlockSpec(memory_space=pltpu.VMEM)
    smem = pl.BlockSpec(memory_space=pltpu.SMEM)
    pos = jnp.transpose(positions, (1, 0, 2))
    vel = jnp.transpose(velocity, (1, 0, 2))
    requests = jnp.pad(neighbours.T.reshape(9, 48), ((0, 7), (0, 80)))
    shifts = jnp.asarray(shift_tiles())
    f32 = jnp.float32

    near, asked = pl.pallas_call(
        lambda *refs: gather_kernel(devices, *refs),
        out_shape=(jax.ShapeDtypeStruct((432, 8, 128), f32), jax.ShapeDtypeStruct((7, 16, 128), jnp.int32)),
        in_specs=[smem, vmem, smem, vmem, vmem, vmem, vmem],
        out_specs=(vmem, vmem),
        scratch_shapes=[
            pltpu.VMEM((432, 8, 128), f32),
            pltpu.VMEM((9, 8, 128), f32),
            pltpu.SMEM((7, 16, 128), jnp.int32),
            pltpu.SemaphoreType.DMA((7,)),
            pltpu.SemaphoreType.DMA((7,)),
            pltpu.SemaphoreType.DMA((14,)),
            pltpu.SemaphoreType.DMA((14,)),
            pltpu.SemaphoreType.DMA,
        ],
        compiler_params=pltpu.CompilerParams(collective_id=0, has_side_effects=True, vmem_limit_bytes=LIMIT),
    )(requests, requests, counts, pos, vel, mass, smoothing)

    flat = near.reshape(3456, 128)
    fresh, mine, edge, packed, index, offs = density_call(
        requests, asked, counts, active, flat, shifts, energy, density_old
    )

    press = pl.pallas_call(
        lambda *refs: pass_kernel(devices, *refs),
        out_shape=jax.ShapeDtypeStruct((432, 1, 128), f32),
        in_specs=[vmem, vmem],
        out_specs=vmem,
        scratch_shapes=[
            pltpu.SemaphoreType.DMA((14,)),
            pltpu.SemaphoreType.DMA((14,)),
            pltpu.SemaphoreType.DMA((4,)),
        ],
        compiler_params=pltpu.CompilerParams(collective_id=1, has_side_effects=True, vmem_limit_bytes=LIMIT),
    )(mine, edge)

    hydro = force_call(counts, active, offs, flat, press.reshape(432, 128), packed, index, fresh)
    return jnp.transpose(hydro, (1, 0, 2))


def solution(mesh):
    placed = (
        P("dom", None, None),
        P("dom", None, None),
        P("dom", None),
        P("dom", None),
        P("dom", None),
        P("dom", None),
        P("dom"),
        P("dom"),
        P("dom", None),
    )
    return jax.shard_map(
        shards, mesh=mesh, in_specs=placed, out_specs=P("dom", None, None), check_vma=False
    )
```

```python
import math

import jax
import jax.numpy as jnp
import numpy as np
from jax import lax
from jax.experimental import pallas as pl
from jax.experimental.pallas import tpu as pltpu
from jax.sharding import PartitionSpec as P

MESH = pl.DeviceIdType.MESH
NORM = 8.0 / math.pi
GAS = 2.0 / 3.0
TINY = 1e-14
LIMIT = 56 * 1024 * 1024

STEPS = (16, 4, 20, 1, 5, 17, 21)
WIDE = ((0, 6), (0, 7), (1, 2), (1, 5), (2, 8))
EDGE = ((6, 8), (5, 6), (5, 7), (4, 2), (4, 5), (3, 0), (3, 1), (3, 3), (3, 4))
HOME = (0, 1, 3, 4)
SPAN = 47


def shift_tiles():
    tiles = np.zeros((27, 8, 128), np.float32)
    for slot in range(27):
        tiles[slot, 1] = slot // 9 - 1
        tiles[slot, 2] = slot // 3 % 3 - 1
        tiles[slot, 3] = slot % 3 - 1
    return tiles


def greet(me, devices):
    barrier = pltpu.get_barrier_semaphore()
    for steps in STEPS:
        for other in (me + steps, me + devices - steps):
            pl.semaphore_signal(barrier, inc=1, device_id=(lax.rem(other, devices),), device_id_type=MESH)
    pl.semaphore_wait(barrier, 2 * len(STEPS))


def gather_kernel(
    devices, req_ref, req_send, counts_ref, pos_ref, vel_ref, mass_ref, smooth_ref,
    near_ref, asked_ref, send_ref, edge_ref, lists_ref, ask_out, ask_in, send_sem, recv_sem, local_sem,
):
    me = lax.axis_index("dom")
    cells = mass_ref.shape[0]
    first = me * cells
    lane = lax.broadcasted_iota(jnp.int32, (1, 128), 1)

    def fill(dst, place, cell):
        cell = jnp.clip(cell - first, 0, cells - 1)
        keep = lane < counts_ref[cell]
        dst[place, 0:1, :] = jnp.where(keep, mass_ref[pl.ds(cell, 1), :], 0.0)
        for axis in range(3):
            dst[place, 1 + axis : 2 + axis, :] = pos_ref[axis, pl.ds(cell, 1), :]
            dst[place, 4 + axis : 5 + axis, :] = vel_ref[axis, pl.ds(cell, 1), :]
        dst[place, 7:8, :] = 1.0 / smooth_ref[pl.ds(cell, 1), :]

    greet(me, devices)
    asks = []
    for place, steps in enumerate(STEPS):
        ask = pltpu.make_async_remote_copy(
            req_send, asked_ref.at[place], ask_out.at[place], ask_in.at[place],
            device_id=(lax.rem(me + steps, devices),), device_id_type=MESH,
        )
        ask.start()
        asks.append(ask)

    def home_step(entry, carry):
        for block in HOME:
            fill(near_ref, block * 48 + entry, req_ref[block, entry])
        return carry

    lax.fori_loop(0, SPAN, home_step, 0)
    copies = []

    def hear(place):
        asks[place].wait_recv()
        listed = pltpu.make_async_copy(asked_ref.at[place], lists_ref.at[place], local_sem.at[place])
        listed.start()
        listed.wait()

    def requester(place):
        return (lax.rem(me + devices - STEPS[place], devices),)

    def serve(group, start):
        def step(entry, carry):
            for place, block in group:
                fill(send_ref, block * 48 + entry, lists_ref[place, block, entry])
            return carry

        lax.fori_loop(0, SPAN, step, 0)
        for number, (place, block) in enumerate(group):
            rows = pl.ds(block * 48, SPAN)
            copy = pltpu.make_async_remote_copy(
                send_ref.at[rows], near_ref.at[rows], send_sem.at[start + number], recv_sem.at[start + number],
                device_id=requester(place), device_id_type=MESH,
            )
            copy.start()
            copies.append(copy)

    hear(0)
    serve(WIDE[0:2], 0)
    hear(1)
    serve(WIDE[2:4], 2)
    hear(2)
    serve(WIDE[4:5], 4)
    for place in (3, 4, 5, 6):
        hear(place)
    for number, (place, block) in enumerate(EDGE):
        fill(edge_ref, number, lists_ref[place, block, SPAN])
        copy = pltpu.make_async_remote_copy(
            edge_ref.at[number], near_ref.at[block * 48 + SPAN], send_sem.at[5 + number], recv_sem.at[5 + number],
            device_id=requester(place), device_id_type=MESH,
        )
        copy.start()
        copies.append(copy)
    for copy in copies:
        copy.wait()
    for ask in asks:
        ask.wait_send()


def rows_of(ref, slot, feature):
    return ref[pl.ds(slot * 128 + feature, 16, stride=8), :]


def pick(values, index):
    return jnp.take_along_axis(values, index, axis=1, mode="promise_in_bounds")


def eye():
    return lax.broadcasted_iota(jnp.int32, (128, 128), 0) == lax.broadcasted_iota(jnp.int32, (128, 128), 1)


def column(row):
    return jnp.broadcast_to(jnp.sum(jnp.where(eye(), row, 0.0), axis=1, keepdims=True), (128, 128))


def row_sums(pairs):
    total = jnp.sum(pairs, axis=1, keepdims=True)
    return jnp.sum(jnp.where(eye(), total, 0.0), axis=0, keepdims=True)


def list_jobs(offs_ref, counts_ref, active_ref, first, order_ref, jobs_ref):
    place = jnp.int32(0)
    ends = []
    for low, high in ((0, 80), (80, 96), (96, 112), (112, 128)):
        for row in range(16):
            own = counts_ref[active_ref[row] - first]
            order_ref[place] = row
            place = place + ((own > low) & (own <= high)).astype(jnp.int32)
        ends.append(place)
    count = jnp.int32(0)
    begin = jnp.int32(0)
    jobs_ref[512] = count
    for number, end in enumerate(ends):
        def one_row(place, count):
            row = order_ref[place]
            chunks = (offs_ref[27, row] + 127) // 128
            for chunk in range(10):
                jobs_ref[count + chunk] = row * 32 + chunk

            def one_chunk(chunk, carry):
                jobs_ref[count + chunk] = row * 32 + chunk
                return carry

            lax.fori_loop(10, chunks, one_chunk, 0)
            return count + chunks

        count = lax.fori_loop(begin, end, one_row, count)
        jobs_ref[count] = 31
        count = count + count % 2
        jobs_ref[513 + number] = count
        begin = end


def run_jobs(jobs_ref, step):
    for number, parts in enumerate((10, 12, 14, 16)):
        def two(pair, carry):
            step(2 * pair, parts)
            step(2 * pair + 1, parts)
            return carry

        lax.fori_loop(jobs_ref[512 + number] // 2, jobs_ref[513 + number] // 2, two, 0)


def pack_rows(offs_ref, row, get, put, width):
    lane = lax.broadcasted_iota(jnp.int32, (width, 128), 1)

    def slot_step(slot, held):
        begin = offs_ref[slot, row]
        end = offs_ref[slot + 1, row]
        turned = get(slot)
        merged = jnp.where(lane >= begin % 128, turned, held)
        put(begin // 128, merged)
        return jnp.where(jnp.broadcast_to(end // 128 > begin // 128, (width, 128)), turned, merged)

    return lax.fori_loop(0, 27, slot_step, get(0), unroll=27)


def density_kernel(
    req_ref, lists_ref, counts_ref, active_ref, near_ref, shift_ref, energy_ref, old_ref,
    fresh_ref, mine_ref, edge_ref, pack_ref, index_ref, offs_out_ref, jobs_ref,
    table_ref, mask_ref, offs_ref, order_ref, x_ref, y_ref, z_ref, inv_ref, sum_ref, local_sem,
):
    cells = old_ref.shape[0]
    first = lax.axis_index("dom") * cells
    lane = lax.broadcasted_iota(jnp.int32, (1, 128), 1)
    lanes = lax.broadcasted_iota(jnp.int32, (16, 128), 1)
    on_diagonal = lax.broadcasted_iota(jnp.int32, (16, 128), 0) == lanes

    lows, highs = [], []
    for axis in range(3):
        own = rows_of(near_ref, 13, 1 + axis)
        lows.append(jnp.min(own, axis=1, keepdims=True))
        highs.append(jnp.max(own, axis=1, keepdims=True))
    widest = jnp.min(rows_of(near_ref, 13, 7), axis=1, keepdims=True)

    def mask_step(slot, carry):
        away = jnp.zeros((16, 128), jnp.float32)
        for axis, step in enumerate((slot // 9, slot // 3 % 3, slot % 3)):
            at = rows_of(near_ref, slot, 1 + axis) + (step - 1).astype(jnp.float32)
            out = jnp.maximum(jnp.maximum(lows[axis] - at, at - highs[axis]), 0.0)
            away = away + out * out
        reach = jnp.minimum(rows_of(near_ref, slot, 7), widest)
        chosen = (rows_of(near_ref, slot, 0) > 0.0) & (away * (reach * reach) <= 1.0001)
        mask_ref[pl.ds(slot * 16, 16), :] = jnp.where(chosen, 1.0, 0.0)
        return carry

    lax.fori_loop(0, 27, mask_step, 0, unroll=27)
    high = lax.broadcasted_iota(jnp.int32, (128, 256), 0)
    wide = lax.broadcasted_iota(jnp.int32, (128, 256), 1)
    counter = jnp.where((wide >= 128) | (high <= wide), 1.0, 0.0).astype(jnp.bfloat16)

    def rank_step(slot, begin):
        chosen = mask_ref[pl.ds(slot * 16, 16), :].astype(jnp.bfloat16)
        ranks = jnp.dot(chosen, counter, preferred_element_type=jnp.float32).astype(jnp.int32)
        order = ranks[:, 0:128]
        wanted = (lanes - begin) & 127
        index = jnp.zeros((16, 128), jnp.int32)
        for step in (64, 32, 16, 8, 4, 2, 1):
            index = index + jnp.where(pick(order, index + (step - 1)) <= wanted, step, 0)
        index_ref[pl.ds(slot * 16, 16), :] = index
        offs_out_ref[pl.ds(slot, 1), :] = jnp.sum(jnp.where(on_diagonal, begin, 0), axis=0, keepdims=True)
        return begin + ranks[:, 128:256]

    total = lax.fori_loop(0, 27, rank_step, jnp.zeros((16, 128), jnp.int32), unroll=27)
    offs_out_ref[27:28, :] = jnp.sum(jnp.where(on_diagonal, total, 0), axis=0, keepdims=True)
    offs_out_ref[28:32, :] = jnp.zeros((4, 128), jnp.int32)
    moved = pltpu.make_async_copy(offs_out_ref, offs_ref, local_sem)
    moved.start()
    table_ref[...] = GAS * energy_ref[...] / old_ref[...]

    def own_step(row, carry):
        own = near_ref[pl.ds(1664 + row * 8, 8), :]
        for ref, feature in ((x_ref, 1), (y_ref, 2), (z_ref, 3), (inv_ref, 7)):
            ref[pl.ds(row * 128, 128), :] = column(own[feature : feature + 1])
        sum_ref[pl.ds(row * 128, 128), :] = jnp.zeros((128, 128), jnp.float32)
        return carry

    lax.fori_loop(0, 16, own_step, 0)
    moved.wait()

    def pack_step(row, carry):
        def get(slot):
            tile = near_ref[pl.ds((slot * 16 + row) * 8, 8), :] + shift_ref[slot]
            index = index_ref[pl.ds(slot * 16 + row, 1), :]
            return pick(tile, jnp.broadcast_to(index, (8, 128)))

        def put(chunk, tile):
            pack_ref[row * 32 + chunk] = tile

        held = pack_rows(offs_ref, row, get, put, 8)
        total = offs_ref[27, row]
        wide = lax.broadcasted_iota(jnp.int32, (8, 128), 1)
        deep = lax.broadcasted_iota(jnp.int32, (8, 128), 0)
        put(total // 128, jnp.where((deep == 0) & (wide >= total % 128), 0.0, held))
        put(31, jnp.where(deep == 0, 0.0, held))
        return carry

    lax.fori_loop(0, 16, pack_step, 0)
    list_jobs(offs_ref, counts_ref, active_ref, first, order_ref, jobs_ref)

    def job_step(job, parts):
        code = jobs_ref[job]
        row = code // 32
        tile = pack_ref[code]
        mass, near_x, near_y, near_z = [jnp.broadcast_to(tile[f : f + 1], (8, 128)) for f in range(4)]
        for part in range(parts):
            at = pl.ds(row * 128 + part * 8, 8)
            gap_x = x_ref[at, :] - near_x
            gap_y = y_ref[at, :] - near_y
            gap_z = z_ref[at, :] - near_z
            square = jnp.maximum(gap_x * gap_x + gap_y * gap_y + gap_z * gap_z, TINY)
            ratio = square * lax.rsqrt(square) * inv_ref[at, :]
            outer = 1.0 - jnp.minimum(ratio, 1.0)
            inner = 1.0 - jnp.minimum(ratio + ratio, 1.0)
            weight = (outer + outer) * (outer * outer) - inner * (inner * inner)
            sum_ref[at, :] = sum_ref[at, :] + weight * mass

    run_jobs(jobs_ref, job_step)

    def end_step(row, carry):
        own = near_ref[pl.ds(1664 + row * 8, 8), :]
        inverse = own[7:8]
        total = row_sums(sum_ref[pl.ds(row * 128, 128), :])
        cell = active_ref[row] - first
        fresh = jnp.where(
            lane < counts_ref[cell], total * (NORM * inverse * inverse * inverse), old_ref[pl.ds(cell, 1), :]
        )
        fresh_ref[row] = fresh
        table_ref[pl.ds(cell, 1), :] = GAS * energy_ref[pl.ds(cell, 1), :] / fresh
        return carry

    lax.fori_loop(0, 16, end_step, 0)

    def collect(entry, carry):
        for block in HOME:
            mine_ref[block * 48 + entry] = table_ref[pl.ds(req_ref[block, entry] - first, 1), :]
        for place, block in WIDE:
            mine_ref[block * 48 + entry] = table_ref[pl.ds(lists_ref[place, block, entry] - first, 1), :]
        return carry

    lax.fori_loop(0, SPAN, collect, 0)
    for number, (place, block) in enumerate(EDGE):
        mine_ref[block * 48 + SPAN] = jnp.zeros((1, 128), jnp.float32)
        edge_ref[number] = table_ref[pl.ds(lists_ref[place, block, SPAN] - first, 1), :]


def pass_kernel(devices, mine_ref, edge_ref, near_ref, send_sem, recv_sem, local_sem):
    me = lax.axis_index("dom")
    greet(me, devices)
    copies = []

    def requester(place):
        return (lax.rem(me + devices - STEPS[place], devices),)

    for number, (place, block) in enumerate(WIDE):
        rows = pl.ds(block * 48, SPAN)
        copies.append(
            pltpu.make_async_remote_copy(
                mine_ref.at[rows], near_ref.at[rows], send_sem.at[number], recv_sem.at[number],
                device_id=requester(place), device_id_type=MESH,
            )
        )
    for number, (place, block) in enumerate(EDGE):
        copies.append(
            pltpu.make_async_remote_copy(
                edge_ref.at[number], near_ref.at[block * 48 + SPAN], send_sem.at[5 + number], recv_sem.at[5 + number],
                device_id=requester(place), device_id_type=MESH,
            )
        )
    for number, block in enumerate(HOME):
        rows = pl.ds(block * 48, SPAN)
        copies.append(pltpu.make_async_copy(mine_ref.at[rows], near_ref.at[rows], local_sem.at[number]))
    for copy in copies:
        copy.start()
    for copy in copies:
        copy.wait()


def slope(ratio):
    low = jnp.minimum(ratio, 1.0)
    high = jnp.minimum(ratio + ratio, 1.0)
    return (high - low) * (2.0 - (low + high))


def force_kernel(
    counts_ref, active_ref, offs_ref, jobs_ref, all_ref, press_ref, pack_ref, index_ref, fresh_ref,
    hydro_ref, near_ref, turned_ref, chunk_ref, x_ref, y_ref, z_ref, vx_ref, vy_ref, vz_ref, inv_ref, own_ref,
    ax_ref, ay_ref, az_ref, rate_ref, own_sem,
):
    cells = counts_ref.shape[0]
    first = lax.axis_index("dom") * cells
    lane = lax.broadcasted_iota(jnp.int32, (1, 128), 1)

    own_copy = pltpu.make_async_copy(all_ref.at[pl.ds(1664, 128)], near_ref, own_sem)
    own_copy.start()

    def turn_step(slot, carry):
        at = pl.ds(slot * 16, 16)
        turned_ref[at, :] = pick(press_ref[at, :], index_ref[at, :])
        return carry

    lax.fori_loop(0, 27, turn_step, 0, unroll=9)
    own_copy.wait()

    def own_step(row, carry):
        own = near_ref[pl.ds(row * 8, 8), :]
        at = pl.ds(row * 128, 128)
        inverse = own[7:8]
        inv_sq = inverse * inverse
        for ref, value in (
            (x_ref, own[1:2]), (y_ref, own[2:3]), (z_ref, own[3:4]),
            (vx_ref, own[4:5]), (vy_ref, own[5:6]), (vz_ref, own[6:7]),
            (inv_ref, inverse), (own_ref, (6.0 * NORM) * (inv_sq * inv_sq) * press_ref[pl.ds(208 + row, 1), :]),
        ):
            ref[at, :] = column(value)
        for ref in (ax_ref, ay_ref, az_ref, rate_ref):
            ref[at, :] = jnp.zeros((128, 128), jnp.float32)

        def get(slot):
            return turned_ref[pl.ds(slot * 16 + row, 1), :]

        def put(chunk, value):
            chunk_ref[pl.ds(row * 32 + chunk, 1), :] = value

        held = pack_rows(offs_ref, row, get, put, 1)
        put(offs_ref[27, row] // 128, held)
        put(31, held)
        return carry

    lax.fori_loop(0, 16, own_step, 0)

    def job_step(job, parts):
        place = jobs_ref[job]
        row = place // 32
        tile = pack_ref[place]
        near_inv = tile[7:8]
        near_sq = near_inv * near_inv
        push = (6.0 * NORM) * tile[0:1] * (near_sq * near_sq) * chunk_ref[pl.ds(place, 1), :]
        mass, near_x, near_y, near_z, near_vx, near_vy, near_vz = [
            jnp.broadcast_to(tile[f : f + 1], (8, 128)) for f in range(7)
        ]
        near_inv = jnp.broadcast_to(near_inv, (8, 128))
        push = jnp.broadcast_to(push, (8, 128))
        for part in range(parts):
            at = pl.ds(row * 128 + part * 8, 8)
            gap_x = x_ref[at, :] - near_x
            gap_y = y_ref[at, :] - near_y
            gap_z = z_ref[at, :] - near_z
            square = jnp.maximum(gap_x * gap_x + gap_y * gap_y + gap_z * gap_z, TINY)
            root = lax.rsqrt(square)
            gap = square * root
            pull = slope(gap * inv_ref[at, :]) * root * mass
            both = own_ref[at, :] * pull + slope(gap * near_inv) * push * root
            work = (vx_ref[at, :] - near_vx) * gap_x + (vy_ref[at, :] - near_vy) * gap_y + (vz_ref[at, :] - near_vz) * gap_z
            ax_ref[at, :] = ax_ref[at, :] + both * gap_x
            ay_ref[at, :] = ay_ref[at, :] + both * gap_y
            az_ref[at, :] = az_ref[at, :] + both * gap_z
            rate_ref[at, :] = rate_ref[at, :] + pull * work

    run_jobs(jobs_ref, job_step)

    def end_step(row, carry):
        own = near_ref[pl.ds(row * 8, 8), :]
        inverse = own[7:8]
        inv_sq = inverse * inverse
        factor = (-6.0 * NORM) * (inv_sq * inv_sq) * press_ref[pl.ds(208 + row, 1), :]
        at = pl.ds(row * 128, 128)
        keep = lane < counts_ref[active_ref[row] - first]
        values = [fresh_ref[row]] + [row_sums(ref[at, :]) for ref in (ax_ref, ay_ref, az_ref)]
        values.append(factor * row_sums(rate_ref[at, :]))
        for number, value in enumerate(values):
            hydro_ref[number, pl.ds(row, 1), :] = jnp.where(keep, value, 0.0)
        return carry

    lax.fori_loop(0, 16, end_step, 0)


def specs(kinds):
    return [pl.BlockSpec(memory_space=pltpu.SMEM if kind == "s" else pltpu.VMEM) for kind in kinds]


def floats(*shape):
    return jax.ShapeDtypeStruct(shape, jnp.float32)


def density_call(*args):
    square = pltpu.VMEM((2048, 128), jnp.float32)
    return pl.pallas_call(
        density_kernel,
        out_shape=(
            floats(16, 1, 128), floats(432, 1, 128), floats(9, 1, 128), floats(512, 8, 128),
            jax.ShapeDtypeStruct((432, 128), jnp.int32), jax.ShapeDtypeStruct((32, 128), jnp.int32),
            jax.ShapeDtypeStruct((640,), jnp.int32),
        ),
        in_specs=specs("ssssvvvv"),
        out_specs=tuple(specs("vvvvvvs")),
        scratch_shapes=[
            pltpu.VMEM((1600, 128), jnp.float32), pltpu.VMEM((432, 128), jnp.float32),
            pltpu.SMEM((32, 128), jnp.int32), pltpu.SMEM((32,), jnp.int32),
        ] + [square] * 5 + [pltpu.SemaphoreType.DMA],
        compiler_params=pltpu.CompilerParams(vmem_limit_bytes=LIMIT),
        name="density",
    )(*args)


def force_call(*args):
    square = pltpu.VMEM((2048, 128), jnp.float32)
    return pl.pallas_call(
        force_kernel,
        out_shape=floats(5, 16, 128),
        in_specs=specs("ssss") + [pl.BlockSpec(memory_space=pl.ANY)] + specs("vvvv"),
        out_specs=specs("v")[0],
        scratch_shapes=[
            pltpu.VMEM((128, 128), jnp.float32), pltpu.VMEM((432, 128), jnp.float32),
            pltpu.VMEM((512, 128), jnp.float32),
        ] + [square] * 12 + [pltpu.SemaphoreType.DMA],
        compiler_params=pltpu.CompilerParams(vmem_limit_bytes=LIMIT),
        name="force",
    )(*args)


def shards(positions, velocity, mass, smoothing, energy, density_old, counts, active, neighbours):
    devices = lax.axis_size("dom")
    vmem = pl.BlockSpec(memory_space=pltpu.VMEM)
    smem = pl.BlockSpec(memory_space=pltpu.SMEM)
    pos = jnp.transpose(positions, (1, 0, 2))
    vel = jnp.transpose(velocity, (1, 0, 2))
    requests = jnp.pad(neighbours.T.reshape(9, 48), ((0, 7), (0, 80)))
    shifts = jnp.asarray(shift_tiles())
    f32 = jnp.float32

    near, asked = pl.pallas_call(
        lambda *refs: gather_kernel(devices, *refs),
        out_shape=(jax.ShapeDtypeStruct((432, 8, 128), f32), jax.ShapeDtypeStruct((7, 16, 128), jnp.int32)),
        in_specs=[smem, vmem, smem, vmem, vmem, vmem, vmem],
        out_specs=(vmem, vmem),
        scratch_shapes=[
            pltpu.VMEM((432, 8, 128), f32),
            pltpu.VMEM((9, 8, 128), f32),
            pltpu.SMEM((7, 16, 128), jnp.int32),
            pltpu.SemaphoreType.DMA((7,)),
            pltpu.SemaphoreType.DMA((7,)),
            pltpu.SemaphoreType.DMA((14,)),
            pltpu.SemaphoreType.DMA((14,)),
            pltpu.SemaphoreType.DMA((7,)),
        ],
        compiler_params=pltpu.CompilerParams(collective_id=0, has_side_effects=True, vmem_limit_bytes=LIMIT),
    )(requests, requests, counts, pos, vel, mass, smoothing)

    flat = near.reshape(3456, 128)
    fresh, mine, edge, packed, index, offs, jobs = density_call(
        requests, asked, counts, active, flat, shifts, energy, density_old
    )

    press = pl.pallas_call(
        lambda *refs: pass_kernel(devices, *refs),
        out_shape=jax.ShapeDtypeStruct((432, 1, 128), f32),
        in_specs=[vmem, vmem],
        out_specs=vmem,
        scratch_shapes=[
            pltpu.SemaphoreType.DMA((14,)),
            pltpu.SemaphoreType.DMA((14,)),
            pltpu.SemaphoreType.DMA((4,)),
        ],
        compiler_params=pltpu.CompilerParams(collective_id=1, has_side_effects=True, vmem_limit_bytes=LIMIT),
    )(mine, edge)

    hydro = force_call(counts, active, offs, jobs, flat, press.reshape(432, 128), packed, index, fresh)
    return jnp.transpose(hydro, (1, 0, 2))


def solution(mesh):
    placed = (
        P("dom", None, None),
        P("dom", None, None),
        P("dom", None),
        P("dom", None),
        P("dom", None),
        P("dom", None),
        P("dom"),
        P("dom"),
        P("dom", None),
    )
    return jax.shard_map(
        shards, mesh=mesh, in_specs=placed, out_specs=P("dom", None, None), check_vma=False
    )
```

```python
import math

import jax
import jax.numpy as jnp
import numpy as np
from jax import lax
from jax.experimental import pallas as pl
from jax.experimental.pallas import tpu as pltpu
from jax.sharding import PartitionSpec as P

MESH = pl.DeviceIdType.MESH
NORM = 8.0 / math.pi
GAS = 2.0 / 3.0
TINY = 1e-14
LIMIT = 56 * 1024 * 1024

STEPS = (16, 4, 20, 1, 5, 17, 21)
BLOCKS = (0, 1, 3, 4, 2, 5, 6, 7, 8)
WIDE = ((1, 4), (1, 5), (0, 6), (0, 7), (2, 8))
EDGE = ((6, 8), (5, 6), (5, 7), (4, 4), (4, 5), (3, 0), (3, 1), (3, 2), (3, 3))
HOME = (0, 1, 2, 3)
SPAN = 47
NEAR_SLOTS = 12
FAR_SLOTS = 15
OWN = 10
SPARE = 15


def near_slot(place):
    return place + 3 * (place // 6)


def far_slot(place):
    return place + jnp.where(place < 3, 6, 12)


def shift_tiles():
    tiles = np.zeros((27, 8, 128), np.float32)
    for place in range(27):
        slot = 3 * BLOCKS[place // 3] + place % 3
        tiles[place, 1] = slot // 9 - 1
        tiles[place, 2] = slot // 3 % 3 - 1
        tiles[place, 3] = slot % 3 - 1
    return tiles


def greet(me, devices):
    barrier = pltpu.get_barrier_semaphore()
    for steps in STEPS:
        for other in (me + steps, me + devices - steps):
            pl.semaphore_signal(barrier, inc=1, device_id=(lax.rem(other, devices),), device_id_type=MESH)
    pl.semaphore_wait(barrier, 2 * len(STEPS))


def gather_kernel(
    devices, req_ref, req_send, counts_ref, pos_ref, vel_ref, mass_ref, smooth_ref,
    near_ref, asked_ref, x_ref, y_ref, xy_ref, far_edge_ref, edge_ref, lists_ref, ask_out, ask_in, send_sem, recv_sem, local_sem,
):
    me = lax.axis_index("dom")
    cells = mass_ref.shape[0]
    first = me * cells
    lane = lax.broadcasted_iota(jnp.int32, (1, 128), 1)

    def fill(dst, place, cell):
        cell = jnp.clip(cell - first, 0, cells - 1)
        keep = lane < counts_ref[cell]
        dst[place, 0:1, :] = jnp.where(keep, mass_ref[pl.ds(cell, 1), :], 0.0)
        for axis in range(3):
            dst[place, 1 + axis : 2 + axis, :] = pos_ref[axis, pl.ds(cell, 1), :]
            dst[place, 4 + axis : 5 + axis, :] = vel_ref[axis, pl.ds(cell, 1), :]
        dst[place, 7:8, :] = 1.0 / smooth_ref[pl.ds(cell, 1), :]

    greet(me, devices)
    asks = []
    for place, steps in enumerate(STEPS):
        ask = pltpu.make_async_remote_copy(
            req_send, asked_ref.at[place], ask_out.at[place], ask_in.at[place],
            device_id=(lax.rem(me + steps, devices),), device_id_type=MESH,
        )
        ask.start()
        asks.append(ask)

    def home_step(entry, carry):
        for block in HOME:
            fill(near_ref, block * 48 + entry, req_ref[block, entry])
        return carry

    lax.fori_loop(0, SPAN, home_step, 0)
    copies = []

    def hear(place):
        asks[place].wait_recv()
        listed = pltpu.make_async_copy(asked_ref.at[place], lists_ref.at[place], local_sem.at[place])
        listed.start()
        listed.wait()

    def requester(place):
        return (lax.rem(me + devices - STEPS[place], devices),)

    def serve(dst, group):
        def step(entry, carry):
            for number, (place, block) in enumerate(group):
                fill(dst, number * SPAN + entry, lists_ref[place, block, entry])
            return carry

        lax.fori_loop(0, SPAN, step, 0)

    for place in (3, 4, 5, 6):
        hear(place)
    for number, (place, block) in enumerate(EDGE):
        fill(edge_ref, number, lists_ref[place, block, SPAN])
        target = near_ref.at[block * 48 + SPAN] if block < 4 else far_edge_ref.at[block - 4]
        copy = pltpu.make_async_remote_copy(
            edge_ref.at[number], target, send_sem.at[number], recv_sem.at[number],
            device_id=requester(place), device_id_type=MESH,
        )
        copy.start()
        copies.append(copy)
    hear(0)
    serve(x_ref, WIDE[2:4])
    hear(1)
    serve(y_ref, WIDE[0:2])
    hear(2)
    serve(xy_ref, WIDE[4:5])
    for copy in copies:
        copy.wait()
    for ask in asks:
        ask.wait_send()


def rows_of(ref, slot, feature):
    return ref[pl.ds(slot * 128 + feature, 16, stride=8), :]


def pick(values, index):
    return jnp.take_along_axis(values, index, axis=1, mode="promise_in_bounds")


def eye():
    return lax.broadcasted_iota(jnp.int32, (128, 128), 0) == lax.broadcasted_iota(jnp.int32, (128, 128), 1)


def column(row):
    return jnp.broadcast_to(jnp.sum(jnp.where(eye(), row, 0.0), axis=1, keepdims=True), (128, 128))


def row_sums(pairs):
    total = jnp.sum(pairs, axis=1, keepdims=True)
    return jnp.sum(jnp.where(eye(), total, 0.0), axis=0, keepdims=True)


def list_jobs(sources, counts_ref, active_ref, first, order_ref, jobs_ref):
    place = jnp.int32(0)
    ends = []
    for low, high in ((0, 80), (80, 96), (96, 112), (112, 128)):
        for row in range(16):
            own = counts_ref[active_ref[row] - first]
            order_ref[place] = row
            place = place + ((own > low) & (own <= high)).astype(jnp.int32)
        ends.append(place)
    count = jnp.int32(0)
    begin = jnp.int32(0)
    jobs_ref[512] = count
    for number, end in enumerate(ends):
        def one_row(place, count):
            row = order_ref[place]
            for offs_ref, slots, base in sources:
                chunks = (offs_ref[slots, row] + 127) // 128
                code = row * 16 + base
                for chunk in range(6):
                    jobs_ref[count + chunk] = code + chunk

                def one_chunk(chunk, carry):
                    jobs_ref[count + chunk] = code + chunk
                    return carry

                lax.fori_loop(6, chunks, one_chunk, 0)
                count = count + chunks
            return count

        count = lax.fori_loop(begin, end, one_row, count)
        jobs_ref[count] = SPARE
        count = count + count % 2
        jobs_ref[513 + number] = count
        begin = end


def run_jobs(jobs_ref, step):
    for number, parts in enumerate((10, 12, 14, 16)):
        def two(pair, carry):
            step(2 * pair, parts)
            step(2 * pair + 1, parts)
            return carry

        lax.fori_loop(jobs_ref[512 + number] // 2, jobs_ref[513 + number] // 2, two, 0)


def pack_rows(offs_ref, slots, row, get, put, width):
    lane = lax.broadcasted_iota(jnp.int32, (width, 128), 1)

    def slot_step(slot, held):
        begin = offs_ref[slot, row]
        end = offs_ref[slot + 1, row]
        turned = get(slot)
        merged = jnp.where(lane >= begin % 128, turned, held)
        put(begin // 128, merged)
        return jnp.where(jnp.broadcast_to(end // 128 > begin // 128, (width, 128)), turned, merged)

    return lax.fori_loop(0, slots, slot_step, get(0), unroll=slots)


def pack_part(
    slots, slot_of, near_ref, own_ref, own_place, shift_ref, pack_ref, index_ref, offs_out_ref, mask_ref, offs_ref, local_sem,
    meanwhile,
):
    lanes = lax.broadcasted_iota(jnp.int32, (16, 128), 1)
    on_diagonal = lax.broadcasted_iota(jnp.int32, (16, 128), 0) == lanes
    lows, highs = [], []
    for axis in range(3):
        own = rows_of(own_ref, own_place, 1 + axis)
        lows.append(jnp.min(own, axis=1, keepdims=True))
        highs.append(jnp.max(own, axis=1, keepdims=True))
    widest = jnp.min(rows_of(own_ref, own_place, 7), axis=1, keepdims=True)

    def mask_step(place, carry):
        slot = slot_of(place)
        away = jnp.zeros((16, 128), jnp.float32)
        for axis, step in enumerate((slot // 9, slot // 3 % 3, slot % 3)):
            at = rows_of(near_ref, place, 1 + axis) + (step - 1).astype(jnp.float32)
            out = jnp.maximum(jnp.maximum(lows[axis] - at, at - highs[axis]), 0.0)
            away = away + out * out
        reach = jnp.minimum(rows_of(near_ref, place, 7), widest)
        chosen = (rows_of(near_ref, place, 0) > 0.0) & (away * (reach * reach) <= 1.0001)
        mask_ref[pl.ds(place * 16, 16), :] = jnp.where(chosen, 1.0, 0.0)
        return carry

    lax.fori_loop(0, slots, mask_step, 0, unroll=slots)
    high = lax.broadcasted_iota(jnp.int32, (128, 256), 0)
    wide = lax.broadcasted_iota(jnp.int32, (128, 256), 1)
    counter = jnp.where((wide >= 128) | (high <= wide), 1.0, 0.0).astype(jnp.bfloat16)

    def rank_step(place, begin):
        chosen = mask_ref[pl.ds(place * 16, 16), :].astype(jnp.bfloat16)
        ranks = jnp.dot(chosen, counter, preferred_element_type=jnp.float32).astype(jnp.int32)
        order = ranks[:, 0:128]
        wanted = (lanes - begin) & 127
        index = jnp.zeros((16, 128), jnp.int32)
        for step in (64, 32, 16, 8, 4, 2, 1):
            index = index + jnp.where(pick(order, index + (step - 1)) <= wanted, step, 0)
        index_ref[pl.ds(place * 16, 16), :] = index
        offs_out_ref[pl.ds(place, 1), :] = jnp.sum(jnp.where(on_diagonal, begin, 0), axis=0, keepdims=True)
        return begin + ranks[:, 128:256]

    total = lax.fori_loop(0, slots, rank_step, jnp.zeros((16, 128), jnp.int32), unroll=slots)
    for place in range(slots, 16):
        offs_out_ref[place : place + 1, :] = jnp.sum(jnp.where(on_diagonal, total, 0), axis=0, keepdims=True)
    moved = pltpu.make_async_copy(offs_out_ref, offs_ref, local_sem)
    moved.start()
    meanwhile()
    moved.wait()
    deep = lax.broadcasted_iota(jnp.int32, (8, 128), 0)
    wide = lax.broadcasted_iota(jnp.int32, (8, 128), 1)

    def pack_step(row, carry):
        def get(place):
            tile = near_ref[pl.ds((place * 16 + row) * 8, 8), :] + shift_ref[place]
            index = index_ref[pl.ds(place * 16 + row, 1), :]
            return pick(tile, jnp.broadcast_to(index, (8, 128)))

        def put(chunk, tile):
            pack_ref[row * 16 + chunk] = tile

        held = pack_rows(offs_ref, slots, row, get, put, 8)
        total = offs_ref[slots, row]
        put(total // 128, jnp.where((deep == 0) & (wide >= total % 128), 0.0, held))
        put(SPARE, jnp.where(deep == 0, 0.0, held))
        return carry

    lax.fori_loop(0, 16, pack_step, 0)


def own_columns(own_ref, own_place, pairs, sums):
    def own_step(row, carry):
        own = own_ref[pl.ds(own_place * 128 + row * 8, 8), :]
        at = pl.ds(row * 128, 128)
        for ref, feature in pairs:
            ref[at, :] = column(own[feature : feature + 1])
        for ref in sums:
            ref[at, :] = jnp.zeros((128, 128), jnp.float32)
        return carry

    lax.fori_loop(0, 16, own_step, 0)


def sum_weights(jobs_ref, pack_ref, x_ref, y_ref, z_ref, inv_ref, sum_ref):
    def job_step(job, parts):
        code = jobs_ref[job]
        row = code // 16
        tile = pack_ref[code]
        mass, near_x, near_y, near_z = [jnp.broadcast_to(tile[f : f + 1], (8, 128)) for f in range(4)]
        for part in range(parts):
            at = pl.ds(row * 128 + part * 8, 8)
            gap_x = x_ref[at, :] - near_x
            gap_y = y_ref[at, :] - near_y
            gap_z = z_ref[at, :] - near_z
            square = jnp.maximum(gap_x * gap_x + gap_y * gap_y + gap_z * gap_z, TINY)
            ratio = square * lax.rsqrt(square) * inv_ref[at, :]
            outer = 1.0 - jnp.minimum(ratio, 1.0)
            inner = 1.0 - jnp.minimum(ratio + ratio, 1.0)
            weight = (outer + outer) * (outer * outer) - inner * (inner * inner)
            sum_ref[at, :] = sum_ref[at, :] + weight * mass

    run_jobs(jobs_ref, job_step)


def near_kernel(
    counts_ref, active_ref, near_ref, shift_ref,
    part_ref, pack_ref, index_ref, offs_out_ref,
    mask_ref, offs_ref, order_ref, jobs_ref, x_ref, y_ref, z_ref, inv_ref, sum_ref, local_sem,
):
    first = lax.axis_index("dom") * counts_ref.shape[0]

    def meanwhile():
        own_columns(near_ref, OWN, ((x_ref, 1), (y_ref, 2), (z_ref, 3), (inv_ref, 7)), (sum_ref,))

    pack_part(
        NEAR_SLOTS, near_slot, near_ref, near_ref, OWN, shift_ref, pack_ref, index_ref, offs_out_ref, mask_ref, offs_ref,
        local_sem, meanwhile,
    )
    list_jobs(((offs_ref, NEAR_SLOTS, 0),), counts_ref, active_ref, first, order_ref, jobs_ref)
    sum_weights(jobs_ref, pack_ref, x_ref, y_ref, z_ref, inv_ref, sum_ref)

    def end_step(row, carry):
        part_ref[row] = row_sums(sum_ref[pl.ds(row * 128, 128), :])
        return carry

    lax.fori_loop(0, 16, end_step, 0)


def far_kernel(
    req_ref, lists_ref, counts_ref, active_ref, near_offs_ref, near_ref, x_got_ref, y_got_ref, xy_got_ref, far_edge_ref,
    shift_ref, energy_ref, old_ref, part_ref,
    fresh_ref, mine_ref, edge_ref, pack_ref, index_ref, offs_out_ref, all_jobs_ref,
    far_ref, own_ref, table_ref, mask_ref, offs_ref, order_ref, jobs_ref, x_ref, y_ref, z_ref, inv_ref, sum_ref,
    local_sem, load_sem,
):
    cells = old_ref.shape[0]
    first = lax.axis_index("dom") * cells
    lane = lax.broadcasted_iota(jnp.int32, (1, 128), 1)
    loads = [(near_ref.at[pl.ds(OWN * 128, 128)], own_ref)]
    for number, (source, block) in enumerate(((y_got_ref, 0), (y_got_ref, 1), (x_got_ref, 0), (x_got_ref, 1), (xy_got_ref, 0))):
        loads.append((source.at[pl.ds(block * SPAN * 8, SPAN * 8)], far_ref.at[pl.ds(number * 384, SPAN * 8)]))
        loads.append((far_edge_ref.at[pl.ds(number * 8, 8)], far_ref.at[pl.ds(number * 384 + SPAN * 8, 8)]))
    loads = [pltpu.make_async_copy(source, target, load_sem.at[number]) for number, (source, target) in enumerate(loads)]
    for load in loads:
        load.start()
    table_ref[...] = GAS * energy_ref[...] / old_ref[...]
    for load in loads:
        load.wait()

    def meanwhile():
        own_columns(own_ref, 0, ((x_ref, 1), (y_ref, 2), (z_ref, 3), (inv_ref, 7)), (sum_ref,))

    pack_part(
        FAR_SLOTS, far_slot, far_ref, own_ref, 0, shift_ref, pack_ref, index_ref, offs_out_ref, mask_ref, offs_ref,
        local_sem, meanwhile,
    )
    list_jobs(((offs_ref, FAR_SLOTS, 0),), counts_ref, active_ref, first, order_ref, jobs_ref)
    list_jobs(
        ((near_offs_ref, NEAR_SLOTS, 0), (offs_ref, FAR_SLOTS, 256)), counts_ref, active_ref, first, order_ref, all_jobs_ref
    )
    sum_weights(jobs_ref, pack_ref, x_ref, y_ref, z_ref, inv_ref, sum_ref)

    def end_step(row, carry):
        inverse = own_ref[pl.ds(row * 8 + 7, 1), :]
        total = part_ref[row] + row_sums(sum_ref[pl.ds(row * 128, 128), :])
        cell = active_ref[row] - first
        fresh = jnp.where(
            lane < counts_ref[cell], total * (NORM * inverse * inverse * inverse), old_ref[pl.ds(cell, 1), :]
        )
        fresh_ref[row] = fresh
        table_ref[pl.ds(cell, 1), :] = GAS * energy_ref[pl.ds(cell, 1), :] / fresh
        return carry

    lax.fori_loop(0, 16, end_step, 0)

    def collect(entry, carry):
        for block in HOME:
            mine_ref[block * 48 + entry] = table_ref[pl.ds(req_ref[block, entry] - first, 1), :]
        for place, block in WIDE:
            mine_ref[block * 48 + entry] = table_ref[pl.ds(lists_ref[place, block, entry] - first, 1), :]
        return carry

    lax.fori_loop(0, SPAN, collect, 0)
    for number, (place, block) in enumerate(EDGE):
        mine_ref[block * 48 + SPAN] = jnp.zeros((1, 128), jnp.float32)
        edge_ref[number] = table_ref[pl.ds(lists_ref[place, block, SPAN] - first, 1), :]


def pass_kernel(devices, mine_ref, edge_ref, near_ref, send_sem, recv_sem, local_sem):
    me = lax.axis_index("dom")
    greet(me, devices)
    copies = []

    def requester(place):
        return (lax.rem(me + devices - STEPS[place], devices),)

    for number, (place, block) in enumerate(WIDE):
        rows = pl.ds(block * 48, SPAN)
        copies.append(
            pltpu.make_async_remote_copy(
                mine_ref.at[rows], near_ref.at[rows], send_sem.at[number], recv_sem.at[number],
                device_id=requester(place), device_id_type=MESH,
            )
        )
    for number, (place, block) in enumerate(EDGE):
        copies.append(
            pltpu.make_async_remote_copy(
                edge_ref.at[number], near_ref.at[block * 48 + SPAN], send_sem.at[5 + number], recv_sem.at[5 + number],
                device_id=requester(place), device_id_type=MESH,
            )
        )
    for number, block in enumerate(HOME):
        rows = pl.ds(block * 48, SPAN)
        copies.append(pltpu.make_async_copy(mine_ref.at[rows], near_ref.at[rows], local_sem.at[number]))
    for copy in copies:
        copy.start()
    for copy in copies:
        copy.wait()


def slope(ratio):
    low = jnp.minimum(ratio, 1.0)
    high = jnp.minimum(ratio + ratio, 1.0)
    return (high - low) * (2.0 - (low + high))


def force_kernel(
    counts_ref, active_ref, near_offs_ref, far_offs_ref, jobs_ref, all_ref, near_pack_ref, far_pack_ref,
    near_index_ref, far_index_ref, press_ref, fresh_ref,
    hydro_ref, pack_ref, near_ref, turned_ref, chunk_ref, x_ref, y_ref, z_ref, vx_ref, vy_ref, vz_ref, inv_ref, own_ref,
    ax_ref, ay_ref, az_ref, rate_ref, own_sem,
):
    cells = counts_ref.shape[0]
    first = lax.axis_index("dom") * cells
    lane = lax.broadcasted_iota(jnp.int32, (1, 128), 1)
    loads = [
        pltpu.make_async_copy(all_ref.at[pl.ds(OWN * 128, 128)], near_ref, own_sem.at[0]),
        pltpu.make_async_copy(near_pack_ref, pack_ref.at[pl.ds(0, 256)], own_sem.at[1]),
        pltpu.make_async_copy(far_pack_ref, pack_ref.at[pl.ds(256, 256)], own_sem.at[2]),
    ]
    for load in loads:
        load.start()
    for index_ref, slots, begin in ((near_index_ref, NEAR_SLOTS, 0), (far_index_ref, FAR_SLOTS, NEAR_SLOTS)):
        for place in range(slots):
            at = pl.ds((begin + place) * 16, 16)
            turned_ref[at, :] = pick(press_ref[at, :], index_ref[place * 16 : place * 16 + 16, :])
    loads[0].wait()

    def own_step(row, carry):
        own = near_ref[pl.ds(row * 8, 8), :]
        at = pl.ds(row * 128, 128)
        inverse = own[7:8]
        inv_sq = inverse * inverse
        for ref, value in (
            (x_ref, own[1:2]), (y_ref, own[2:3]), (z_ref, own[3:4]),
            (vx_ref, own[4:5]), (vy_ref, own[5:6]), (vz_ref, own[6:7]),
            (inv_ref, inverse), (own_ref, (6.0 * NORM) * (inv_sq * inv_sq) * press_ref[pl.ds(OWN * 16 + row, 1), :]),
        ):
            ref[at, :] = column(value)
        for ref in (ax_ref, ay_ref, az_ref, rate_ref):
            ref[at, :] = jnp.zeros((128, 128), jnp.float32)

        for offs_ref, slots, begin, base in (
            (near_offs_ref, NEAR_SLOTS, 0, 0), (far_offs_ref, FAR_SLOTS, NEAR_SLOTS, 256)
        ):
            def get(place):
                return turned_ref[pl.ds((begin + place) * 16 + row, 1), :]

            def put(chunk, value):
                chunk_ref[pl.ds(base + row * 16 + chunk, 1), :] = value

            held = pack_rows(offs_ref, slots, row, get, put, 1)
            put(offs_ref[slots, row] // 128, held)
            put(SPARE, held)
        return carry

    lax.fori_loop(0, 16, own_step, 0)
    loads[1].wait()
    loads[2].wait()

    def job_step(job, parts):
        place = jobs_ref[job]
        row = place % 256 // 16
        tile = pack_ref[place]
        near_inv = tile[7:8]
        near_sq = near_inv * near_inv
        push = (6.0 * NORM) * tile[0:1] * (near_sq * near_sq) * chunk_ref[pl.ds(place, 1), :]
        mass, near_x, near_y, near_z, near_vx, near_vy, near_vz = [
            jnp.broadcast_to(tile[f : f + 1], (8, 128)) for f in range(7)
        ]
        near_inv = jnp.broadcast_to(near_inv, (8, 128))
        push = jnp.broadcast_to(push, (8, 128))
        for part in range(parts):
            at = pl.ds(row * 128 + part * 8, 8)
            gap_x = x_ref[at, :] - near_x
            gap_y = y_ref[at, :] - near_y
            gap_z = z_ref[at, :] - near_z
            square = jnp.maximum(gap_x * gap_x + gap_y * gap_y + gap_z * gap_z, TINY)
            root = lax.rsqrt(square)
            gap = square * root
            pull = slope(gap * inv_ref[at, :]) * root * mass
            both = own_ref[at, :] * pull + slope(gap * near_inv) * push * root
            work = (vx_ref[at, :] - near_vx) * gap_x + (vy_ref[at, :] - near_vy) * gap_y + (vz_ref[at, :] - near_vz) * gap_z
            ax_ref[at, :] = ax_ref[at, :] + both * gap_x
            ay_ref[at, :] = ay_ref[at, :] + both * gap_y
            az_ref[at, :] = az_ref[at, :] + both * gap_z
            rate_ref[at, :] = rate_ref[at, :] + pull * work

    run_jobs(jobs_ref, job_step)

    def end_step(row, carry):
        own = near_ref[pl.ds(row * 8, 8), :]
        inverse = own[7:8]
        inv_sq = inverse * inverse
        factor = (-6.0 * NORM) * (inv_sq * inv_sq) * press_ref[pl.ds(OWN * 16 + row, 1), :]
        at = pl.ds(row * 128, 128)
        keep = lane < counts_ref[active_ref[row] - first]
        values = [fresh_ref[row]] + [row_sums(ref[at, :]) for ref in (ax_ref, ay_ref, az_ref)]
        values.append(factor * row_sums(rate_ref[at, :]))
        for number, value in enumerate(values):
            hydro_ref[number, pl.ds(row, 1), :] = jnp.where(keep, value, 0.0)
        return carry

    lax.fori_loop(0, 16, end_step, 0)


def specs(kinds):
    return [pl.BlockSpec(memory_space=pltpu.SMEM if kind == "s" else pltpu.VMEM) for kind in kinds]


def floats(*shape):
    return jax.ShapeDtypeStruct(shape, jnp.float32)


def ints(*shape):
    return jax.ShapeDtypeStruct(shape, jnp.int32)


SQUARE = pltpu.VMEM((2048, 128), jnp.float32)


def near_call(*args):
    return pl.pallas_call(
        near_kernel,
        out_shape=(floats(16, 1, 128), floats(256, 8, 128), ints(192, 128), ints(16, 128)),
        in_specs=specs("ssvv"),
        out_specs=tuple(specs("vvvv")),
        scratch_shapes=[
            pltpu.VMEM((192, 128), jnp.float32), pltpu.SMEM((16, 128), jnp.int32),
            pltpu.SMEM((32,), jnp.int32), pltpu.SMEM((640,), jnp.int32),
        ] + [SQUARE] * 5 + [pltpu.SemaphoreType.DMA],
        compiler_params=pltpu.CompilerParams(vmem_limit_bytes=LIMIT),
        cost_estimate=pl.CostEstimate(flops=100_000_000, bytes_accessed=45_000_000, transcendentals=0),
        name="near_density",
    )(*args)


def far_call(*args):
    return pl.pallas_call(
        far_kernel,
        out_shape=(
            floats(16, 1, 128), floats(432, 1, 128), floats(9, 1, 128), floats(256, 8, 128),
            ints(240, 128), ints(16, 128), ints(640),
        ),
        in_specs=specs("sssss") + [pl.BlockSpec(memory_space=pl.ANY)] * 5 + specs("vvvv"),
        out_specs=tuple(specs("vvvvvvs")),
        scratch_shapes=[
            pltpu.VMEM((1920, 128), jnp.float32), pltpu.VMEM((128, 128), jnp.float32),
            pltpu.VMEM((1600, 128), jnp.float32), pltpu.VMEM((240, 128), jnp.float32),
            pltpu.SMEM((16, 128), jnp.int32), pltpu.SMEM((32,), jnp.int32), pltpu.SMEM((640,), jnp.int32),
        ] + [SQUARE] * 5 + [pltpu.SemaphoreType.DMA, pltpu.SemaphoreType.DMA((11,))],
        compiler_params=pltpu.CompilerParams(vmem_limit_bytes=LIMIT),
        name="far_density",
    )(*args)


def force_call(*args):
    return pl.pallas_call(
        force_kernel,
        out_shape=floats(5, 16, 128),
        in_specs=specs("sssss") + [pl.BlockSpec(memory_space=pl.ANY)] * 3 + specs("vvvv"),
        out_specs=specs("v")[0],
        scratch_shapes=[
            pltpu.VMEM((512, 8, 128), jnp.float32), pltpu.VMEM((128, 128), jnp.float32),
            pltpu.VMEM((432, 128), jnp.float32), pltpu.VMEM((512, 128), jnp.float32),
        ] + [SQUARE] * 12 + [pltpu.SemaphoreType.DMA((3,))],
        compiler_params=pltpu.CompilerParams(vmem_limit_bytes=LIMIT),
        name="force",
    )(*args)


def shards(positions, velocity, mass, smoothing, energy, density_old, counts, active, neighbours):
    devices = lax.axis_size("dom")
    vmem = pl.BlockSpec(memory_space=pltpu.VMEM)
    smem = pl.BlockSpec(memory_space=pltpu.SMEM)
    pos = jnp.transpose(positions, (1, 0, 2))
    vel = jnp.transpose(velocity, (1, 0, 2))
    blocks = neighbours.T.reshape(9, 48)
    requests = jnp.pad(
        jnp.concatenate([blocks[0:2], blocks[3:5], blocks[2:3], blocks[5:9]], axis=0), ((0, 7), (0, 80))
    )
    shifts = shift_tiles()
    f32 = jnp.float32

    near, asked, for_x, for_y, for_xy, far_edge = pl.pallas_call(
        lambda *refs: gather_kernel(devices, *refs),
        out_shape=(
            floats(192, 8, 128), ints(7, 16, 128), floats(94, 8, 128), floats(94, 8, 128), floats(47, 8, 128), floats(5, 8, 128)
        ),
        in_specs=[smem, vmem, smem, vmem, vmem, vmem, vmem],
        out_specs=(vmem,) * 6,
        scratch_shapes=[
            pltpu.VMEM((9, 8, 128), f32),
            pltpu.SMEM((7, 16, 128), jnp.int32),
            pltpu.SemaphoreType.DMA((7,)),
            pltpu.SemaphoreType.DMA((7,)),
            pltpu.SemaphoreType.DMA((9,)),
            pltpu.SemaphoreType.DMA((9,)),
            pltpu.SemaphoreType.DMA((7,)),
        ],
        compiler_params=pltpu.CompilerParams(collective_id=0, has_side_effects=True, vmem_limit_bytes=LIMIT),
        name="gather",
    )(requests, requests, counts, pos, vel, mass, smoothing)

    def fetched(value, steps):
        pairs = [(source, (source - steps) % devices) for source in range(devices)]
        return lax.ppermute(value, "dom", pairs).reshape(-1, 128)

    x_got, y_got, xy_got = fetched(for_x, 16), fetched(for_y, 4), fetched(for_xy, 20)
    flat = near.reshape(1536, 128)
    part, near_pack, near_index, near_offs = near_call(counts, active, flat, jnp.asarray(shifts[:12]))
    fresh, mine, edge, far_pack, far_index, far_offs, jobs = far_call(
        requests, asked, counts, active, near_offs, flat, x_got, y_got, xy_got, far_edge.reshape(40, 128),
        jnp.asarray(shifts[12:]), energy, density_old, part,
    )

    press = pl.pallas_call(
        lambda *refs: pass_kernel(devices, *refs),
        out_shape=jax.ShapeDtypeStruct((432, 1, 128), f32),
        in_specs=[vmem, vmem],
        out_specs=vmem,
        scratch_shapes=[
            pltpu.SemaphoreType.DMA((14,)),
            pltpu.SemaphoreType.DMA((14,)),
            pltpu.SemaphoreType.DMA((4,)),
        ],
        compiler_params=pltpu.CompilerParams(collective_id=1, has_side_effects=True, vmem_limit_bytes=LIMIT),
        name="exchange",
    )(mine, edge)

    hydro = force_call(
        counts, active, near_offs, far_offs, jobs, flat, near_pack, far_pack, near_index, far_index,
        press.reshape(432, 128), fresh,
    )
    return jnp.transpose(hydro, (1, 0, 2))


def solution(mesh):
    placed = (
        P("dom", None, None),
        P("dom", None, None),
        P("dom", None),
        P("dom", None),
        P("dom", None),
        P("dom", None),
        P("dom"),
        P("dom"),
        P("dom", None),
    )
    return jax.shard_map(
        shards, mesh=mesh, in_specs=placed, out_specs=P("dom", None, None), check_vma=False
    )
```

```python
import math

import jax
import jax.numpy as jnp
import numpy as np
from jax import lax
from jax.experimental import pallas as pl
from jax.experimental.pallas import tpu as pltpu
from jax.sharding import PartitionSpec as P

MESH = pl.DeviceIdType.MESH
NORM = 8.0 / math.pi
GAS = 2.0 / 3.0
TINY = 1e-14
LIMIT = 56 * 1024 * 1024

STEPS = (16, 4, 20, 1, 5, 17, 21)
WIDE = ((0, 6), (0, 7), (1, 2), (1, 5), (2, 8))
EDGE = ((6, 8), (5, 6), (5, 7), (4, 2), (4, 5), (3, 0), (3, 1), (3, 3), (3, 4))
HOME = (0, 1, 3, 4)
SPAN = 47
COLUMNS = (1, 2, 3, 7, 4, 5, 6)


def shift_tiles():
    tiles = np.zeros((27, 8, 128), np.float32)
    for slot in range(27):
        tiles[slot, 1] = slot // 9 - 1
        tiles[slot, 2] = slot // 3 % 3 - 1
        tiles[slot, 3] = slot % 3 - 1
    return tiles


def greet(me, devices):
    barrier = pltpu.get_barrier_semaphore()
    for steps in STEPS:
        for other in (me + steps, me + devices - steps):
            pl.semaphore_signal(barrier, inc=1, device_id=(lax.rem(other, devices),), device_id_type=MESH)
    pl.semaphore_wait(barrier, 2 * len(STEPS))


def gather_kernel(
    devices, req_ref, req_send, counts_ref, pos_all, vel_all, mass_all, smooth_all,
    near_ref, asked_ref, columns_ref, pos_ref, vel_ref, mass_ref, smooth_ref, square_ref, send_ref, edge_ref, lists_ref,
    ask_out, ask_in, send_sem, recv_sem, local_sem, table_sem, column_sem,
):
    me = lax.axis_index("dom")
    cells = mass_ref.shape[0]
    tables = [
        pltpu.make_async_copy(source, target, table_sem.at[number])
        for number, (source, target) in enumerate(
            ((pos_all, pos_ref), (vel_all, vel_ref), (mass_all, mass_ref), (smooth_all, smooth_ref))
        )
    ]
    for table in tables:
        table.start()
    first = me * cells
    lane = lax.broadcasted_iota(jnp.int32, (1, 128), 1)

    def fill(dst, place, cell):
        cell = jnp.clip(cell - first, 0, cells - 1)
        keep = lane < counts_ref[cell]
        dst[place, 0:1, :] = jnp.where(keep, mass_ref[pl.ds(cell, 1), :], 0.0)
        for axis in range(3):
            dst[place, 1 + axis : 2 + axis, :] = pos_ref[axis, pl.ds(cell, 1), :]
            dst[place, 4 + axis : 5 + axis, :] = vel_ref[axis, pl.ds(cell, 1), :]
        dst[place, 7:8, :] = 1.0 / smooth_ref[pl.ds(cell, 1), :]

    greet(me, devices)
    asks = []
    for place, steps in enumerate(STEPS):
        ask = pltpu.make_async_remote_copy(
            req_send, asked_ref.at[place], ask_out.at[place], ask_in.at[place],
            device_id=(lax.rem(me + steps, devices),), device_id_type=MESH,
        )
        ask.start()
        asks.append(ask)

    for table in tables:
        table.wait()

    def home_step(entry, carry):
        for block in HOME:
            fill(near_ref, block * 48 + entry, req_ref[block, entry])
        return carry

    lax.fori_loop(0, SPAN, home_step, 0)
    copies = []
    lists = []
    for place, ask in enumerate(asks):
        ask.wait_recv()
        lists.append(pltpu.make_async_copy(asked_ref.at[place], lists_ref.at[place], local_sem.at[place]))
        lists[-1].start()

    def requester(place):
        return (lax.rem(me + devices - STEPS[place], devices),)

    def serve(group, start):
        def step(entry, carry):
            for place, block in group:
                fill(send_ref, block * 48 + entry, lists_ref[place, block, entry])
            return carry

        lax.fori_loop(0, SPAN, step, 0)
        for number, (place, block) in enumerate(group):
            rows = pl.ds(block * 48, SPAN)
            copy = pltpu.make_async_remote_copy(
                send_ref.at[rows], near_ref.at[rows], send_sem.at[start + number], recv_sem.at[start + number],
                device_id=requester(place), device_id_type=MESH,
            )
            copy.start()
            copies.append(copy)

    lists[0].wait()
    serve(WIDE[0:2], 0)
    lists[1].wait()
    serve(WIDE[2:4], 2)
    lists[2].wait()
    serve(WIDE[4:5], 4)
    for place in (3, 4, 5, 6):
        lists[place].wait()
    for number, (place, block) in enumerate(EDGE):
        fill(edge_ref, number, lists_ref[place, block, SPAN])
        copy = pltpu.make_async_remote_copy(
            edge_ref.at[number], near_ref.at[block * 48 + SPAN], send_sem.at[5 + number], recv_sem.at[5 + number],
            device_id=requester(place), device_id_type=MESH,
        )
        copy.start()
        copies.append(copy)

    def own_step(row, carry):
        for number, feature in enumerate(COLUMNS):
            square_ref[number, pl.ds(row * 128, 128), :] = column(near_ref[208 + row, feature : feature + 1, :])
        return carry

    lax.fori_loop(0, 16, own_step, 0)
    stored = pltpu.make_async_copy(square_ref, columns_ref, column_sem)
    stored.start()
    for copy in copies:
        copy.wait()
    for ask in asks:
        ask.wait_send()
    stored.wait()


def rows_of(ref, slot, feature):
    return ref[pl.ds(slot * 128 + feature, 16, stride=8), :]


def pick(values, index):
    return jnp.take_along_axis(values, index, axis=1, mode="promise_in_bounds")


def eye():
    return lax.broadcasted_iota(jnp.int32, (128, 128), 0) == lax.broadcasted_iota(jnp.int32, (128, 128), 1)


def column(row):
    return jnp.broadcast_to(jnp.sum(jnp.where(eye(), row, 0.0), axis=1, keepdims=True), (128, 128))


def row_sums(pairs):
    total = jnp.sum(pairs, axis=1, keepdims=True)
    return jnp.sum(jnp.where(eye(), total, 0.0), axis=0, keepdims=True)


def list_jobs(offs_ref, counts_ref, active_ref, first, order_ref, jobs_ref):
    place = jnp.int32(0)
    ends = []
    for low, high in ((0, 80), (80, 96), (96, 112), (112, 128)):
        for row in range(16):
            own = counts_ref[active_ref[row] - first]
            order_ref[place] = row
            place = place + ((own > low) & (own <= high)).astype(jnp.int32)
        ends.append(place)
    count = jnp.int32(0)
    begin = jnp.int32(0)
    jobs_ref[512] = count
    for number, end in enumerate(ends):
        def one_row(place, count):
            row = order_ref[place]
            chunks = (offs_ref[27, row] + 127) >> 7
            for chunk in range(10):
                jobs_ref[count + chunk] = row * 32 + chunk

            def one_chunk(chunk, carry):
                jobs_ref[count + chunk] = row * 32 + chunk
                return carry

            lax.fori_loop(10, chunks, one_chunk, 0)
            return count + chunks

        count = lax.fori_loop(begin, end, one_row, count)
        jobs_ref[count] = 31
        count = count + (count & 1)
        jobs_ref[513 + number] = count
        begin = end


def run_jobs(jobs_ref, step):
    for number, parts in enumerate((10, 12, 14, 16)):
        def two(pair, carry):
            step(2 * pair, parts)
            step(2 * pair + 1, parts)
            return carry

        lax.fori_loop(jobs_ref[512 + number] >> 1, jobs_ref[513 + number] >> 1, two, 0)


def pack_rows(offs_ref, row, get, put, width):
    lane = lax.broadcasted_iota(jnp.int32, (width, 128), 1)

    def slot_step(slot, held):
        begin = offs_ref[slot, row]
        end = offs_ref[slot + 1, row]
        turned = get(slot)
        merged = jnp.where(lane >= (begin & 127), turned, held)
        put(begin >> 7, merged)
        return jnp.where(jnp.broadcast_to((end >> 7) > (begin >> 7), (width, 128)), turned, merged)

    return lax.fori_loop(0, 27, slot_step, get(0), unroll=27)


def density_kernel(
    req_ref, lists_ref, counts_ref, active_ref, near_ref, columns_ref, shift_ref, energy_ref, old_ref,
    fresh_ref, mine_ref, edge_ref, pack_ref, index_ref, offs_out_ref, jobs_ref,
    table_ref, mask_ref, offs_ref, order_ref, x_ref, y_ref, z_ref, inv_ref, sum_ref, local_sem, column_sem,
):
    cells = old_ref.shape[0]
    first = lax.axis_index("dom") * cells
    lane = lax.broadcasted_iota(jnp.int32, (1, 128), 1)
    lanes = lax.broadcasted_iota(jnp.int32, (16, 128), 1)
    on_diagonal = lax.broadcasted_iota(jnp.int32, (16, 128), 0) == lanes
    loads = [
        pltpu.make_async_copy(columns_ref.at[number], ref, column_sem.at[number])
        for number, ref in enumerate((x_ref, y_ref, z_ref, inv_ref))
    ]
    for load in loads:
        load.start()

    lows, highs = [], []
    for axis in range(3):
        own = rows_of(near_ref, 13, 1 + axis)
        lows.append(jnp.min(own, axis=1, keepdims=True))
        highs.append(jnp.max(own, axis=1, keepdims=True))
    widest = jnp.min(rows_of(near_ref, 13, 7), axis=1, keepdims=True)

    def mask_step(slot, carry):
        away = jnp.zeros((16, 128), jnp.float32)
        for axis, step in enumerate((slot // 9, slot // 3 % 3, slot % 3)):
            at = rows_of(near_ref, slot, 1 + axis) + (step - 1).astype(jnp.float32)
            out = jnp.maximum(jnp.maximum(lows[axis] - at, at - highs[axis]), 0.0)
            away = away + out * out
        reach = jnp.minimum(rows_of(near_ref, slot, 7), widest)
        chosen = (rows_of(near_ref, slot, 0) > 0.0) & (away * (reach * reach) <= 1.0001)
        mask_ref[pl.ds(slot * 16, 16), :] = jnp.where(chosen, 1.0, 0.0)
        return carry

    lax.fori_loop(0, 27, mask_step, 0, unroll=27)
    high = lax.broadcasted_iota(jnp.int32, (128, 256), 0)
    wide = lax.broadcasted_iota(jnp.int32, (128, 256), 1)
    counter = jnp.where((wide >= 128) | (high <= wide), 1.0, 0.0).astype(jnp.bfloat16)

    def rank_step(slot, begin):
        chosen = mask_ref[pl.ds(slot * 16, 16), :].astype(jnp.bfloat16)
        ranks = jnp.dot(chosen, counter, preferred_element_type=jnp.float32).astype(jnp.int32)
        order = ranks[:, 0:128]
        wanted = (lanes - begin) & 127
        index = jnp.zeros((16, 128), jnp.int32)
        for step in (64, 32, 16, 8, 4, 2, 1):
            index = index + jnp.where(pick(order, index + (step - 1)) <= wanted, step, 0)
        index_ref[pl.ds(slot * 16, 16), :] = index
        offs_out_ref[pl.ds(slot, 1), :] = jnp.sum(jnp.where(on_diagonal, begin, 0), axis=0, keepdims=True)
        return begin + ranks[:, 128:256]

    total = lax.fori_loop(0, 27, rank_step, jnp.zeros((16, 128), jnp.int32), unroll=27)
    offs_out_ref[27:28, :] = jnp.sum(jnp.where(on_diagonal, total, 0), axis=0, keepdims=True)
    offs_out_ref[28:32, :] = jnp.zeros((4, 128), jnp.int32)
    moved = pltpu.make_async_copy(offs_out_ref, offs_ref, local_sem)
    moved.start()
    table_ref[...] = GAS * energy_ref[...] / old_ref[...]

    def own_step(row, carry):
        sum_ref[pl.ds(row * 128, 128), :] = jnp.zeros((128, 128), jnp.float32)
        return carry

    lax.fori_loop(0, 16, own_step, 0)
    moved.wait()

    def pack_step(row, carry):
        def get(slot):
            tile = near_ref[pl.ds((slot * 16 + row) * 8, 8), :] + shift_ref[slot]
            index = index_ref[pl.ds(slot * 16 + row, 1), :]
            return pick(tile, jnp.broadcast_to(index, (8, 128)))

        def put(chunk, tile):
            pack_ref[row * 32 + chunk] = tile

        held = pack_rows(offs_ref, row, get, put, 8)
        total = offs_ref[27, row]
        wide = lax.broadcasted_iota(jnp.int32, (8, 128), 1)
        deep = lax.broadcasted_iota(jnp.int32, (8, 128), 0)
        put(total >> 7, jnp.where((deep == 0) & (wide >= (total & 127)), 0.0, held))
        put(31, jnp.where(deep == 0, 0.0, held))
        return carry

    lax.fori_loop(0, 16, pack_step, 0)
    list_jobs(offs_ref, counts_ref, active_ref, first, order_ref, jobs_ref)
    for load in loads:
        load.wait()

    def job_step(job, parts):
        code = jobs_ref[job]
        row = code >> 5
        tile = pack_ref[code]
        mass, near_x, near_y, near_z = [jnp.broadcast_to(tile[f : f + 1], (8, 128)) for f in range(4)]
        for part in range(parts):
            at = pl.ds(row * 128 + part * 8, 8)
            gap_x = x_ref[at, :] - near_x
            gap_y = y_ref[at, :] - near_y
            gap_z = z_ref[at, :] - near_z
            square = jnp.maximum(gap_x * gap_x + gap_y * gap_y + gap_z * gap_z, TINY)
            ratio = square * lax.rsqrt(square) * inv_ref[at, :]
            outer = jnp.maximum(1.0 - ratio, 0.0)
            inner = jnp.maximum(outer - ratio, 0.0)
            weight = (outer + outer) * (outer * outer) - inner * (inner * inner)
            sum_ref[at, :] = sum_ref[at, :] + weight * mass

    run_jobs(jobs_ref, job_step)

    def end_step(row, carry):
        own = near_ref[pl.ds(1664 + row * 8, 8), :]
        inverse = own[7:8]
        total = row_sums(sum_ref[pl.ds(row * 128, 128), :])
        cell = active_ref[row] - first
        fresh = jnp.where(
            lane < counts_ref[cell], total * (NORM * inverse * inverse * inverse), old_ref[pl.ds(cell, 1), :]
        )
        fresh_ref[row] = fresh
        table_ref[pl.ds(cell, 1), :] = GAS * energy_ref[pl.ds(cell, 1), :] / fresh
        return carry

    lax.fori_loop(0, 16, end_step, 0)

    def collect(entry, carry):
        for block in HOME:
            mine_ref[block * 48 + entry] = table_ref[pl.ds(req_ref[block, entry] - first, 1), :]
        for place, block in WIDE:
            mine_ref[block * 48 + entry] = table_ref[pl.ds(lists_ref[place, block, entry] - first, 1), :]
        return carry

    lax.fori_loop(0, SPAN, collect, 0)
    for number, (place, block) in enumerate(EDGE):
        mine_ref[block * 48 + SPAN] = jnp.zeros((1, 128), jnp.float32)
        edge_ref[number] = table_ref[pl.ds(lists_ref[place, block, SPAN] - first, 1), :]


def pass_kernel(devices, mine_ref, edge_ref, near_ref, send_sem, recv_sem, local_sem):
    me = lax.axis_index("dom")
    greet(me, devices)
    copies = []

    def requester(place):
        return (lax.rem(me + devices - STEPS[place], devices),)

    for number, (place, block) in enumerate(WIDE):
        rows = pl.ds(block * 48, SPAN)
        copies.append(
            pltpu.make_async_remote_copy(
                mine_ref.at[rows], near_ref.at[rows], send_sem.at[number], recv_sem.at[number],
                device_id=requester(place), device_id_type=MESH,
            )
        )
    for number, (place, block) in enumerate(EDGE):
        copies.append(
            pltpu.make_async_remote_copy(
                edge_ref.at[number], near_ref.at[block * 48 + SPAN], send_sem.at[5 + number], recv_sem.at[5 + number],
                device_id=requester(place), device_id_type=MESH,
            )
        )
    for number, block in enumerate(HOME):
        rows = pl.ds(block * 48, SPAN)
        copies.append(pltpu.make_async_copy(mine_ref.at[rows], near_ref.at[rows], local_sem.at[number]))
    for copy in copies:
        copy.start()
    for copy in copies:
        copy.wait()


def slope(ratio):
    outer = jnp.maximum(1.0 - ratio, 0.0)
    low = jnp.minimum(outer, ratio)
    return low * ((outer + outer) - low)


def force_kernel(
    counts_ref, active_ref, offs_ref, jobs_ref, all_ref, columns_ref, press_ref, pack_ref, index_ref, fresh_ref,
    hydro_ref, near_ref, turned_ref, chunk_ref, x_ref, y_ref, z_ref, vx_ref, vy_ref, vz_ref, inv_ref, own_ref,
    ax_ref, ay_ref, az_ref, rate_ref, own_sem, column_sem,
):
    cells = counts_ref.shape[0]
    first = lax.axis_index("dom") * cells
    lane = lax.broadcasted_iota(jnp.int32, (1, 128), 1)

    own_copy = pltpu.make_async_copy(all_ref.at[pl.ds(1664, 128)], near_ref, own_sem)
    own_copy.start()
    loads = [
        pltpu.make_async_copy(columns_ref.at[number], ref, column_sem.at[number])
        for number, ref in enumerate((x_ref, y_ref, z_ref, inv_ref, vx_ref, vy_ref, vz_ref))
    ]
    for load in loads:
        load.start()

    def turn_step(slot, carry):
        at = pl.ds(slot * 16, 16)
        turned_ref[at, :] = pick(press_ref[at, :], index_ref[at, :])
        return carry

    lax.fori_loop(0, 27, turn_step, 0, unroll=9)
    own_copy.wait()

    def own_step(row, carry):
        own = near_ref[pl.ds(row * 8, 8), :]
        at = pl.ds(row * 128, 128)
        inverse = own[7:8]
        inv_sq = inverse * inverse
        own_ref[at, :] = column((6.0 * NORM) * (inv_sq * inv_sq) * press_ref[pl.ds(208 + row, 1), :])
        for ref in (ax_ref, ay_ref, az_ref, rate_ref):
            ref[at, :] = jnp.zeros((128, 128), jnp.float32)

        def get(slot):
            return turned_ref[pl.ds(slot * 16 + row, 1), :]

        def put(chunk, value):
            chunk_ref[pl.ds(row * 32 + chunk, 1), :] = value

        held = pack_rows(offs_ref, row, get, put, 1)
        put(offs_ref[27, row] >> 7, held)
        put(31, held)
        return carry

    lax.fori_loop(0, 16, own_step, 0)
    for load in loads:
        load.wait()

    def job_step(job, parts):
        place = jobs_ref[job]
        row = place >> 5
        tile = pack_ref[place]
        near_inv = tile[7:8]
        near_sq = near_inv * near_inv
        push = (6.0 * NORM) * tile[0:1] * (near_sq * near_sq) * chunk_ref[pl.ds(place, 1), :]
        mass, near_x, near_y, near_z, near_vx, near_vy, near_vz = [
            jnp.broadcast_to(tile[f : f + 1], (8, 128)) for f in range(7)
        ]
        near_inv = jnp.broadcast_to(near_inv, (8, 128))
        push = jnp.broadcast_to(push, (8, 128))
        for part in range(parts):
            at = pl.ds(row * 128 + part * 8, 8)
            gap_x = x_ref[at, :] - near_x
            gap_y = y_ref[at, :] - near_y
            gap_z = z_ref[at, :] - near_z
            square = jnp.maximum(gap_x * gap_x + gap_y * gap_y + gap_z * gap_z, TINY)
            root = lax.rsqrt(square)
            gap = square * root
            pull = slope(gap * inv_ref[at, :]) * root * mass
            both = own_ref[at, :] * pull + slope(gap * near_inv) * push * root
            work = (vx_ref[at, :] - near_vx) * gap_x + (vy_ref[at, :] - near_vy) * gap_y + (vz_ref[at, :] - near_vz) * gap_z
            ax_ref[at, :] = ax_ref[at, :] + both * gap_x
            ay_ref[at, :] = ay_ref[at, :] + both * gap_y
            az_ref[at, :] = az_ref[at, :] + both * gap_z
            rate_ref[at, :] = rate_ref[at, :] + pull * work

    run_jobs(jobs_ref, job_step)

    def end_step(row, carry):
        own = near_ref[pl.ds(row * 8, 8), :]
        inverse = own[7:8]
        inv_sq = inverse * inverse
        factor = (-6.0 * NORM) * (inv_sq * inv_sq) * press_ref[pl.ds(208 + row, 1), :]
        at = pl.ds(row * 128, 128)
        keep = lane < counts_ref[active_ref[row] - first]
        values = [fresh_ref[row]] + [row_sums(ref[at, :]) for ref in (ax_ref, ay_ref, az_ref)]
        values.append(factor * row_sums(rate_ref[at, :]))
        for number, value in enumerate(values):
            hydro_ref[number, pl.ds(row, 1), :] = jnp.where(keep, value, 0.0)
        return carry

    lax.fori_loop(0, 16, end_step, 0)


def specs(kinds):
    return [pl.BlockSpec(memory_space=pltpu.SMEM if kind == "s" else pltpu.VMEM) for kind in kinds]


def floats(*shape):
    return jax.ShapeDtypeStruct(shape, jnp.float32)


def density_call(*args):
    square = pltpu.VMEM((2048, 128), jnp.float32)
    return pl.pallas_call(
        density_kernel,
        out_shape=(
            floats(16, 1, 128), floats(432, 1, 128), floats(9, 1, 128), floats(512, 8, 128),
            jax.ShapeDtypeStruct((432, 128), jnp.int32), jax.ShapeDtypeStruct((32, 128), jnp.int32),
            jax.ShapeDtypeStruct((640,), jnp.int32),
        ),
        in_specs=specs("ssssv") + [pl.BlockSpec(memory_space=pl.ANY)] + specs("vvv"),
        out_specs=tuple(specs("vvvvvvs")),
        scratch_shapes=[
            pltpu.VMEM((1600, 128), jnp.float32), pltpu.VMEM((432, 128), jnp.float32),
            pltpu.SMEM((32, 128), jnp.int32), pltpu.SMEM((32,), jnp.int32),
        ] + [square] * 5 + [pltpu.SemaphoreType.DMA, pltpu.SemaphoreType.DMA((4,))],
        compiler_params=pltpu.CompilerParams(vmem_limit_bytes=LIMIT),
        name="density",
    )(*args)


def force_call(*args):
    square = pltpu.VMEM((2048, 128), jnp.float32)
    return pl.pallas_call(
        force_kernel,
        out_shape=floats(5, 16, 128),
        in_specs=specs("ssss") + [pl.BlockSpec(memory_space=pl.ANY)] * 2 + specs("vvvv"),
        out_specs=specs("v")[0],
        scratch_shapes=[
            pltpu.VMEM((128, 128), jnp.float32), pltpu.VMEM((432, 128), jnp.float32),
            pltpu.VMEM((512, 128), jnp.float32),
        ] + [square] * 12 + [pltpu.SemaphoreType.DMA, pltpu.SemaphoreType.DMA((7,))],
        compiler_params=pltpu.CompilerParams(vmem_limit_bytes=LIMIT),
        name="force",
    )(*args)


def shards(positions, velocity, mass, smoothing, energy, density_old, counts, active, neighbours):
    devices = lax.axis_size("dom")
    vmem = pl.BlockSpec(memory_space=pltpu.VMEM)
    smem = pl.BlockSpec(memory_space=pltpu.SMEM)
    pos = jnp.transpose(positions, (1, 0, 2))
    vel = jnp.transpose(velocity, (1, 0, 2))
    requests = jnp.pad(neighbours.T.reshape(9, 48), ((0, 7), (0, 80)))
    shifts = jnp.asarray(shift_tiles())
    f32 = jnp.float32

    anywhere = pl.BlockSpec(memory_space=pl.ANY)
    near, asked, columns = pl.pallas_call(
        lambda *refs: gather_kernel(devices, *refs),
        out_shape=(floats(432, 8, 128), jax.ShapeDtypeStruct((7, 16, 128), jnp.int32), floats(7, 2048, 128)),
        in_specs=[smem, vmem, smem, anywhere, anywhere, anywhere, anywhere],
        out_specs=(vmem, vmem, anywhere),
        scratch_shapes=[
            pltpu.VMEM((3, 1600, 128), f32),
            pltpu.VMEM((3, 1600, 128), f32),
            pltpu.VMEM((1600, 128), f32),
            pltpu.VMEM((1600, 128), f32),
            pltpu.VMEM((7, 2048, 128), f32),
            pltpu.VMEM((432, 8, 128), f32),
            pltpu.VMEM((9, 8, 128), f32),
            pltpu.SMEM((7, 16, 128), jnp.int32),
            pltpu.SemaphoreType.DMA((7,)),
            pltpu.SemaphoreType.DMA((7,)),
            pltpu.SemaphoreType.DMA((14,)),
            pltpu.SemaphoreType.DMA((14,)),
            pltpu.SemaphoreType.DMA((7,)),
            pltpu.SemaphoreType.DMA((4,)),
            pltpu.SemaphoreType.DMA,
        ],
        compiler_params=pltpu.CompilerParams(collective_id=0, has_side_effects=True, vmem_limit_bytes=LIMIT),
    )(requests, requests, counts, pos, vel, mass, smoothing)

    flat = near.reshape(3456, 128)
    fresh, mine, edge, packed, index, offs, jobs = density_call(
        requests, asked, counts, active, flat, columns, shifts, energy, density_old
    )

    press = pl.pallas_call(
        lambda *refs: pass_kernel(devices, *refs),
        out_shape=jax.ShapeDtypeStruct((432, 1, 128), f32),
        in_specs=[vmem, vmem],
        out_specs=vmem,
        scratch_shapes=[
            pltpu.SemaphoreType.DMA((14,)),
            pltpu.SemaphoreType.DMA((14,)),
            pltpu.SemaphoreType.DMA((4,)),
        ],
        compiler_params=pltpu.CompilerParams(collective_id=1, has_side_effects=True, vmem_limit_bytes=LIMIT),
    )(mine, edge)

    hydro = force_call(counts, active, offs, jobs, flat, columns, press.reshape(432, 128), packed, index, fresh)
    return jnp.transpose(hydro, (1, 0, 2))


def solution(mesh):
    placed = (
        P("dom", None, None),
        P("dom", None, None),
        P("dom", None),
        P("dom", None),
        P("dom", None),
        P("dom", None),
        P("dom"),
        P("dom"),
        P("dom", None),
    )
    return jax.shard_map(
        shards, mesh=mesh, in_specs=placed, out_specs=P("dom", None, None), check_vma=False
    )
```

```python
import math

import jax
import jax.numpy as jnp
import numpy as np
from jax import lax
from jax.experimental import pallas as pl
from jax.experimental.pallas import tpu as pltpu
from jax.sharding import PartitionSpec as P

MESH = pl.DeviceIdType.MESH
NORM = 8.0 / math.pi
GAS = 2.0 / 3.0
TINY = 1e-14
LIMIT = 56 * 1024 * 1024

STEPS = (16, 4, 20, 1, 5, 17, 21)
WIDE = ((0, 6), (0, 7), (1, 2), (1, 5), (2, 8))
EDGE = ((6, 8), (5, 6), (5, 7), (4, 2), (4, 5), (3, 0), (3, 1), (3, 3), (3, 4))
HOME = (0, 1, 3, 4)
SPAN = 47
COLUMNS = (1, 2, 3, 7, 4, 5, 6)


def shift_tiles():
    tiles = np.zeros((27, 8, 128), np.float32)
    for slot in range(27):
        tiles[slot, 1] = slot // 9 - 1
        tiles[slot, 2] = slot // 3 % 3 - 1
        tiles[slot, 3] = slot % 3 - 1
    return tiles


def greet(me, devices):
    barrier = pltpu.get_barrier_semaphore()
    for steps in STEPS:
        for other in (me + steps, me + devices - steps):
            pl.semaphore_signal(barrier, inc=1, device_id=(lax.rem(other, devices),), device_id_type=MESH)
    pl.semaphore_wait(barrier, 2 * len(STEPS))


def gather_kernel(
    devices, req_ref, req_send, counts_ref, active_ref, pos_all, vel_all, mass_all, smooth_all, energy_all, old_all,
    near_ref, press_ref, fresh_ref, columns_ref,
    pos_ref, vel_ref, mass_ref, smooth_ref, energy_ref, old_ref, asked_ref, square_ref, sum_ref, table_ref, own_ref,
    send_ref, edge_ref, give_ref, give_edge_ref, lists_ref,
    ask_out, ask_in, send_sem, recv_sem, give_out, give_in, local_sem, table_sem, column_sem,
):
    me = lax.axis_index("dom")
    cells = mass_ref.shape[0]
    tables = [
        pltpu.make_async_copy(source, target, table_sem.at[number])
        for number, (source, target) in enumerate(
            (
                (pos_all, pos_ref), (vel_all, vel_ref), (mass_all, mass_ref), (smooth_all, smooth_ref),
                (energy_all, energy_ref), (old_all, old_ref),
            )
        )
    ]
    for table in tables:
        table.start()
    first = me * cells
    lane = lax.broadcasted_iota(jnp.int32, (1, 128), 1)

    def local(cell):
        return jnp.clip(cell - first, 0, cells - 1)

    def fill(dst, place, cell):
        cell = local(cell)
        keep = lane < counts_ref[cell]
        dst[place, 0:1, :] = jnp.where(keep, mass_ref[pl.ds(cell, 1), :], 0.0)
        for axis in range(3):
            dst[place, 1 + axis : 2 + axis, :] = pos_ref[axis, pl.ds(cell, 1), :]
            dst[place, 4 + axis : 5 + axis, :] = vel_ref[axis, pl.ds(cell, 1), :]
        dst[place, 7:8, :] = 1.0 / smooth_ref[pl.ds(cell, 1), :]

    greet(me, devices)
    asks = []
    for place, steps in enumerate(STEPS):
        ask = pltpu.make_async_remote_copy(
            req_send, asked_ref.at[place], ask_out.at[place], ask_in.at[place],
            device_id=(lax.rem(me + steps, devices),), device_id_type=MESH,
        )
        ask.start()
        asks.append(ask)

    for table in tables:
        table.wait()

    def home_step(entry, carry):
        for block in HOME:
            fill(near_ref, block * 48 + entry, req_ref[block, entry])
        return carry

    lax.fori_loop(0, SPAN, home_step, 0)
    copies = []
    lists = []
    for place, ask in enumerate(asks):
        ask.wait_recv()
        lists.append(pltpu.make_async_copy(asked_ref.at[place], lists_ref.at[place], local_sem.at[place]))
        lists[-1].start()

    def requester(place):
        return (lax.rem(me + devices - STEPS[place], devices),)

    def serve(group, start):
        def step(entry, carry):
            for place, block in group:
                fill(send_ref, block * 48 + entry, lists_ref[place, block, entry])
            return carry

        lax.fori_loop(0, SPAN, step, 0)
        for number, (place, block) in enumerate(group):
            rows = pl.ds(block * 48, SPAN)
            copy = pltpu.make_async_remote_copy(
                send_ref.at[rows], near_ref.at[rows], send_sem.at[start + number], recv_sem.at[start + number],
                device_id=requester(place), device_id_type=MESH,
            )
            copy.start()
            copies.append(copy)

    lists[0].wait()
    serve(WIDE[0:2], 0)
    lists[1].wait()
    serve(WIDE[2:4], 2)
    lists[2].wait()
    serve(WIDE[4:5], 4)
    for place in (3, 4, 5, 6):
        lists[place].wait()
    for number, (place, block) in enumerate(EDGE):
        fill(edge_ref, number, lists_ref[place, block, SPAN])
        copy = pltpu.make_async_remote_copy(
            edge_ref.at[number], near_ref.at[block * 48 + SPAN], send_sem.at[5 + number], recv_sem.at[5 + number],
            device_id=requester(place), device_id_type=MESH,
        )
        copy.start()
        copies.append(copy)

    def own_step(row, carry):
        for number, feature in enumerate(COLUMNS):
            square_ref[number, pl.ds(row * 128, 128), :] = column(near_ref[208 + row, feature : feature + 1, :])
        return carry

    lax.fori_loop(0, 16, own_step, 0)
    stored = pltpu.make_async_copy(square_ref, columns_ref, column_sem)
    stored.start()
    sum_ref[...] = jnp.zeros((2048, 128), jnp.float32)

    def add_tiles(row, tiles):
        near = []
        for index, *shift in tiles:
            tile = near_ref[index]
            near.append([tile[0:1]] + [tile[1 + axis : 2 + axis] + shift[axis] for axis in range(3)])
        for part in range(4):
            at = pl.ds(row * 128 + part * 32, 32)
            own_x, own_y, own_z, own_inv = [square_ref[number, at, :] for number in range(4)]
            total = sum_ref[at, :]
            for mass, near_x, near_y, near_z in near:
                gap_x = own_x - near_x
                gap_y = own_y - near_y
                gap_z = own_z - near_z
                square = jnp.maximum(gap_x * gap_x + gap_y * gap_y + gap_z * gap_z, TINY)
                ratio = square * lax.rsqrt(square) * own_inv
                outer = jnp.maximum(1.0 - ratio, 0.0)
                inner = jnp.maximum(outer - ratio, 0.0)
                total = total + ((outer + outer) * (outer * outer) - inner * (inner * inner)) * mass
            sum_ref[at, :] = total

    def add_blocks(blocks):
        def step(entry, carry):
            high = (entry // 16 - 1).astype(jnp.float32)
            add_tiles(entry % 16, [(block * 48 + entry, block // 3 - 1.0, block % 3 - 1.0, high) for block in blocks])
            return carry

        lax.fori_loop(0, SPAN, step, 0)

    add_blocks(HOME)
    for blocks, numbers in (((6, 7), (0, 1)), ((2, 5), (2, 3)), ((8,), (4,))):
        for number in numbers:
            copies[number].wait_recv()
        add_blocks(blocks)
    for copy in copies[5:]:
        copy.wait_recv()
    for begin in (0, 3, 6):
        add_tiles(15, [(block * 48 + SPAN, block // 3 - 1.0, block % 3 - 1.0, 1.0) for block in range(begin, begin + 3)])

    def fresh_step(row, carry):
        inverse = near_ref[208 + row, 7:8, :]
        cell = local(active_ref[row])
        fresh = jnp.where(
            lane < counts_ref[cell],
            row_sums(sum_ref[pl.ds(row * 128, 128), :]) * (NORM * inverse * inverse * inverse),
            old_ref[pl.ds(cell, 1), :],
        )
        fresh_ref[row] = fresh
        own_ref[row] = GAS * energy_ref[pl.ds(cell, 1), :] / fresh
        return carry

    lax.fori_loop(0, 16, fresh_step, 0)
    deep = lax.broadcasted_iota(jnp.int32, (32, 128), 0)
    own_cells = [local(active_ref[row]) for row in range(16)]

    def table_step(part, carry):
        at = pl.ds(part * 32, 32)
        value = GAS * energy_ref[at, :] / old_ref[at, :]
        for row in range(16):
            value = jnp.where(deep == own_cells[row] - part * 32, own_ref[row], value)
        table_ref[at, :] = value
        return carry

    lax.fori_loop(0, cells // 32, table_step, 0)

    def give_step(entry, carry):
        for place, block in WIDE:
            give_ref[block * 48 + entry] = table_ref[pl.ds(local(lists_ref[place, block, entry]), 1), :]
        return carry

    lax.fori_loop(0, SPAN, give_step, 0)
    gives = []
    for number, (place, block) in enumerate(WIDE):
        rows = pl.ds(block * 48, SPAN)
        gives.append((place, give_ref.at[rows], press_ref.at[rows]))
    for number, (place, block) in enumerate(EDGE):
        give_edge_ref[number] = table_ref[pl.ds(local(lists_ref[place, block, SPAN]), 1), :]
        gives.append((place, give_edge_ref.at[number], press_ref.at[block * 48 + SPAN]))
    gives = [
        pltpu.make_async_remote_copy(
            source, target, give_out.at[number], give_in.at[number], device_id=requester(place), device_id_type=MESH
        )
        for number, (place, source, target) in enumerate(gives)
    ]
    for give in gives:
        give.start()

    def keep_step(entry, carry):
        for block in HOME:
            press_ref[block * 48 + entry] = table_ref[pl.ds(local(req_ref[block, entry]), 1), :]
        return carry

    lax.fori_loop(0, SPAN, keep_step, 0)
    for ask in asks:
        ask.wait_send()
    for copy in copies:
        copy.wait_send()
    stored.wait()
    for give in gives:
        give.wait()


def rows_of(ref, slot, feature):
    return ref[pl.ds(slot * 128 + feature, 16, stride=8), :]


def pick(values, index):
    return jnp.take_along_axis(values, index, axis=1, mode="promise_in_bounds")


def eye():
    return lax.broadcasted_iota(jnp.int32, (128, 128), 0) == lax.broadcasted_iota(jnp.int32, (128, 128), 1)


def column(row):
    return jnp.broadcast_to(jnp.sum(jnp.where(eye(), row, 0.0), axis=1, keepdims=True), (128, 128))


def row_sums(pairs):
    total = jnp.sum(pairs, axis=1, keepdims=True)
    return jnp.sum(jnp.where(eye(), total, 0.0), axis=0, keepdims=True)


def list_jobs(offs_ref, counts_ref, active_ref, first, order_ref, jobs_ref):
    place = jnp.int32(0)
    ends = []
    for low, high in ((0, 80), (80, 96), (96, 112), (112, 128)):
        for row in range(16):
            own = counts_ref[active_ref[row] - first]
            order_ref[place] = row
            place = place + ((own > low) & (own <= high)).astype(jnp.int32)
        ends.append(place)
    count = jnp.int32(0)
    begin = jnp.int32(0)
    jobs_ref[512] = count
    for number, end in enumerate(ends):
        def one_row(place, count):
            row = order_ref[place]
            chunks = (offs_ref[27, row] + 127) >> 7
            for chunk in range(10):
                jobs_ref[count + chunk] = row * 32 + chunk

            def one_chunk(chunk, carry):
                jobs_ref[count + chunk] = row * 32 + chunk
                return carry

            lax.fori_loop(10, chunks, one_chunk, 0)
            return count + chunks

        count = lax.fori_loop(begin, end, one_row, count)
        jobs_ref[count] = 31
        count = count + (count & 1)
        jobs_ref[513 + number] = count
        begin = end


def run_jobs(jobs_ref, step):
    for number, parts in enumerate((10, 12, 14, 16)):
        def two(pair, carry):
            step(2 * pair, parts)
            step(2 * pair + 1, parts)
            return carry

        lax.fori_loop(jobs_ref[512 + number] >> 1, jobs_ref[513 + number] >> 1, two, 0)


def slope(ratio):
    outer = jnp.maximum(1.0 - ratio, 0.0)
    low = jnp.minimum(outer, ratio)
    return low * ((outer + outer) - low)


def force_kernel(
    counts_ref, active_ref, columns_ref, near_ref, press_ref, shift_ref, fresh_ref,
    hydro_ref, pack_ref, chunk_ref, index_ref, mask_ref, offs_out_ref, turned_ref, offs_ref, order_ref, jobs_ref,
    x_ref, y_ref, z_ref, vx_ref, vy_ref, vz_ref, inv_ref, own_ref, ax_ref, ay_ref, az_ref, rate_ref, local_sem, column_sem,
):
    cells = counts_ref.shape[0]
    first = lax.axis_index("dom") * cells
    lane = lax.broadcasted_iota(jnp.int32, (1, 128), 1)
    lanes = lax.broadcasted_iota(jnp.int32, (16, 128), 1)
    on_diagonal = lax.broadcasted_iota(jnp.int32, (16, 128), 0) == lanes
    loads = [
        pltpu.make_async_copy(columns_ref.at[number], ref, column_sem.at[number])
        for number, ref in enumerate((x_ref, y_ref, z_ref, inv_ref, vx_ref, vy_ref, vz_ref))
    ]
    for load in loads:
        load.start()
    lows, highs = [], []
    for axis in range(3):
        own = rows_of(near_ref, 13, 1 + axis)
        lows.append(jnp.min(own, axis=1, keepdims=True))
        highs.append(jnp.max(own, axis=1, keepdims=True))
    widest = jnp.min(rows_of(near_ref, 13, 7), axis=1, keepdims=True)

    for slot in range(27):
        away = jnp.zeros((16, 128), jnp.float32)
        for axis, step in enumerate((slot // 9, slot // 3 % 3, slot % 3)):
            at = rows_of(near_ref, slot, 1 + axis) + (step - 1.0)
            out = jnp.maximum(jnp.maximum(lows[axis] - at, at - highs[axis]), 0.0)
            away = away + out * out
        reach = jnp.minimum(rows_of(near_ref, slot, 7), widest)
        chosen = (rows_of(near_ref, slot, 0) > 0.0) & (away * (reach * reach) <= 1.0001)
        mask_ref[slot * 16 : slot * 16 + 16, :] = jnp.where(chosen, 1.0, 0.0)
    high = lax.broadcasted_iota(jnp.int32, (128, 256), 0)
    wide = lax.broadcasted_iota(jnp.int32, (128, 256), 1)
    counter = jnp.where((wide >= 128) | (high <= wide), 1.0, 0.0).astype(jnp.bfloat16)
    begin = jnp.zeros((16, 128), jnp.int32)
    for slot in range(27):
        at = pl.ds(slot * 16, 16)
        ranks = jnp.dot(mask_ref[at, :].astype(jnp.bfloat16), counter, preferred_element_type=jnp.float32)
        ranks = ranks.astype(jnp.int32)
        order = ranks[:, 0:128]
        wanted = (lanes - begin) & 127
        index = jnp.zeros((16, 128), jnp.int32)
        for step in (64, 32, 16, 8, 4, 2, 1):
            index = index + jnp.where(pick(order, index + (step - 1)) <= wanted, step, 0)
        index_ref[at, :] = index
        turned_ref[at, :] = pick(press_ref[at, :], index)
        offs_out_ref[slot : slot + 1, :] = jnp.sum(jnp.where(on_diagonal, begin, 0), axis=0, keepdims=True)
        begin = begin + ranks[:, 128:256]
    offs_out_ref[27:28, :] = jnp.sum(jnp.where(on_diagonal, begin, 0), axis=0, keepdims=True)
    offs_out_ref[28:32, :] = jnp.zeros((4, 128), jnp.int32)
    moved = pltpu.make_async_copy(offs_out_ref, offs_ref, local_sem)
    moved.start()

    def own_step(row, carry):
        own = near_ref[pl.ds(1664 + row * 8, 8), :]
        at = pl.ds(row * 128, 128)
        inv_sq = own[7:8] * own[7:8]
        own_ref[at, :] = column((6.0 * NORM) * (inv_sq * inv_sq) * press_ref[pl.ds(208 + row, 1), :])
        for ref in (ax_ref, ay_ref, az_ref, rate_ref):
            ref[at, :] = jnp.zeros((128, 128), jnp.float32)
        return carry

    lax.fori_loop(0, 16, own_step, 0)
    moved.wait()
    deep = lax.broadcasted_iota(jnp.int32, (8, 128), 0)
    across = lax.broadcasted_iota(jnp.int32, (8, 128), 1)

    def pack_step(row, carry):
        def put(chunk, tile, value):
            pack_ref[row * 32 + chunk] = tile
            chunk_ref[pl.ds(row * 32 + chunk, 1), :] = value

        def slot_step(slot, held):
            begin = offs_ref[slot, row]
            end = offs_ref[slot + 1, row]
            at = slot * 16 + row
            tile = near_ref[pl.ds(at * 8, 8), :] + shift_ref[slot]
            tile = pick(tile, jnp.broadcast_to(index_ref[pl.ds(at, 1), :], (8, 128)))
            value = turned_ref[pl.ds(at, 1), :]
            start = begin & 127
            merged = jnp.where(across >= start, tile, held[0])
            merged_value = jnp.where(lane >= start, value, held[1])
            put(begin >> 7, merged, merged_value)
            more = (end >> 7) > (begin >> 7)
            return (
                jnp.where(jnp.broadcast_to(more, (8, 128)), tile, merged),
                jnp.where(jnp.broadcast_to(more, (1, 128)), value, merged_value),
            )

        held = (near_ref[pl.ds(row * 8, 8), :], turned_ref[pl.ds(row, 1), :])
        held = lax.fori_loop(0, 27, slot_step, held, unroll=27)
        total = offs_ref[27, row]
        put(total >> 7, jnp.where((deep == 0) & (across >= (total & 127)), 0.0, held[0]), held[1])
        put(31, jnp.where(deep == 0, 0.0, held[0]), held[1])
        return carry

    lax.fori_loop(0, 16, pack_step, 0)
    list_jobs(offs_ref, counts_ref, active_ref, first, order_ref, jobs_ref)
    for load in loads:
        load.wait()

    def job_step(job, parts):
        place = jobs_ref[job]
        row = place >> 5
        tile = pack_ref[place]
        near_inv = tile[7:8]
        near_sq = near_inv * near_inv
        push = (6.0 * NORM) * tile[0:1] * (near_sq * near_sq) * chunk_ref[pl.ds(place, 1), :]
        mass, near_x, near_y, near_z, near_vx, near_vy, near_vz = [
            jnp.broadcast_to(tile[f : f + 1], (8, 128)) for f in range(7)
        ]
        near_inv = jnp.broadcast_to(near_inv, (8, 128))
        push = jnp.broadcast_to(push, (8, 128))
        for part in range(parts):
            at = pl.ds(row * 128 + part * 8, 8)
            gap_x = x_ref[at, :] - near_x
            gap_y = y_ref[at, :] - near_y
            gap_z = z_ref[at, :] - near_z
            square = jnp.maximum(gap_x * gap_x + gap_y * gap_y + gap_z * gap_z, TINY)
            root = lax.rsqrt(square)
            gap = square * root
            pull = slope(gap * inv_ref[at, :]) * root * mass
            both = own_ref[at, :] * pull + slope(gap * near_inv) * push * root
            work = (vx_ref[at, :] - near_vx) * gap_x + (vy_ref[at, :] - near_vy) * gap_y + (vz_ref[at, :] - near_vz) * gap_z
            ax_ref[at, :] = ax_ref[at, :] + both * gap_x
            ay_ref[at, :] = ay_ref[at, :] + both * gap_y
            az_ref[at, :] = az_ref[at, :] + both * gap_z
            rate_ref[at, :] = rate_ref[at, :] + pull * work

    run_jobs(jobs_ref, job_step)

    def end_step(row, carry):
        own = near_ref[pl.ds(1664 + row * 8, 8), :]
        inverse = own[7:8]
        inv_sq = inverse * inverse
        factor = (-6.0 * NORM) * (inv_sq * inv_sq) * press_ref[pl.ds(208 + row, 1), :]
        at = pl.ds(row * 128, 128)
        keep = lane < counts_ref[active_ref[row] - first]
        values = [fresh_ref[row]] + [row_sums(ref[at, :]) for ref in (ax_ref, ay_ref, az_ref)]
        values.append(factor * row_sums(rate_ref[at, :]))
        for number, value in enumerate(values):
            hydro_ref[number, pl.ds(row, 1), :] = jnp.where(keep, value, 0.0)
        return carry

    lax.fori_loop(0, 16, end_step, 0)


def specs(kinds):
    return [pl.BlockSpec(memory_space=pltpu.SMEM if kind == "s" else pltpu.VMEM) for kind in kinds]


def floats(*shape):
    return jax.ShapeDtypeStruct(shape, jnp.float32)


def force_call(*args):
    square = pltpu.VMEM((2048, 128), jnp.float32)
    return pl.pallas_call(
        force_kernel,
        out_shape=floats(5, 16, 128),
        in_specs=specs("ss") + [pl.BlockSpec(memory_space=pl.ANY)] + specs("vvvv"),
        out_specs=specs("v")[0],
        scratch_shapes=[
            pltpu.VMEM((512, 8, 128), jnp.float32), pltpu.VMEM((512, 128), jnp.float32),
            pltpu.VMEM((432, 128), jnp.int32), pltpu.VMEM((432, 128), jnp.float32), pltpu.VMEM((32, 128), jnp.int32),
            pltpu.VMEM((432, 128), jnp.float32), pltpu.SMEM((32, 128), jnp.int32), pltpu.SMEM((32,), jnp.int32),
            pltpu.SMEM((640,), jnp.int32),
        ] + [square] * 12 + [pltpu.SemaphoreType.DMA, pltpu.SemaphoreType.DMA((7,))],
        compiler_params=pltpu.CompilerParams(vmem_limit_bytes=LIMIT),
        name="force",
    )(*args)


def shards(positions, velocity, mass, smoothing, energy, density_old, counts, active, neighbours):
    devices = lax.axis_size("dom")
    vmem = pl.BlockSpec(memory_space=pltpu.VMEM)
    smem = pl.BlockSpec(memory_space=pltpu.SMEM)
    pos = jnp.transpose(positions, (1, 0, 2))
    vel = jnp.transpose(velocity, (1, 0, 2))
    requests = jnp.pad(neighbours.T.reshape(9, 48), ((0, 7), (0, 80)))
    shifts = jnp.asarray(shift_tiles())
    f32 = jnp.float32

    anywhere = pl.BlockSpec(memory_space=pl.ANY)
    near, press, fresh, columns = pl.pallas_call(
        lambda *refs: gather_kernel(devices, *refs),
        out_shape=(floats(432, 8, 128), floats(432, 1, 128), floats(16, 1, 128), floats(7, 2048, 128)),
        in_specs=[smem, vmem, smem, smem] + [anywhere] * 6,
        out_specs=(vmem, vmem, vmem, anywhere),
        scratch_shapes=[
            pltpu.VMEM((3, 1600, 128), f32),
            pltpu.VMEM((3, 1600, 128), f32),
            pltpu.VMEM((1600, 128), f32),
            pltpu.VMEM((1600, 128), f32),
            pltpu.VMEM((1600, 128), f32),
            pltpu.VMEM((1600, 128), f32),
            pltpu.VMEM((7, 16, 128), jnp.int32),
            pltpu.VMEM((7, 2048, 128), f32),
            pltpu.VMEM((2048, 128), f32),
            pltpu.VMEM((1600, 128), f32),
            pltpu.VMEM((16, 1, 128), f32),
            pltpu.VMEM((432, 8, 128), f32),
            pltpu.VMEM((9, 8, 128), f32),
            pltpu.VMEM((432, 1, 128), f32),
            pltpu.VMEM((9, 1, 128), f32),
            pltpu.SMEM((7, 16, 128), jnp.int32),
            pltpu.SemaphoreType.DMA((7,)),
            pltpu.SemaphoreType.DMA((7,)),
            pltpu.SemaphoreType.DMA((14,)),
            pltpu.SemaphoreType.DMA((14,)),
            pltpu.SemaphoreType.DMA((14,)),
            pltpu.SemaphoreType.DMA((14,)),
            pltpu.SemaphoreType.DMA((7,)),
            pltpu.SemaphoreType.DMA((6,)),
            pltpu.SemaphoreType.DMA,
        ],
        compiler_params=pltpu.CompilerParams(collective_id=0, has_side_effects=True, vmem_limit_bytes=LIMIT),
        name="cells",
    )(requests, requests, counts, active, pos, vel, mass, smoothing, energy, density_old)

    hydro = force_call(
        counts, active, columns, near.reshape(3456, 128), press.reshape(432, 128), shifts, fresh
    )
    return jnp.transpose(hydro, (1, 0, 2))


def solution(mesh):
    placed = (
        P("dom", None, None),
        P("dom", None, None),
        P("dom", None),
        P("dom", None),
        P("dom", None),
        P("dom", None),
        P("dom"),
        P("dom"),
        P("dom", None),
    )
    return jax.shard_map(
        shards, mesh=mesh, in_specs=placed, out_specs=P("dom", None, None), check_vma=False
    )
```

```python
import math

import jax
import jax.numpy as jnp
import numpy as np
from jax import lax
from jax.experimental import pallas as pl
from jax.experimental.pallas import tpu as pltpu
from jax.sharding import PartitionSpec as P

MESH = pl.DeviceIdType.MESH
NORM = 8.0 / math.pi
GAS = 2.0 / 3.0
TINY = 1e-14
LIMIT = 56 * 1024 * 1024

STEPS = (16, 4, 20, 1, 5, 17, 21)
WIDE = ((0, 6), (0, 7), (1, 2), (1, 5), (2, 8))
EDGE = ((6, 8), (5, 6), (5, 7), (4, 2), (4, 5), (3, 0), (3, 1), (3, 3), (3, 4))
HOME = (0, 1, 3, 4)
SPAN = 47
COLUMNS = (1, 2, 3, 7, 4, 5, 6)


def shift_tiles():
    tiles = np.zeros((27, 8, 128), np.float32)
    for slot in range(27):
        tiles[slot, 1] = slot // 9 - 1
        tiles[slot, 2] = slot // 3 % 3 - 1
        tiles[slot, 3] = slot % 3 - 1
    return tiles


def greet(me, devices):
    barrier = pltpu.get_barrier_semaphore()
    for steps in STEPS:
        for other in (me + steps, me + devices - steps):
            pl.semaphore_signal(barrier, inc=1, device_id=(lax.rem(other, devices),), device_id_type=MESH)


def gather_kernel(
    devices, req_ref, req_send, counts_ref, active_ref, pos_all, vel_all, mass_all, smooth_all, energy_all, old_all,
    near_ref, press_ref, fresh_ref, columns_ref,
    pos_ref, vel_ref, mass_ref, smooth_ref, energy_ref, old_ref, asked_ref, square_ref, sum_ref, table_ref, own_ref,
    send_ref, edge_ref, give_ref, give_edge_ref, lists_ref,
    ask_out, ask_in, send_sem, recv_sem, give_out, give_in, local_sem, table_sem, column_sem,
):
    me = lax.axis_index("dom")
    cells = mass_ref.shape[0]
    tables = [
        pltpu.make_async_copy(source, target, table_sem.at[number])
        for number, (source, target) in enumerate(
            (
                (pos_all, pos_ref), (vel_all, vel_ref), (mass_all, mass_ref), (smooth_all, smooth_ref),
                (energy_all, energy_ref), (old_all, old_ref),
            )
        )
    ]
    for table in tables:
        table.start()
    first = me * cells
    lane = lax.broadcasted_iota(jnp.int32, (1, 128), 1)

    def local(cell):
        return jnp.clip(cell - first, 0, cells - 1)

    def fill(dst, place, cell):
        cell = local(cell)
        keep = lane < counts_ref[cell]
        dst[place, 0:1, :] = jnp.where(keep, mass_ref[pl.ds(cell, 1), :], 0.0)
        for axis in range(3):
            dst[place, 1 + axis : 2 + axis, :] = pos_ref[axis, pl.ds(cell, 1), :]
            dst[place, 4 + axis : 5 + axis, :] = vel_ref[axis, pl.ds(cell, 1), :]
        dst[place, 7:8, :] = 1.0 / smooth_ref[pl.ds(cell, 1), :]

    greet(me, devices)
    pl.semaphore_wait(pltpu.get_barrier_semaphore(), 2 * len(STEPS))
    asks = []
    for place, steps in enumerate(STEPS):
        ask = pltpu.make_async_remote_copy(
            req_send, asked_ref.at[place], ask_out.at[place], ask_in.at[place],
            device_id=(lax.rem(me + steps, devices),), device_id_type=MESH,
        )
        ask.start()
        asks.append(ask)

    for table in tables:
        table.wait()

    def home_step(entry, carry):
        for block in HOME:
            fill(near_ref, block * 48 + entry, req_ref[block, entry])
        return carry

    lax.fori_loop(0, SPAN, home_step, 0)

    def own_step(row, carry):
        for number, feature in enumerate(COLUMNS):
            square_ref[number, pl.ds(row * 128, 128), :] = column(near_ref[208 + row, feature : feature + 1, :])
        return carry

    lax.fori_loop(0, 16, own_step, 0)
    stored = pltpu.make_async_copy(square_ref, columns_ref, column_sem)
    stored.start()
    sum_ref[...] = jnp.zeros((2048, 128), jnp.float32)

    def add_tiles(row, tiles):
        near = []
        for index, *shift in tiles:
            tile = near_ref[index]
            near.append([tile[0:1]] + [tile[1 + axis : 2 + axis] + shift[axis] for axis in range(3)])
        for part in range(4):
            at = pl.ds(row * 128 + part * 32, 32)
            own_x, own_y, own_z, own_inv = [square_ref[number, at, :] for number in range(4)]
            total = sum_ref[at, :]
            for mass, near_x, near_y, near_z in near:
                gap_x = own_x - near_x
                gap_y = own_y - near_y
                gap_z = own_z - near_z
                square = jnp.maximum(gap_x * gap_x + gap_y * gap_y + gap_z * gap_z, TINY)
                ratio = square * lax.rsqrt(square) * own_inv
                outer = jnp.maximum(1.0 - ratio, 0.0)
                inner = jnp.maximum(outer - ratio, 0.0)
                total = total + ((outer + outer) * (outer * outer) - inner * (inner * inner)) * mass
            sum_ref[at, :] = total

    def add_blocks(blocks, begin, end):
        def step(entry, carry):
            high = (entry // 16 - 1).astype(jnp.float32)
            add_tiles(entry % 16, [(block * 48 + entry, block // 3 - 1.0, block % 3 - 1.0, high) for block in blocks])
            return carry

        lax.fori_loop(begin, end, step, 0)

    def hear(places):
        lists = []
        for place in places:
            asks[place].wait_recv()
            lists.append(pltpu.make_async_copy(asked_ref.at[place], lists_ref.at[place], local_sem.at[place]))
            lists[-1].start()
        for listed in lists:
            listed.wait()

    def requester(place):
        return (lax.rem(me + devices - STEPS[place], devices),)

    hear((0, 1, 2))
    copies = []
    edges = []

    def serve(third):
        size = 15 if third == 2 else 16

        def serve_step(entry, carry):
            entry = third * 16 + entry
            for place, block in WIDE:
                fill(send_ref, block * 48 + entry, lists_ref[place, block, entry])
            return carry

        lax.fori_loop(0, size, serve_step, 0)
        for place, block in WIDE:
            rows = pl.ds(block * 48 + third * 16, size)
            copy = pltpu.make_async_remote_copy(
                send_ref.at[rows], near_ref.at[rows], send_sem.at[len(copies)], recv_sem.at[len(copies)],
                device_id=requester(place), device_id_type=MESH,
            )
            copy.start()
            copies.append(copy)

    serve(0)
    hear((3, 4, 5, 6))
    for number, (place, block) in enumerate(EDGE):
        fill(edge_ref, number, lists_ref[place, block, SPAN])
        copy = pltpu.make_async_remote_copy(
            edge_ref.at[number], near_ref.at[block * 48 + SPAN], send_sem.at[15 + number], recv_sem.at[15 + number],
            device_id=requester(place), device_id_type=MESH,
        )
        copy.start()
        edges.append(copy)

    serve(1)
    add_blocks(HOME, 0, 16)
    serve(2)
    add_blocks(HOME, 16, 32)
    add_blocks(HOME, 32, SPAN)

    def table_step(part, carry):
        at = pl.ds(part * 32, 32)
        table_ref[at, :] = GAS * energy_ref[at, :] / old_ref[at, :]
        return carry

    lax.fori_loop(0, cells // 32, table_step, 0)
    for third in range(3):
        for copy in copies[5 * third : 5 * third + 5]:
            copy.wait_recv()
        if third == 2:
            for copy in edges:
                copy.wait_recv()
            for begin in (0, 3, 6):
                add_tiles(
                    15, [(block * 48 + SPAN, block // 3 - 1.0, block % 3 - 1.0, 1.0) for block in range(begin, begin + 3)]
                )
        add_blocks((6, 7, 2, 5, 8), third * 16, min(third * 16 + 16, SPAN))

    def fresh_step(row, carry):
        inverse = near_ref[208 + row, 7:8, :]
        cell = local(active_ref[row])
        fresh = jnp.where(
            lane < counts_ref[cell],
            row_sums(sum_ref[pl.ds(row * 128, 128), :]) * (NORM * inverse * inverse * inverse),
            old_ref[pl.ds(cell, 1), :],
        )
        fresh_ref[row] = fresh
        own_ref[row] = GAS * energy_ref[pl.ds(cell, 1), :] / fresh
        return carry

    lax.fori_loop(0, 16, fresh_step, 0, unroll=4)
    deep = lax.broadcasted_iota(jnp.int32, (32, 128), 0)
    own_cells = [local(active_ref[row]) for row in range(16)]

    def patch_step(part, carry):
        at = pl.ds(part * 32, 32)
        value = table_ref[at, :]
        for row in range(16):
            value = jnp.where(deep == own_cells[row] - part * 32, own_ref[row], value)
        table_ref[at, :] = value
        return carry

    lax.fori_loop(0, cells // 32, patch_step, 0)

    def give_step(entry, carry):
        for place, block in WIDE:
            give_ref[block * 48 + entry] = table_ref[pl.ds(local(lists_ref[place, block, entry]), 1), :]
        return carry

    lax.fori_loop(0, SPAN, give_step, 0)
    gives = []
    for number, (place, block) in enumerate(WIDE):
        rows = pl.ds(block * 48, SPAN)
        gives.append((place, give_ref.at[rows], press_ref.at[rows]))
    for number, (place, block) in enumerate(EDGE):
        give_edge_ref[number] = table_ref[pl.ds(local(lists_ref[place, block, SPAN]), 1), :]
        gives.append((place, give_edge_ref.at[number], press_ref.at[block * 48 + SPAN]))
    gives = [
        pltpu.make_async_remote_copy(
            source, target, give_out.at[number], give_in.at[number], device_id=requester(place), device_id_type=MESH
        )
        for number, (place, source, target) in enumerate(gives)
    ]
    for give in gives:
        give.start()

    def keep_step(entry, carry):
        for block in HOME:
            press_ref[block * 48 + entry] = table_ref[pl.ds(local(req_ref[block, entry]), 1), :]
        return carry

    lax.fori_loop(0, SPAN, keep_step, 0)
    for ask in asks:
        ask.wait_send()
    for copy in copies + edges:
        copy.wait_send()
    stored.wait()
    for give in gives:
        give.wait()


def rows_of(ref, slot, feature):
    return ref[pl.ds(slot * 128 + feature, 16, stride=8), :]


def pick(values, index):
    return jnp.take_along_axis(values, index, axis=1, mode="promise_in_bounds")


def eye():
    return lax.broadcasted_iota(jnp.int32, (128, 128), 0) == lax.broadcasted_iota(jnp.int32, (128, 128), 1)


def column(row):
    return jnp.broadcast_to(jnp.sum(jnp.where(eye(), row, 0.0), axis=1, keepdims=True), (128, 128))


def row_sums(pairs):
    total = jnp.sum(pairs, axis=1, keepdims=True)
    return jnp.sum(jnp.where(eye(), total, 0.0), axis=0, keepdims=True)


def list_jobs(offs_ref, counts_ref, active_ref, first, order_ref, jobs_ref):
    place = jnp.int32(0)
    ends = []
    for low, high in ((0, 80), (80, 96), (96, 112), (112, 128)):
        for row in range(16):
            own = counts_ref[active_ref[row] - first]
            order_ref[place] = row
            place = place + ((own > low) & (own <= high)).astype(jnp.int32)
        ends.append(place)
    count = jnp.int32(0)
    begin = jnp.int32(0)
    jobs_ref[512] = count
    for number, end in enumerate(ends):
        def one_row(place, count):
            row = order_ref[place]
            chunks = (offs_ref[27, row] + 127) >> 7
            for chunk in range(10):
                jobs_ref[count + chunk] = row * 32 + chunk

            def one_chunk(chunk, carry):
                jobs_ref[count + chunk] = row * 32 + chunk
                return carry

            lax.fori_loop(10, chunks, one_chunk, 0)
            return count + chunks

        count = lax.fori_loop(begin, end, one_row, count)
        jobs_ref[count] = 31
        count = count + (count & 1)
        jobs_ref[513 + number] = count
        begin = end


def run_jobs(jobs_ref, step):
    for number, parts in enumerate((10, 12, 14, 16)):
        def two(pair, carry):
            step(2 * pair, parts)
            step(2 * pair + 1, parts)
            return carry

        lax.fori_loop(jobs_ref[512 + number] >> 1, jobs_ref[513 + number] >> 1, two, 0)


def slope(ratio):
    outer = jnp.maximum(1.0 - ratio, 0.0)
    low = jnp.minimum(outer, ratio)
    return low * ((outer + outer) - low)


def force_kernel(
    counts_ref, active_ref, columns_ref, near_ref, press_ref, shift_ref, fresh_ref,
    hydro_ref, pack_ref, chunk_ref, index_ref, mask_ref, offs_out_ref, turned_ref, offs_ref, order_ref, jobs_ref,
    x_ref, y_ref, z_ref, vx_ref, vy_ref, vz_ref, inv_ref, own_ref, ax_ref, ay_ref, az_ref, rate_ref, local_sem, column_sem,
):
    cells = counts_ref.shape[0]
    first = lax.axis_index("dom") * cells
    lane = lax.broadcasted_iota(jnp.int32, (1, 128), 1)
    lanes = lax.broadcasted_iota(jnp.int32, (16, 128), 1)
    on_diagonal = lax.broadcasted_iota(jnp.int32, (16, 128), 0) == lanes
    loads = [
        pltpu.make_async_copy(columns_ref.at[number], ref, column_sem.at[number])
        for number, ref in enumerate((x_ref, y_ref, z_ref, inv_ref, vx_ref, vy_ref, vz_ref))
    ]
    for load in loads:
        load.start()
    lows, highs = [], []
    for axis in range(3):
        own = rows_of(near_ref, 13, 1 + axis)
        lows.append(jnp.min(own, axis=1, keepdims=True))
        highs.append(jnp.max(own, axis=1, keepdims=True))
    widest = jnp.min(rows_of(near_ref, 13, 7), axis=1, keepdims=True)

    for slot in range(27):
        away = jnp.zeros((16, 128), jnp.float32)
        for axis, step in enumerate((slot // 9, slot // 3 % 3, slot % 3)):
            at = rows_of(near_ref, slot, 1 + axis) + (step - 1.0)
            out = jnp.maximum(jnp.maximum(lows[axis] - at, at - highs[axis]), 0.0)
            away = away + out * out
        reach = jnp.minimum(rows_of(near_ref, slot, 7), widest)
        chosen = (rows_of(near_ref, slot, 0) > 0.0) & (away * (reach * reach) <= 1.0001)
        mask_ref[slot * 16 : slot * 16 + 16, :] = jnp.where(chosen, 1.0, 0.0)
    high = lax.broadcasted_iota(jnp.int32, (128, 256), 0)
    wide = lax.broadcasted_iota(jnp.int32, (128, 256), 1)
    counter = jnp.where((wide >= 128) | (high <= wide), 1.0, 0.0).astype(jnp.bfloat16)
    begin = jnp.zeros((16, 128), jnp.int32)
    for slot in range(27):
        at = pl.ds(slot * 16, 16)
        ranks = jnp.dot(mask_ref[at, :].astype(jnp.bfloat16), counter, preferred_element_type=jnp.float32)
        ranks = ranks.astype(jnp.int32)
        order = ranks[:, 0:128]
        wanted = (lanes - begin) & 127
        index = jnp.zeros((16, 128), jnp.int32)
        for step in (64, 32, 16, 8, 4, 2, 1):
            index = index + jnp.where(pick(order, index + (step - 1)) <= wanted, step, 0)
        index_ref[at, :] = index
        turned_ref[at, :] = pick(press_ref[at, :], index)
        offs_out_ref[slot : slot + 1, :] = jnp.sum(jnp.where(on_diagonal, begin, 0), axis=0, keepdims=True)
        begin = begin + ranks[:, 128:256]
    offs_out_ref[27:28, :] = jnp.sum(jnp.where(on_diagonal, begin, 0), axis=0, keepdims=True)
    offs_out_ref[28:32, :] = jnp.zeros((4, 128), jnp.int32)
    moved = pltpu.make_async_copy(offs_out_ref, offs_ref, local_sem)
    moved.start()

    def own_step(row, carry):
        own = near_ref[pl.ds(1664 + row * 8, 8), :]
        at = pl.ds(row * 128, 128)
        inv_sq = own[7:8] * own[7:8]
        own_ref[at, :] = column((6.0 * NORM) * (inv_sq * inv_sq) * press_ref[pl.ds(208 + row, 1), :])
        for ref in (ax_ref, ay_ref, az_ref, rate_ref):
            ref[at, :] = jnp.zeros((128, 128), jnp.float32)
        return carry

    lax.fori_loop(0, 16, own_step, 0)
    moved.wait()
    deep = lax.broadcasted_iota(jnp.int32, (8, 128), 0)
    across = lax.broadcasted_iota(jnp.int32, (8, 128), 1)

    def pack_step(row, carry):
        def put(chunk, tile, value):
            pack_ref[row * 32 + chunk] = tile
            chunk_ref[pl.ds(row * 32 + chunk, 1), :] = value

        def slot_step(slot, held):
            begin = offs_ref[slot, row]
            end = offs_ref[slot + 1, row]
            at = slot * 16 + row
            tile = near_ref[pl.ds(at * 8, 8), :] + shift_ref[slot]
            tile = pick(tile, jnp.broadcast_to(index_ref[pl.ds(at, 1), :], (8, 128)))
            value = turned_ref[pl.ds(at, 1), :]
            start = begin & 127
            merged = jnp.where(across >= start, tile, held[0])
            merged_value = jnp.where(lane >= start, value, held[1])
            put(begin >> 7, merged, merged_value)
            more = (end >> 7) > (begin >> 7)
            return (
                jnp.where(jnp.broadcast_to(more, (8, 128)), tile, merged),
                jnp.where(jnp.broadcast_to(more, (1, 128)), value, merged_value),
            )

        held = (near_ref[pl.ds(row * 8, 8), :], turned_ref[pl.ds(row, 1), :])
        held = lax.fori_loop(0, 27, slot_step, held, unroll=27)
        total = offs_ref[27, row]
        put(total >> 7, jnp.where((deep == 0) & (across >= (total & 127)), 0.0, held[0]), held[1])
        put(31, jnp.where(deep == 0, 0.0, held[0]), held[1])
        return carry

    lax.fori_loop(0, 16, pack_step, 0)
    list_jobs(offs_ref, counts_ref, active_ref, first, order_ref, jobs_ref)
    for load in loads:
        load.wait()

    def job_step(job, parts):
        place = jobs_ref[job]
        row = place >> 5
        tile = pack_ref[place]
        near_inv = tile[7:8]
        near_sq = near_inv * near_inv
        push = (6.0 * NORM) * tile[0:1] * (near_sq * near_sq) * chunk_ref[pl.ds(place, 1), :]
        mass, near_x, near_y, near_z, near_vx, near_vy, near_vz = [
            jnp.broadcast_to(tile[f : f + 1], (8, 128)) for f in range(7)
        ]
        near_inv = jnp.broadcast_to(near_inv, (8, 128))
        push = jnp.broadcast_to(push, (8, 128))
        for part in range(parts):
            at = pl.ds(row * 128 + part * 8, 8)
            gap_x = x_ref[at, :] - near_x
            gap_y = y_ref[at, :] - near_y
            gap_z = z_ref[at, :] - near_z
            square = jnp.maximum(gap_x * gap_x + gap_y * gap_y + gap_z * gap_z, TINY)
            root = lax.rsqrt(square)
            gap = square * root
            pull = slope(gap * inv_ref[at, :]) * root * mass
            both = own_ref[at, :] * pull + slope(gap * near_inv) * push * root
            work = (vx_ref[at, :] - near_vx) * gap_x + (vy_ref[at, :] - near_vy) * gap_y + (vz_ref[at, :] - near_vz) * gap_z
            ax_ref[at, :] = ax_ref[at, :] + both * gap_x
            ay_ref[at, :] = ay_ref[at, :] + both * gap_y
            az_ref[at, :] = az_ref[at, :] + both * gap_z
            rate_ref[at, :] = rate_ref[at, :] + pull * work

    run_jobs(jobs_ref, job_step)

    def end_step(row, carry):
        own = near_ref[pl.ds(1664 + row * 8, 8), :]
        inverse = own[7:8]
        inv_sq = inverse * inverse
        factor = (-6.0 * NORM) * (inv_sq * inv_sq) * press_ref[pl.ds(208 + row, 1), :]
        at = pl.ds(row * 128, 128)
        keep = lane < counts_ref[active_ref[row] - first]
        values = [fresh_ref[row]] + [row_sums(ref[at, :]) for ref in (ax_ref, ay_ref, az_ref)]
        values.append(factor * row_sums(rate_ref[at, :]))
        for number, value in enumerate(values):
            hydro_ref[number, pl.ds(row, 1), :] = jnp.where(keep, value, 0.0)
        return carry

    lax.fori_loop(0, 16, end_step, 0)


def specs(kinds):
    return [pl.BlockSpec(memory_space=pltpu.SMEM if kind == "s" else pltpu.VMEM) for kind in kinds]


def floats(*shape):
    return jax.ShapeDtypeStruct(shape, jnp.float32)


def force_call(*args):
    square = pltpu.VMEM((2048, 128), jnp.float32)
    return pl.pallas_call(
        force_kernel,
        out_shape=floats(5, 16, 128),
        in_specs=specs("ss") + [pl.BlockSpec(memory_space=pl.ANY)] + specs("vvvv"),
        out_specs=specs("v")[0],
        scratch_shapes=[
            pltpu.VMEM((512, 8, 128), jnp.float32), pltpu.VMEM((512, 128), jnp.float32),
            pltpu.VMEM((432, 128), jnp.int32), pltpu.VMEM((432, 128), jnp.float32), pltpu.VMEM((32, 128), jnp.int32),
            pltpu.VMEM((432, 128), jnp.float32), pltpu.SMEM((32, 128), jnp.int32), pltpu.SMEM((32,), jnp.int32),
            pltpu.SMEM((640,), jnp.int32),
        ] + [square] * 12 + [pltpu.SemaphoreType.DMA, pltpu.SemaphoreType.DMA((7,))],
        compiler_params=pltpu.CompilerParams(vmem_limit_bytes=LIMIT),
        name="force",
    )(*args)


def shards(positions, velocity, mass, smoothing, energy, density_old, counts, active, neighbours):
    devices = lax.axis_size("dom")
    vmem = pl.BlockSpec(memory_space=pltpu.VMEM)
    smem = pl.BlockSpec(memory_space=pltpu.SMEM)
    pos = jnp.transpose(positions, (1, 0, 2))
    vel = jnp.transpose(velocity, (1, 0, 2))
    requests = jnp.pad(neighbours.T.reshape(9, 48), ((0, 7), (0, 80)))
    shifts = jnp.asarray(shift_tiles())
    f32 = jnp.float32

    anywhere = pl.BlockSpec(memory_space=pl.ANY)
    near, press, fresh, columns = pl.pallas_call(
        lambda *refs: gather_kernel(devices, *refs),
        out_shape=(floats(432, 8, 128), floats(432, 1, 128), floats(16, 1, 128), floats(7, 2048, 128)),
        in_specs=[smem, vmem, smem, smem] + [anywhere] * 6,
        out_specs=(vmem, vmem, vmem, anywhere),
        scratch_shapes=[
            pltpu.VMEM((3, 1600, 128), f32),
            pltpu.VMEM((3, 1600, 128), f32),
            pltpu.VMEM((1600, 128), f32),
            pltpu.VMEM((1600, 128), f32),
            pltpu.VMEM((1600, 128), f32),
            pltpu.VMEM((1600, 128), f32),
            pltpu.VMEM((7, 16, 128), jnp.int32),
            pltpu.VMEM((7, 2048, 128), f32),
            pltpu.VMEM((2048, 128), f32),
            pltpu.VMEM((1600, 128), f32),
            pltpu.VMEM((16, 1, 128), f32),
            pltpu.VMEM((432, 8, 128), f32),
            pltpu.VMEM((9, 8, 128), f32),
            pltpu.VMEM((432, 1, 128), f32),
            pltpu.VMEM((9, 1, 128), f32),
            pltpu.SMEM((7, 16, 128), jnp.int32),
            pltpu.SemaphoreType.DMA((7,)),
            pltpu.SemaphoreType.DMA((7,)),
            pltpu.SemaphoreType.DMA((24,)),
            pltpu.SemaphoreType.DMA((24,)),
            pltpu.SemaphoreType.DMA((14,)),
            pltpu.SemaphoreType.DMA((14,)),
            pltpu.SemaphoreType.DMA((7,)),
            pltpu.SemaphoreType.DMA((6,)),
            pltpu.SemaphoreType.DMA,
        ],
        compiler_params=pltpu.CompilerParams(collective_id=0, has_side_effects=True, vmem_limit_bytes=LIMIT),
        name="cells",
    )(requests, requests, counts, active, pos, vel, mass, smoothing, energy, density_old)

    hydro = force_call(
        counts, active, columns, near.reshape(3456, 128), press.reshape(432, 128), shifts, fresh
    )
    return jnp.transpose(hydro, (1, 0, 2))


def solution(mesh):
    placed = (
        P("dom", None, None),
        P("dom", None, None),
        P("dom", None),
        P("dom", None),
        P("dom", None),
        P("dom", None),
        P("dom"),
        P("dom"),
        P("dom", None),
    )
    return jax.shard_map(
        shards, mesh=mesh, in_specs=placed, out_specs=P("dom", None, None), check_vma=False
    )
```

```python
import math

import jax
import jax.numpy as jnp
import numpy as np
from jax import lax
from jax.experimental import pallas as pl
from jax.experimental.pallas import tpu as pltpu
from jax.sharding import PartitionSpec as P

MESH = pl.DeviceIdType.MESH
NORM = 8.0 / math.pi
GAS = 2.0 / 3.0
TINY = 1e-14
LIMIT = 56 * 1024 * 1024

STEPS = (16, 4, 20, 1, 5, 17, 21)
WIDE = ((0, 6), (0, 7), (1, 2), (1, 5), (2, 8))
EDGE = ((6, 8), (5, 6), (5, 7), (4, 2), (4, 5), (3, 0), (3, 1), (3, 3), (3, 4))
HOME = (0, 1, 3, 4)
SPAN = 47
COLUMNS = (1, 2, 3, 7, 4, 5, 6)


def shift_tiles():
    tiles = np.zeros((27, 8, 128), np.float32)
    for slot in range(27):
        tiles[slot, 1] = slot // 9 - 1
        tiles[slot, 2] = slot // 3 % 3 - 1
        tiles[slot, 3] = slot % 3 - 1
    return tiles


def greet(me, devices):
    barrier = pltpu.get_barrier_semaphore()
    for steps in STEPS:
        for other in (me + steps, me + devices - steps):
            pl.semaphore_signal(barrier, inc=1, device_id=(lax.rem(other, devices),), device_id_type=MESH)


def gather_kernel(
    devices, req_ref, req_send, counts_ref, active_ref, pos_all, vel_all, mass_all, smooth_all, energy_all, old_all,
    near_ref, press_ref, fresh_ref, columns_ref,
    pos_ref, vel_ref, mass_ref, smooth_ref, energy_ref, old_ref, asked_ref, square_ref, sum_ref, table_ref, own_ref,
    send_ref, edge_ref, give_ref, give_edge_ref, lists_ref,
    ask_out, ask_in, send_sem, recv_sem, give_out, give_in, local_sem, table_sem, column_sem,
):
    me = lax.axis_index("dom")
    cells = mass_ref.shape[0]
    tables = [
        pltpu.make_async_copy(source, target, table_sem.at[number])
        for number, (source, target) in enumerate(
            (
                (pos_all, pos_ref), (vel_all, vel_ref), (mass_all, mass_ref), (smooth_all, smooth_ref),
                (energy_all, energy_ref), (old_all, old_ref),
            )
        )
    ]
    for table in tables:
        table.start()
    first = me * cells
    lane = lax.broadcasted_iota(jnp.int32, (1, 128), 1)

    def local(cell):
        return jnp.clip(cell - first, 0, cells - 1)

    def fill(dst, place, cell):
        cell = local(cell)
        keep = lane < counts_ref[cell]
        dst[place, 0:1, :] = jnp.where(keep, mass_ref[pl.ds(cell, 1), :], 0.0)
        for axis in range(3):
            dst[place, 1 + axis : 2 + axis, :] = pos_ref[axis, pl.ds(cell, 1), :]
            dst[place, 4 + axis : 5 + axis, :] = vel_ref[axis, pl.ds(cell, 1), :]
        dst[place, 7:8, :] = 1.0 / smooth_ref[pl.ds(cell, 1), :]

    greet(me, devices)
    pl.semaphore_wait(pltpu.get_barrier_semaphore(), 2 * len(STEPS))
    asks = []
    for place, steps in enumerate(STEPS):
        ask = pltpu.make_async_remote_copy(
            req_send, asked_ref.at[place], ask_out.at[place], ask_in.at[place],
            device_id=(lax.rem(me + steps, devices),), device_id_type=MESH,
        )
        ask.start()
        asks.append(ask)

    for table in tables:
        table.wait()

    def home_step(entry, carry):
        for block in HOME:
            fill(near_ref, block * 48 + entry, req_ref[entry & 15, block * 3 + (entry >> 4)])
        return carry

    lax.fori_loop(0, SPAN, home_step, 0)

    def own_step(row, carry):
        for number, feature in enumerate(COLUMNS):
            square_ref[number, pl.ds(row * 128, 128), :] = column(near_ref[208 + row, feature : feature + 1, :])
        return carry

    lax.fori_loop(0, 16, own_step, 0)
    stored = pltpu.make_async_copy(square_ref, columns_ref, column_sem)
    stored.start()
    sum_ref[...] = jnp.zeros((2048, 128), jnp.float32)

    def add_tiles(row, tiles):
        near = []
        for index, *shift in tiles:
            tile = near_ref[index]
            near.append([tile[0:1]] + [tile[1 + axis : 2 + axis] + shift[axis] for axis in range(3)])
        for part in range(4):
            at = pl.ds(row * 128 + part * 32, 32)
            own_x, own_y, own_z, own_inv = [square_ref[number, at, :] for number in range(4)]
            total = sum_ref[at, :]
            for mass, near_x, near_y, near_z in near:
                gap_x = own_x - near_x
                gap_y = own_y - near_y
                gap_z = own_z - near_z
                square = jnp.maximum(gap_x * gap_x + gap_y * gap_y + gap_z * gap_z, TINY)
                ratio = square * lax.rsqrt(square) * own_inv
                outer = jnp.maximum(1.0 - ratio, 0.0)
                inner = jnp.maximum(outer - ratio, 0.0)
                total = total + ((outer + outer) * (outer * outer) - inner * (inner * inner)) * mass
            sum_ref[at, :] = total

    def add_blocks(blocks, begin, end):
        def step(entry, carry):
            high = (entry // 16 - 1).astype(jnp.float32)
            add_tiles(entry % 16, [(block * 48 + entry, block // 3 - 1.0, block % 3 - 1.0, high) for block in blocks])
            return carry

        lax.fori_loop(begin, end, step, 0)

    def hear(places):
        lists = []
        for place in places:
            asks[place].wait_recv()
            lists.append(pltpu.make_async_copy(asked_ref.at[place], lists_ref.at[place], local_sem.at[place]))
            lists[-1].start()
        for listed in lists:
            listed.wait()

    def requester(place):
        return (lax.rem(me + devices - STEPS[place], devices),)

    hear((0, 1, 2))
    copies = []
    edges = []

    def serve(third):
        size = 15 if third == 2 else 16

        def serve_step(entry, carry):
            for place, block in WIDE:
                fill(send_ref, block * 48 + third * 16 + entry, lists_ref[place, entry, block * 3 + third])
            return carry

        lax.fori_loop(0, size, serve_step, 0)
        for place, block in WIDE:
            rows = pl.ds(block * 48 + third * 16, size)
            copy = pltpu.make_async_remote_copy(
                send_ref.at[rows], near_ref.at[rows], send_sem.at[len(copies)], recv_sem.at[len(copies)],
                device_id=requester(place), device_id_type=MESH,
            )
            copy.start()
            copies.append(copy)

    serve(0)
    hear((3, 4, 5, 6))
    for number, (place, block) in enumerate(EDGE):
        fill(edge_ref, number, lists_ref[place, 15, block * 3 + 2])
        copy = pltpu.make_async_remote_copy(
            edge_ref.at[number], near_ref.at[block * 48 + SPAN], send_sem.at[15 + number], recv_sem.at[15 + number],
            device_id=requester(place), device_id_type=MESH,
        )
        copy.start()
        edges.append(copy)

    serve(1)
    add_blocks(HOME, 0, 16)
    serve(2)
    add_blocks(HOME, 16, 32)
    add_blocks(HOME, 32, SPAN)

    def table_step(part, carry):
        at = pl.ds(part * 32, 32)
        table_ref[at, :] = GAS * energy_ref[at, :] / old_ref[at, :]
        return carry

    lax.fori_loop(0, cells // 32, table_step, 0)
    for third in range(3):
        for copy in copies[5 * third : 5 * third + 5]:
            copy.wait_recv()
        if third == 2:
            for copy in edges:
                copy.wait_recv()
            for begin in (0, 3, 6):
                add_tiles(
                    15, [(block * 48 + SPAN, block // 3 - 1.0, block % 3 - 1.0, 1.0) for block in range(begin, begin + 3)]
                )
        add_blocks((6, 7, 2, 5, 8), third * 16, min(third * 16 + 16, SPAN))

    def fresh_step(row, carry):
        inverse = near_ref[208 + row, 7:8, :]
        cell = local(active_ref[row])
        fresh = jnp.where(
            lane < counts_ref[cell],
            row_sums(sum_ref[pl.ds(row * 128, 128), :]) * (NORM * inverse * inverse * inverse),
            old_ref[pl.ds(cell, 1), :],
        )
        fresh_ref[row] = fresh
        own_ref[row] = GAS * energy_ref[pl.ds(cell, 1), :] / fresh
        return carry

    lax.fori_loop(0, 16, fresh_step, 0, unroll=4)
    deep = lax.broadcasted_iota(jnp.int32, (32, 128), 0)
    own_cells = [local(active_ref[row]) for row in range(16)]

    def patch_step(part, carry):
        at = pl.ds(part * 32, 32)
        value = table_ref[at, :]
        for row in range(16):
            value = jnp.where(deep == own_cells[row] - part * 32, own_ref[row], value)
        table_ref[at, :] = value
        return carry

    lax.fori_loop(0, cells // 32, patch_step, 0)

    def give_step(entry, carry):
        for place, block in WIDE:
            give_ref[block * 48 + entry] = table_ref[pl.ds(local(lists_ref[place, entry & 15, block * 3 + (entry >> 4)]), 1), :]
        return carry

    def send_give(number, place, source, target):
        give = pltpu.make_async_remote_copy(
            source, target, give_out.at[number], give_in.at[number], device_id=requester(place), device_id_type=MESH
        )
        give.start()
        return give

    gives = []
    for number, (place, block) in enumerate(EDGE):
        give_edge_ref[number] = table_ref[pl.ds(local(lists_ref[place, 15, block * 3 + 2]), 1), :]
        gives.append(send_give(number, place, give_edge_ref.at[number], press_ref.at[block * 48 + SPAN]))
    lax.fori_loop(0, SPAN, give_step, 0)
    for number, (place, block) in enumerate(WIDE):
        rows = pl.ds(block * 48, SPAN)
        gives.append(send_give(9 + number, place, give_ref.at[rows], press_ref.at[rows]))

    def keep_step(entry, carry):
        for block in HOME:
            press_ref[block * 48 + entry] = table_ref[pl.ds(local(req_ref[entry & 15, block * 3 + (entry >> 4)]), 1), :]
        return carry

    lax.fori_loop(0, SPAN, keep_step, 0)
    for ask in asks:
        ask.wait_send()
    for copy in copies + edges:
        copy.wait_send()
    stored.wait()
    for give in gives:
        give.wait()


def rows_of(ref, slot, feature):
    return ref[pl.ds(slot * 128 + feature, 16, stride=8), :]


def pick(values, index):
    return jnp.take_along_axis(values, index, axis=1, mode="promise_in_bounds")


def eye():
    return lax.broadcasted_iota(jnp.int32, (128, 128), 0) == lax.broadcasted_iota(jnp.int32, (128, 128), 1)


def column(row):
    return jnp.broadcast_to(jnp.sum(jnp.where(eye(), row, 0.0), axis=1, keepdims=True), (128, 128))


def row_sums(pairs):
    total = jnp.sum(pairs, axis=1, keepdims=True)
    return jnp.sum(jnp.where(eye(), total, 0.0), axis=0, keepdims=True)


def list_jobs(offs_ref, counts_ref, active_ref, first, order_ref, jobs_ref):
    place = jnp.int32(0)
    ends = []
    for low, high in ((0, 80), (80, 96), (96, 112), (112, 128)):
        for row in range(16):
            own = counts_ref[active_ref[row] - first]
            order_ref[place] = row
            place = place + ((own > low) & (own <= high)).astype(jnp.int32)
        ends.append(place)
    count = jnp.int32(0)
    begin = jnp.int32(0)
    jobs_ref[512] = count
    for number, end in enumerate(ends):
        def one_row(place, count):
            row = order_ref[place]
            chunks = (offs_ref[27, row] + 127) >> 7
            for chunk in range(10):
                jobs_ref[count + chunk] = row * 32 + chunk

            def one_chunk(chunk, carry):
                jobs_ref[count + chunk] = row * 32 + chunk
                return carry

            lax.fori_loop(10, chunks, one_chunk, 0)
            return count + chunks

        count = lax.fori_loop(begin, end, one_row, count)
        jobs_ref[count] = 31
        count = count + (count & 1)
        jobs_ref[513 + number] = count
        begin = end


def run_jobs(jobs_ref, step):
    for number, parts in enumerate((10, 12, 14, 16)):
        def two(pair, carry):
            step(2 * pair, parts)
            step(2 * pair + 1, parts)
            return carry

        lax.fori_loop(jobs_ref[512 + number] >> 1, jobs_ref[513 + number] >> 1, two, 0)


def slope(ratio):
    outer = jnp.maximum(1.0 - ratio, 0.0)
    low = jnp.minimum(outer, ratio)
    return low * ((outer + outer) - low)


def force_kernel(
    counts_ref, active_ref, columns_ref, near_ref, press_ref, shift_ref, fresh_ref,
    hydro_ref, pack_ref, chunk_ref, index_ref, mask_ref, offs_out_ref, turned_ref, offs_ref, order_ref, jobs_ref,
    x_ref, y_ref, z_ref, vx_ref, vy_ref, vz_ref, inv_ref, own_ref, ax_ref, ay_ref, az_ref, rate_ref, local_sem, column_sem,
):
    cells = counts_ref.shape[0]
    first = lax.axis_index("dom") * cells
    lane = lax.broadcasted_iota(jnp.int32, (1, 128), 1)
    lanes = lax.broadcasted_iota(jnp.int32, (16, 128), 1)
    on_diagonal = lax.broadcasted_iota(jnp.int32, (16, 128), 0) == lanes
    loads = [
        pltpu.make_async_copy(columns_ref.at[number], ref, column_sem.at[number])
        for number, ref in enumerate((x_ref, y_ref, z_ref, inv_ref, vx_ref, vy_ref, vz_ref))
    ]
    for load in loads:
        load.start()
    lows, highs = [], []
    for axis in range(3):
        own = rows_of(near_ref, 13, 1 + axis)
        lows.append(jnp.min(own, axis=1, keepdims=True))
        highs.append(jnp.max(own, axis=1, keepdims=True))
    widest = jnp.min(rows_of(near_ref, 13, 7), axis=1, keepdims=True)

    for slot in range(27):
        away = jnp.zeros((16, 128), jnp.float32)
        for axis, step in enumerate((slot // 9, slot // 3 % 3, slot % 3)):
            at = rows_of(near_ref, slot, 1 + axis) + (step - 1.0)
            out = jnp.maximum(jnp.maximum(lows[axis] - at, at - highs[axis]), 0.0)
            away = away + out * out
        reach = jnp.minimum(rows_of(near_ref, slot, 7), widest)
        chosen = (rows_of(near_ref, slot, 0) > 0.0) & (away * (reach * reach) <= 1.0001)
        mask_ref[slot * 16 : slot * 16 + 16, :] = jnp.where(chosen, 1.0, 0.0)
    high = lax.broadcasted_iota(jnp.int32, (128, 256), 0)
    wide = lax.broadcasted_iota(jnp.int32, (128, 256), 1)
    counter = jnp.where((wide >= 128) | (high <= wide), 1.0, 0.0).astype(jnp.bfloat16)
    begin = jnp.zeros((16, 128), jnp.int32)
    for slot in range(27):
        at = pl.ds(slot * 16, 16)
        ranks = jnp.dot(mask_ref[at, :].astype(jnp.bfloat16), counter, preferred_element_type=jnp.float32)
        ranks = ranks.astype(jnp.int32)
        order = ranks[:, 0:128]
        wanted = (lanes - begin) & 127
        index = jnp.zeros((16, 128), jnp.int32)
        for step in (64, 32, 16, 8, 4, 2, 1):
            index = index + jnp.where(pick(order, index + (step - 1)) <= wanted, step, 0)
        index_ref[at, :] = index
        turned_ref[at, :] = pick(press_ref[at, :], index)
        offs_out_ref[slot : slot + 1, :] = jnp.sum(jnp.where(on_diagonal, begin, 0), axis=0, keepdims=True)
        begin = begin + ranks[:, 128:256]
    offs_out_ref[27:28, :] = jnp.sum(jnp.where(on_diagonal, begin, 0), axis=0, keepdims=True)
    offs_out_ref[28:32, :] = jnp.zeros((4, 128), jnp.int32)
    moved = pltpu.make_async_copy(offs_out_ref, offs_ref, local_sem)
    moved.start()

    def own_step(row, carry):
        own = near_ref[pl.ds(1664 + row * 8, 8), :]
        at = pl.ds(row * 128, 128)
        inv_sq = own[7:8] * own[7:8]
        own_ref[at, :] = column((6.0 * NORM) * (inv_sq * inv_sq) * press_ref[pl.ds(208 + row, 1), :])
        for ref in (ax_ref, ay_ref, az_ref, rate_ref):
            ref[at, :] = jnp.zeros((128, 128), jnp.float32)
        return carry

    lax.fori_loop(0, 16, own_step, 0)
    moved.wait()
    deep = lax.broadcasted_iota(jnp.int32, (8, 128), 0)
    across = lax.broadcasted_iota(jnp.int32, (8, 128), 1)

    def pack_step(row, carry):
        def put(chunk, tile, value):
            pack_ref[row * 32 + chunk] = tile
            chunk_ref[pl.ds(row * 32 + chunk, 1), :] = value

        def slot_step(slot, held):
            begin = offs_ref[slot, row]
            end = offs_ref[slot + 1, row]
            at = slot * 16 + row
            tile = near_ref[pl.ds(at * 8, 8), :] + shift_ref[slot]
            tile = pick(tile, jnp.broadcast_to(index_ref[pl.ds(at, 1), :], (8, 128)))
            value = turned_ref[pl.ds(at, 1), :]
            start = begin & 127
            merged = jnp.where(across >= start, tile, held[0])
            merged_value = jnp.where(lane >= start, value, held[1])
            put(begin >> 7, merged, merged_value)
            more = (end >> 7) > (begin >> 7)
            return (
                jnp.where(jnp.broadcast_to(more, (8, 128)), tile, merged),
                jnp.where(jnp.broadcast_to(more, (1, 128)), value, merged_value),
            )

        held = (near_ref[pl.ds(row * 8, 8), :], turned_ref[pl.ds(row, 1), :])
        held = lax.fori_loop(0, 27, slot_step, held, unroll=27)
        total = offs_ref[27, row]
        put(total >> 7, jnp.where((deep == 0) & (across >= (total & 127)), 0.0, held[0]), held[1])
        put(31, jnp.where(deep == 0, 0.0, held[0]), held[1])
        return carry

    lax.fori_loop(0, 16, pack_step, 0, unroll=2)
    list_jobs(offs_ref, counts_ref, active_ref, first, order_ref, jobs_ref)
    for load in loads:
        load.wait()

    def job_step(job, parts):
        place = jobs_ref[job]
        row = place >> 5
        tile = pack_ref[place]
        near_inv = tile[7:8]
        near_sq = near_inv * near_inv
        push = (6.0 * NORM) * tile[0:1] * (near_sq * near_sq) * chunk_ref[pl.ds(place, 1), :]
        mass, near_x, near_y, near_z, near_vx, near_vy, near_vz = [
            jnp.broadcast_to(tile[f : f + 1], (8, 128)) for f in range(7)
        ]
        near_inv = jnp.broadcast_to(near_inv, (8, 128))
        push = jnp.broadcast_to(push, (8, 128))
        for part in range(parts):
            at = pl.ds(row * 128 + part * 8, 8)
            gap_x = x_ref[at, :] - near_x
            gap_y = y_ref[at, :] - near_y
            gap_z = z_ref[at, :] - near_z
            square = jnp.maximum(gap_x * gap_x + gap_y * gap_y + gap_z * gap_z, TINY)
            root = lax.rsqrt(square)
            gap = square * root
            pull = slope(gap * inv_ref[at, :]) * root * mass
            both = own_ref[at, :] * pull + slope(gap * near_inv) * push * root
            work = (vx_ref[at, :] - near_vx) * gap_x + (vy_ref[at, :] - near_vy) * gap_y + (vz_ref[at, :] - near_vz) * gap_z
            ax_ref[at, :] = ax_ref[at, :] + both * gap_x
            ay_ref[at, :] = ay_ref[at, :] + both * gap_y
            az_ref[at, :] = az_ref[at, :] + both * gap_z
            rate_ref[at, :] = rate_ref[at, :] + pull * work

    run_jobs(jobs_ref, job_step)

    def end_step(row, carry):
        own = near_ref[pl.ds(1664 + row * 8, 8), :]
        inverse = own[7:8]
        inv_sq = inverse * inverse
        factor = (-6.0 * NORM) * (inv_sq * inv_sq) * press_ref[pl.ds(208 + row, 1), :]
        at = pl.ds(row * 128, 128)
        keep = lane < counts_ref[active_ref[row] - first]
        values = [fresh_ref[row]] + [row_sums(ref[at, :]) for ref in (ax_ref, ay_ref, az_ref)]
        values.append(factor * row_sums(rate_ref[at, :]))
        for number, value in enumerate(values):
            hydro_ref[number, pl.ds(row, 1), :] = jnp.where(keep, value, 0.0)
        return carry

    lax.fori_loop(0, 16, end_step, 0, unroll=2)


def specs(kinds):
    return [pl.BlockSpec(memory_space=pltpu.SMEM if kind == "s" else pltpu.VMEM) for kind in kinds]


def floats(*shape):
    return jax.ShapeDtypeStruct(shape, jnp.float32)


def force_call(*args):
    square = pltpu.VMEM((2048, 128), jnp.float32)
    return pl.pallas_call(
        force_kernel,
        out_shape=floats(5, 16, 128),
        in_specs=specs("ss") + [pl.BlockSpec(memory_space=pl.ANY)] + specs("vvvv"),
        out_specs=specs("v")[0],
        scratch_shapes=[
            pltpu.VMEM((512, 8, 128), jnp.float32), pltpu.VMEM((512, 128), jnp.float32),
            pltpu.VMEM((432, 128), jnp.int32), pltpu.VMEM((432, 128), jnp.float32), pltpu.VMEM((32, 128), jnp.int32),
            pltpu.VMEM((432, 128), jnp.float32), pltpu.SMEM((32, 128), jnp.int32), pltpu.SMEM((32,), jnp.int32),
            pltpu.SMEM((640,), jnp.int32),
        ] + [square] * 12 + [pltpu.SemaphoreType.DMA, pltpu.SemaphoreType.DMA((7,))],
        compiler_params=pltpu.CompilerParams(vmem_limit_bytes=LIMIT),
        name="force",
    )(*args)


def shards(positions, velocity, mass, smoothing, energy, density_old, counts, active, neighbours):
    devices = lax.axis_size("dom")
    vmem = pl.BlockSpec(memory_space=pltpu.VMEM)
    smem = pl.BlockSpec(memory_space=pltpu.SMEM)
    pos = jnp.transpose(positions, (1, 0, 2))
    vel = jnp.transpose(velocity, (1, 0, 2))
    requests = jnp.pad(neighbours, ((0, 0), (0, 101)))
    shifts = jnp.asarray(shift_tiles())
    f32 = jnp.float32

    anywhere = pl.BlockSpec(memory_space=pl.ANY)
    near, press, fresh, columns = pl.pallas_call(
        lambda *refs: gather_kernel(devices, *refs),
        out_shape=(floats(432, 8, 128), floats(432, 1, 128), floats(16, 1, 128), floats(7, 2048, 128)),
        in_specs=[smem, vmem, smem, smem] + [anywhere] * 6,
        out_specs=(vmem, vmem, vmem, anywhere),
        scratch_shapes=[
            pltpu.VMEM((3, 1600, 128), f32),
            pltpu.VMEM((3, 1600, 128), f32),
            pltpu.VMEM((1600, 128), f32),
            pltpu.VMEM((1600, 128), f32),
            pltpu.VMEM((1600, 128), f32),
            pltpu.VMEM((1600, 128), f32),
            pltpu.VMEM((7, 16, 128), jnp.int32),
            pltpu.VMEM((7, 2048, 128), f32),
            pltpu.VMEM((2048, 128), f32),
            pltpu.VMEM((1600, 128), f32),
            pltpu.VMEM((16, 1, 128), f32),
            pltpu.VMEM((432, 8, 128), f32),
            pltpu.VMEM((9, 8, 128), f32),
            pltpu.VMEM((432, 1, 128), f32),
            pltpu.VMEM((9, 1, 128), f32),
            pltpu.SMEM((7, 16, 128), jnp.int32),
            pltpu.SemaphoreType.DMA((7,)),
            pltpu.SemaphoreType.DMA((7,)),
            pltpu.SemaphoreType.DMA((24,)),
            pltpu.SemaphoreType.DMA((24,)),
            pltpu.SemaphoreType.DMA((14,)),
            pltpu.SemaphoreType.DMA((14,)),
            pltpu.SemaphoreType.DMA((7,)),
            pltpu.SemaphoreType.DMA((6,)),
            pltpu.SemaphoreType.DMA,
        ],
        compiler_params=pltpu.CompilerParams(collective_id=0, has_side_effects=True, vmem_limit_bytes=LIMIT),
        name="cells",
    )(requests, requests, counts, active, pos, vel, mass, smoothing, energy, density_old)

    hydro = force_call(
        counts, active, columns, near.reshape(3456, 128), press.reshape(432, 128), shifts, fresh
    )
    return jnp.transpose(hydro, (1, 0, 2))


def solution(mesh):
    placed = (
        P("dom", None, None),
        P("dom", None, None),
        P("dom", None),
        P("dom", None),
        P("dom", None),
        P("dom", None),
        P("dom"),
        P("dom"),
        P("dom", None),
    )
    return jax.shard_map(
        shards, mesh=mesh, in_specs=placed, out_specs=P("dom", None, None), check_vma=False
    )
```

```python
import math

import jax
import jax.numpy as jnp
import numpy as np
from jax import lax
from jax.experimental import pallas as pl
from jax.experimental.pallas import tpu as pltpu
from jax.sharding import PartitionSpec as P

MESH = pl.DeviceIdType.MESH
NORM = 8.0 / math.pi
GAS = 2.0 / 3.0
TINY = 1e-14
LIMIT = 56 * 1024 * 1024

STEPS = (16, 4, 20, 1, 5, 17, 21)
WIDE = ((0, 6), (0, 7), (1, 2), (1, 5), (2, 8))
EDGE = ((6, 8), (5, 6), (5, 7), (4, 2), (4, 5), (3, 0), (3, 1), (3, 3), (3, 4))
HOME = (0, 1, 3, 4)
SPAN = 47
COLUMNS = (1, 2, 3, 7, 4, 5, 6)


def shift_tiles():
    tiles = np.zeros((27, 8, 128), np.float32)
    for slot in range(27):
        tiles[slot, 1] = slot // 9 - 1
        tiles[slot, 2] = slot // 3 % 3 - 1
        tiles[slot, 3] = slot % 3 - 1
    return tiles


def greet(me, devices):
    barrier = pltpu.get_barrier_semaphore()
    for steps in STEPS:
        for other in (me + steps, me + devices - steps):
            pl.semaphore_signal(barrier, inc=1, device_id=(lax.rem(other, devices),), device_id_type=MESH)


def gather_kernel(
    devices, req_ref, req_send, counts_ref, active_ref, pos_all, vel_all, mass_all, smooth_all, energy_all, old_all,
    near_ref, press_ref, fresh_ref, columns_ref,
    pos_ref, vel_ref, mass_ref, smooth_ref, energy_ref, old_ref, asked_ref, square_ref, sum_ref, table_ref, own_ref,
    send_ref, edge_ref, give_ref, give_edge_ref, lists_ref,
    ask_out, ask_in, send_sem, recv_sem, give_out, give_in, local_sem, table_sem, column_sem,
):
    me = lax.axis_index("dom")
    cells = mass_ref.shape[0]
    tables = [
        pltpu.make_async_copy(source, target, table_sem.at[number])
        for number, (source, target) in enumerate(
            (
                (pos_all, pos_ref), (vel_all, vel_ref), (mass_all, mass_ref), (smooth_all, smooth_ref),
                (energy_all, energy_ref), (old_all, old_ref),
            )
        )
    ]
    for table in tables:
        table.start()
    first = me * cells
    lane = lax.broadcasted_iota(jnp.int32, (1, 128), 1)

    def local(cell):
        return jnp.clip(cell - first, 0, cells - 1)

    def fill(dst, place, cell):
        cell = local(cell)
        keep = lane < counts_ref[cell]
        dst[place, 0:1, :] = jnp.where(keep, mass_ref[pl.ds(cell, 1), :], 0.0)
        for axis in range(3):
            dst[place, 1 + axis : 2 + axis, :] = pos_ref[axis, pl.ds(cell, 1), :]
            dst[place, 4 + axis : 5 + axis, :] = vel_ref[axis, pl.ds(cell, 1), :]
        dst[place, 7:8, :] = 1.0 / smooth_ref[pl.ds(cell, 1), :]

    greet(me, devices)
    pl.semaphore_wait(pltpu.get_barrier_semaphore(), 2 * len(STEPS))
    asks = []
    for place, steps in enumerate(STEPS):
        ask = pltpu.make_async_remote_copy(
            req_send, asked_ref.at[place], ask_out.at[place], ask_in.at[place],
            device_id=(lax.rem(me + steps, devices),), device_id_type=MESH,
        )
        ask.start()
        asks.append(ask)

    for table in tables:
        table.wait()

    def home_step(entry, carry):
        for block in HOME:
            fill(near_ref, block * 48 + entry, req_ref[entry & 15, block * 3 + (entry >> 4)])
        return carry

    lax.fori_loop(0, SPAN, home_step, 0)

    def own_step(row, carry):
        for number, feature in enumerate(COLUMNS):
            square_ref[number, pl.ds(row * 128, 128), :] = column(near_ref[208 + row, feature : feature + 1, :])
        return carry

    lax.fori_loop(0, 16, own_step, 0)
    stored = pltpu.make_async_copy(square_ref, columns_ref, column_sem)
    stored.start()
    sum_ref[...] = jnp.zeros((2048, 128), jnp.float32)

    def add_tiles(row, tiles):
        near = []
        for index, *shift in tiles:
            tile = near_ref[index]
            near.append([tile[0:1]] + [tile[1 + axis : 2 + axis] + shift[axis] for axis in range(3)])
        for part in range(4):
            at = pl.ds(row * 128 + part * 32, 32)
            own_x, own_y, own_z, own_inv = [square_ref[number, at, :] for number in range(4)]
            total = sum_ref[at, :]
            for mass, near_x, near_y, near_z in near:
                gap_x = own_x - near_x
                gap_y = own_y - near_y
                gap_z = own_z - near_z
                square = jnp.maximum(gap_x * gap_x + gap_y * gap_y + gap_z * gap_z, TINY)
                ratio = square * lax.rsqrt(square) * own_inv
                outer = jnp.maximum(1.0 - ratio, 0.0)
                inner = jnp.maximum(outer - ratio, 0.0)
                total = total + ((outer + outer) * (outer * outer) - inner * (inner * inner)) * mass
            sum_ref[at, :] = total

    def add_blocks(blocks, begin, end):
        def step(entry, carry):
            high = (entry // 16 - 1).astype(jnp.float32)
            add_tiles(entry % 16, [(block * 48 + entry, block // 3 - 1.0, block % 3 - 1.0, high) for block in blocks])
            return carry

        lax.fori_loop(begin, end, step, 0)

    def hear(places):
        lists = []
        for place in places:
            asks[place].wait_recv()
            lists.append(pltpu.make_async_copy(asked_ref.at[place], lists_ref.at[place], local_sem.at[place]))
            lists[-1].start()
        for listed in lists:
            listed.wait()

    def requester(place):
        return (lax.rem(me + devices - STEPS[place], devices),)

    hear((0, 1, 2))
    copies = []
    edges = []

    def serve(third):
        size = 15 if third == 2 else 16

        def serve_step(entry, carry):
            for place, block in WIDE:
                fill(send_ref, block * 48 + third * 16 + entry, lists_ref[place, entry, block * 3 + third])
            return carry

        lax.fori_loop(0, size, serve_step, 0)
        for place, block in WIDE:
            rows = pl.ds(block * 48 + third * 16, size)
            copy = pltpu.make_async_remote_copy(
                send_ref.at[rows], near_ref.at[rows], send_sem.at[len(copies)], recv_sem.at[len(copies)],
                device_id=requester(place), device_id_type=MESH,
            )
            copy.start()
            copies.append(copy)

    serve(0)
    hear((3, 4, 5, 6))
    for number, (place, block) in enumerate(EDGE):
        fill(edge_ref, number, lists_ref[place, 15, block * 3 + 2])
        copy = pltpu.make_async_remote_copy(
            edge_ref.at[number], near_ref.at[block * 48 + SPAN], send_sem.at[15 + number], recv_sem.at[15 + number],
            device_id=requester(place), device_id_type=MESH,
        )
        copy.start()
        edges.append(copy)

    serve(1)
    add_blocks(HOME, 0, 16)
    serve(2)
    add_blocks(HOME, 16, 32)
    add_blocks(HOME, 32, SPAN)

    def table_step(part, carry):
        at = pl.ds(part * 32, 32)
        table_ref[at, :] = GAS * energy_ref[at, :] / old_ref[at, :]
        return carry

    lax.fori_loop(0, cells // 32, table_step, 0)
    for third in range(3):
        for copy in copies[5 * third : 5 * third + 5]:
            copy.wait_recv()
        if third == 2:
            for copy in edges:
                copy.wait_recv()
            for begin in (0, 3, 6):
                add_tiles(
                    15, [(block * 48 + SPAN, block // 3 - 1.0, block % 3 - 1.0, 1.0) for block in range(begin, begin + 3)]
                )
        add_blocks((6, 7, 2, 5, 8), third * 16, min(third * 16 + 16, SPAN))

    def fresh_step(row, carry):
        inverse = near_ref[208 + row, 7:8, :]
        cell = local(active_ref[row])
        fresh = jnp.where(
            lane < counts_ref[cell],
            row_sums(sum_ref[pl.ds(row * 128, 128), :]) * (NORM * inverse * inverse * inverse),
            old_ref[pl.ds(cell, 1), :],
        )
        fresh_ref[row] = fresh
        own_ref[row] = GAS * energy_ref[pl.ds(cell, 1), :] / fresh
        return carry

    lax.fori_loop(0, 16, fresh_step, 0, unroll=4)
    deep = lax.broadcasted_iota(jnp.int32, (32, 128), 0)
    own_cells = [local(active_ref[row]) for row in range(16)]

    def patch_step(part, carry):
        at = pl.ds(part * 32, 32)
        value = table_ref[at, :]
        for row in range(16):
            value = jnp.where(deep == own_cells[row] - part * 32, own_ref[row], value)
        table_ref[at, :] = value
        return carry

    lax.fori_loop(0, cells // 32, patch_step, 0)

    def give_step(entry, carry):
        for place, block in WIDE:
            give_ref[block * 48 + entry] = table_ref[pl.ds(local(lists_ref[place, entry & 15, block * 3 + (entry >> 4)]), 1), :]
        return carry

    def send_give(number, place, source, target):
        give = pltpu.make_async_remote_copy(
            source, target, give_out.at[number], give_in.at[number], device_id=requester(place), device_id_type=MESH
        )
        give.start()
        return give

    gives = []
    for number, (place, block) in enumerate(EDGE):
        give_edge_ref[number] = table_ref[pl.ds(local(lists_ref[place, 15, block * 3 + 2]), 1), :]
        gives.append(send_give(number, place, give_edge_ref.at[number], press_ref.at[block * 48 + SPAN]))
    lax.fori_loop(0, SPAN, give_step, 0)
    for number, (place, block) in enumerate(WIDE):
        rows = pl.ds(block * 48, SPAN)
        gives.append(send_give(9 + number, place, give_ref.at[rows], press_ref.at[rows]))

    def keep_step(entry, carry):
        for block in HOME:
            press_ref[block * 48 + entry] = table_ref[pl.ds(local(req_ref[entry & 15, block * 3 + (entry >> 4)]), 1), :]
        return carry

    lax.fori_loop(0, SPAN, keep_step, 0)
    for ask in asks:
        ask.wait_send()
    for copy in copies + edges:
        copy.wait_send()
    stored.wait()
    for give in gives:
        give.wait()


def rows_of(ref, slot, feature):
    return ref[pl.ds(slot * 128 + feature, 16, stride=8), :]


def pick(values, index):
    return jnp.take_along_axis(values, index, axis=1, mode="promise_in_bounds")


def eye():
    return lax.broadcasted_iota(jnp.int32, (128, 128), 0) == lax.broadcasted_iota(jnp.int32, (128, 128), 1)


def column(row):
    return jnp.broadcast_to(jnp.sum(jnp.where(eye(), row, 0.0), axis=1, keepdims=True), (128, 128))


def row_sums(pairs):
    total = jnp.sum(pairs, axis=1, keepdims=True)
    return jnp.sum(jnp.where(eye(), total, 0.0), axis=0, keepdims=True)


def list_jobs(offs_ref, counts_ref, active_ref, first, order_ref, jobs_ref):
    place = jnp.int32(0)
    ends = []
    for low, high in ((0, 80), (80, 96), (96, 112), (112, 128)):
        for row in range(16):
            own = counts_ref[active_ref[row] - first]
            order_ref[place] = row
            place = place + ((own > low) & (own <= high)).astype(jnp.int32)
        ends.append(place)
    count = jnp.int32(0)
    begin = jnp.int32(0)
    jobs_ref[512] = count
    for number, end in enumerate(ends):
        def one_row(place, count):
            row = order_ref[place]
            chunks = (offs_ref[27, row] + 127) >> 7
            for chunk in range(10):
                jobs_ref[count + chunk] = row * 32 + chunk

            def one_chunk(chunk, carry):
                jobs_ref[count + chunk] = row * 32 + chunk
                return carry

            lax.fori_loop(10, chunks, one_chunk, 0)
            return count + chunks

        count = lax.fori_loop(begin, end, one_row, count)
        for extra in range(3):
            jobs_ref[count + extra] = 31
        count = (count + 3) & ~3
        jobs_ref[513 + number] = count
        begin = end


def run_jobs(jobs_ref, step):
    for number, parts in enumerate((10, 12, 14, 16)):
        def two(pair, carry):
            for number in range(4):
                step(4 * pair + number, parts)
            return carry

        lax.fori_loop(jobs_ref[512 + number] >> 2, jobs_ref[513 + number] >> 2, two, 0)


def slope(ratio):
    outer = jnp.maximum(1.0 - ratio, 0.0)
    low = jnp.minimum(outer, ratio)
    return low * ((outer + outer) - low)


def force_kernel(
    counts_ref, active_ref, columns_ref, near_ref, press_ref, shift_ref, fresh_ref,
    hydro_ref, pack_ref, chunk_ref, index_ref, mask_ref, offs_out_ref, turned_ref, offs_ref, order_ref, jobs_ref,
    x_ref, y_ref, z_ref, vx_ref, vy_ref, vz_ref, inv_ref, own_ref, ax_ref, ay_ref, az_ref, rate_ref, local_sem, column_sem,
):
    cells = counts_ref.shape[0]
    first = lax.axis_index("dom") * cells
    lane = lax.broadcasted_iota(jnp.int32, (1, 128), 1)
    lanes = lax.broadcasted_iota(jnp.int32, (16, 128), 1)
    on_diagonal = lax.broadcasted_iota(jnp.int32, (16, 128), 0) == lanes
    loads = [
        pltpu.make_async_copy(columns_ref.at[number], ref, column_sem.at[number])
        for number, ref in enumerate((x_ref, y_ref, z_ref, inv_ref, vx_ref, vy_ref, vz_ref))
    ]
    for load in loads:
        load.start()
    lows, highs = [], []
    for axis in range(3):
        own = rows_of(near_ref, 13, 1 + axis)
        lows.append(jnp.min(own, axis=1, keepdims=True))
        highs.append(jnp.max(own, axis=1, keepdims=True))
    widest = jnp.min(rows_of(near_ref, 13, 7), axis=1, keepdims=True)

    for slot in range(27):
        away = jnp.zeros((16, 128), jnp.float32)
        for axis, step in enumerate((slot // 9, slot // 3 % 3, slot % 3)):
            at = rows_of(near_ref, slot, 1 + axis) + (step - 1.0)
            out = jnp.maximum(jnp.maximum(lows[axis] - at, at - highs[axis]), 0.0)
            away = away + out * out
        reach = jnp.minimum(rows_of(near_ref, slot, 7), widest)
        chosen = (rows_of(near_ref, slot, 0) > 0.0) & (away * (reach * reach) <= 1.0001)
        mask_ref[slot * 16 : slot * 16 + 16, :] = jnp.where(chosen, 1.0, 0.0)
    high = lax.broadcasted_iota(jnp.int32, (128, 256), 0)
    wide = lax.broadcasted_iota(jnp.int32, (128, 256), 1)
    counter = jnp.where((wide >= 128) | (high <= wide), 1.0, 0.0).astype(jnp.bfloat16)
    begin = jnp.zeros((16, 128), jnp.int32)
    for slot in range(27):
        at = pl.ds(slot * 16, 16)
        ranks = jnp.dot(mask_ref[at, :].astype(jnp.bfloat16), counter, preferred_element_type=jnp.float32)
        ranks = ranks.astype(jnp.int32)
        order = ranks[:, 0:128]
        wanted = (lanes - begin) & 127
        index = jnp.zeros((16, 128), jnp.int32)
        for step in (64, 32, 16, 8, 4, 2, 1):
            index = index + jnp.where(pick(order, index + (step - 1)) <= wanted, step, 0)
        index_ref[at, :] = index
        turned_ref[at, :] = pick(press_ref[at, :], index)
        offs_out_ref[slot : slot + 1, :] = jnp.sum(jnp.where(on_diagonal, begin, 0), axis=0, keepdims=True)
        begin = begin + ranks[:, 128:256]
    offs_out_ref[27:28, :] = jnp.sum(jnp.where(on_diagonal, begin, 0), axis=0, keepdims=True)
    offs_out_ref[28:32, :] = jnp.zeros((4, 128), jnp.int32)
    moved = pltpu.make_async_copy(offs_out_ref, offs_ref, local_sem)
    moved.start()

    def own_step(row, carry):
        own = near_ref[pl.ds(1664 + row * 8, 8), :]
        at = pl.ds(row * 128, 128)
        inv_sq = own[7:8] * own[7:8]
        own_ref[at, :] = column((6.0 * NORM) * (inv_sq * inv_sq) * press_ref[pl.ds(208 + row, 1), :])
        for ref in (ax_ref, ay_ref, az_ref, rate_ref):
            ref[at, :] = jnp.zeros((128, 128), jnp.float32)
        return carry

    lax.fori_loop(0, 16, own_step, 0)
    moved.wait()
    deep = lax.broadcasted_iota(jnp.int32, (8, 128), 0)
    across = lax.broadcasted_iota(jnp.int32, (8, 128), 1)

    def pack_step(row, carry):
        def put(chunk, tile, value):
            pack_ref[row * 32 + chunk] = tile
            chunk_ref[pl.ds(row * 32 + chunk, 1), :] = value

        def slot_step(slot, held):
            begin = offs_ref[slot, row]
            end = offs_ref[slot + 1, row]
            at = slot * 16 + row
            tile = near_ref[pl.ds(at * 8, 8), :] + shift_ref[slot]
            tile = pick(tile, jnp.broadcast_to(index_ref[pl.ds(at, 1), :], (8, 128)))
            value = turned_ref[pl.ds(at, 1), :]
            start = begin & 127
            merged = jnp.where(across >= start, tile, held[0])
            merged_value = jnp.where(lane >= start, value, held[1])
            put(begin >> 7, merged, merged_value)
            more = (end >> 7) > (begin >> 7)
            return (
                jnp.where(jnp.broadcast_to(more, (8, 128)), tile, merged),
                jnp.where(jnp.broadcast_to(more, (1, 128)), value, merged_value),
            )

        held = (near_ref[pl.ds(row * 8, 8), :], turned_ref[pl.ds(row, 1), :])
        held = lax.fori_loop(0, 27, slot_step, held, unroll=27)
        total = offs_ref[27, row]
        put(total >> 7, jnp.where((deep == 0) & (across >= (total & 127)), 0.0, held[0]), held[1])
        put(31, jnp.where(deep == 0, 0.0, held[0]), held[1])
        return carry

    lax.fori_loop(0, 16, pack_step, 0, unroll=2)
    list_jobs(offs_ref, counts_ref, active_ref, first, order_ref, jobs_ref)
    for load in loads:
        load.wait()

    def job_step(job, parts):
        place = jobs_ref[job]
        row = place >> 5
        tile = pack_ref[place]
        near_inv = tile[7:8]
        near_sq = near_inv * near_inv
        push = (6.0 * NORM) * tile[0:1] * (near_sq * near_sq) * chunk_ref[pl.ds(place, 1), :]
        mass, near_x, near_y, near_z, near_vx, near_vy, near_vz = [
            jnp.broadcast_to(tile[f : f + 1], (8, 128)) for f in range(7)
        ]
        near_inv = jnp.broadcast_to(near_inv, (8, 128))
        push = jnp.broadcast_to(push, (8, 128))
        for part in range(parts):
            at = pl.ds(row * 128 + part * 8, 8)
            gap_x = x_ref[at, :] - near_x
            gap_y = y_ref[at, :] - near_y
            gap_z = z_ref[at, :] - near_z
            square = jnp.maximum(gap_x * gap_x + gap_y * gap_y + gap_z * gap_z, TINY)
            root = lax.rsqrt(square)
            gap = square * root
            pull = slope(gap * inv_ref[at, :]) * root * mass
            both = own_ref[at, :] * pull + slope(gap * near_inv) * push * root
            work = (vx_ref[at, :] - near_vx) * gap_x + (vy_ref[at, :] - near_vy) * gap_y + (vz_ref[at, :] - near_vz) * gap_z
            ax_ref[at, :] = ax_ref[at, :] + both * gap_x
            ay_ref[at, :] = ay_ref[at, :] + both * gap_y
            az_ref[at, :] = az_ref[at, :] + both * gap_z
            rate_ref[at, :] = rate_ref[at, :] + pull * work

    run_jobs(jobs_ref, job_step)

    def end_step(row, carry):
        own = near_ref[pl.ds(1664 + row * 8, 8), :]
        inverse = own[7:8]
        inv_sq = inverse * inverse
        factor = (-6.0 * NORM) * (inv_sq * inv_sq) * press_ref[pl.ds(208 + row, 1), :]
        at = pl.ds(row * 128, 128)
        keep = lane < counts_ref[active_ref[row] - first]
        values = [fresh_ref[row]] + [row_sums(ref[at, :]) for ref in (ax_ref, ay_ref, az_ref)]
        values.append(factor * row_sums(rate_ref[at, :]))
        for number, value in enumerate(values):
            hydro_ref[number, pl.ds(row, 1), :] = jnp.where(keep, value, 0.0)
        return carry

    lax.fori_loop(0, 16, end_step, 0, unroll=2)


def specs(kinds):
    return [pl.BlockSpec(memory_space=pltpu.SMEM if kind == "s" else pltpu.VMEM) for kind in kinds]


def floats(*shape):
    return jax.ShapeDtypeStruct(shape, jnp.float32)


def force_call(*args):
    square = pltpu.VMEM((2048, 128), jnp.float32)
    return pl.pallas_call(
        force_kernel,
        out_shape=floats(5, 16, 128),
        in_specs=specs("ss") + [pl.BlockSpec(memory_space=pl.ANY)] + specs("vvvv"),
        out_specs=specs("v")[0],
        scratch_shapes=[
            pltpu.VMEM((512, 8, 128), jnp.float32), pltpu.VMEM((512, 128), jnp.float32),
            pltpu.VMEM((432, 128), jnp.int32), pltpu.VMEM((432, 128), jnp.float32), pltpu.VMEM((32, 128), jnp.int32),
            pltpu.VMEM((432, 128), jnp.float32), pltpu.SMEM((32, 128), jnp.int32), pltpu.SMEM((32,), jnp.int32),
            pltpu.SMEM((640,), jnp.int32),
        ] + [square] * 12 + [pltpu.SemaphoreType.DMA, pltpu.SemaphoreType.DMA((7,))],
        compiler_params=pltpu.CompilerParams(vmem_limit_bytes=LIMIT),
        name="force",
    )(*args)


def shards(positions, velocity, mass, smoothing, energy, density_old, counts, active, neighbours):
    devices = lax.axis_size("dom")
    vmem = pl.BlockSpec(memory_space=pltpu.VMEM)
    smem = pl.BlockSpec(memory_space=pltpu.SMEM)
    pos = jnp.transpose(positions, (1, 0, 2))
    vel = jnp.transpose(velocity, (1, 0, 2))
    requests = jnp.pad(neighbours, ((0, 0), (0, 101)))
    shifts = jnp.asarray(shift_tiles())
    f32 = jnp.float32

    anywhere = pl.BlockSpec(memory_space=pl.ANY)
    near, press, fresh, columns = pl.pallas_call(
        lambda *refs: gather_kernel(devices, *refs),
        out_shape=(floats(432, 8, 128), floats(432, 1, 128), floats(16, 1, 128), floats(7, 2048, 128)),
        in_specs=[smem, vmem, smem, smem] + [anywhere] * 6,
        out_specs=(vmem, vmem, vmem, anywhere),
        scratch_shapes=[
            pltpu.VMEM((3, 1600, 128), f32),
            pltpu.VMEM((3, 1600, 128), f32),
            pltpu.VMEM((1600, 128), f32),
            pltpu.VMEM((1600, 128), f32),
            pltpu.VMEM((1600, 128), f32),
            pltpu.VMEM((1600, 128), f32),
            pltpu.VMEM((7, 16, 128), jnp.int32),
            pltpu.VMEM((7, 2048, 128), f32),
            pltpu.VMEM((2048, 128), f32),
            pltpu.VMEM((1600, 128), f32),
            pltpu.VMEM((16, 1, 128), f32),
            pltpu.VMEM((432, 8, 128), f32),
            pltpu.VMEM((9, 8, 128), f32),
            pltpu.VMEM((432, 1, 128), f32),
            pltpu.VMEM((9, 1, 128), f32),
            pltpu.SMEM((7, 16, 128), jnp.int32),
            pltpu.SemaphoreType.DMA((7,)),
            pltpu.SemaphoreType.DMA((7,)),
            pltpu.SemaphoreType.DMA((24,)),
            pltpu.SemaphoreType.DMA((24,)),
            pltpu.SemaphoreType.DMA((14,)),
            pltpu.SemaphoreType.DMA((14,)),
            pltpu.SemaphoreType.DMA((7,)),
            pltpu.SemaphoreType.DMA((6,)),
            pltpu.SemaphoreType.DMA,
        ],
        compiler_params=pltpu.CompilerParams(collective_id=0, has_side_effects=True, vmem_limit_bytes=LIMIT),
        name="cells",
    )(requests, requests, counts, active, pos, vel, mass, smoothing, energy, density_old)

    hydro = force_call(
        counts, active, columns, near.reshape(3456, 128), press.reshape(432, 128), shifts, fresh
    )
    return jnp.transpose(hydro, (1, 0, 2))


def solution(mesh):
    placed = (
        P("dom", None, None),
        P("dom", None, None),
        P("dom", None),
        P("dom", None),
        P("dom", None),
        P("dom", None),
        P("dom"),
        P("dom"),
        P("dom", None),
    )
    return jax.shard_map(
        shards, mesh=mesh, in_specs=placed, out_specs=P("dom", None, None), check_vma=False
    )
```
